32 devices in a mesh: ctx: 16 (over z, x, core), head: 2 (over y).
Axes of the slice: x: 2, y: 2, z: 4, core: 2. Of those that a mesh axis runs over, the one named last changes fastest.
Arguments:
- queries: bfloat16 [3072, 6144], P(('ctx', 'head')), may hold values from -9 to 9
- noisy_token_keys: bfloat16 [3072, 1024], P(('ctx', 'head')), may hold values from -9 to 9
- noisy_token_values: bfloat16 [3072, 1024], P(('ctx', 'head')), may hold values from -6 to 6
- clean_token_keys: bfloat16 [1024, 1024], P(('ctx', 'head')), may hold values from -9 to 9
- clean_token_values: bfloat16 [1024, 1024], P(('ctx', 'head')), may hold values from -6 to 6
- output_gradient: bfloat16 [3072, 6144], P(('ctx', 'head')), may hold values from -6 to 6
- history_list: int32 [16, 16], replicated, may hold values from -1 to 1, as said below
Outputs:
- attn_out: bfloat16 [3072, 6144], P(('ctx', 'head'))
- grad_query: bfloat16 [3072, 6144], P(('ctx', 'head'))
- noisy_key_gradient: bfloat16 [3072, 1024], P(('ctx', 'head'))
- noisy_value_gradient: bfloat16 [3072, 1024], P(('ctx', 'head'))
- grad_key_clean: bfloat16 [1024, 1024], P(('ctx', 'head'))
- grad_value_clean: bfloat16 [1024, 1024], P(('ctx', 'head'))
The draws below stay inside these ranges and needn't reach their ends.
Inputs may be any that keep to these rules, and one draw needn't show every extreme that they name: history_list[d, s] is -1 or a block number below 2; it is -1 unless floor(s / 2) < floor(d / 2); each row has at most 14 entries that are not -1, and some row has exactly 14.
All inputs are finite; a program needn't handle non-finite values.
Results may differ from the reference program's by a relative error of at most 0.018.
Values may be sent and summed in bfloat16 or wider, within the bound.
No kernel may reach another device: no remote copies, remote signals or barrier semaphores. Data moves between devices by JAX's collectives and lax.ppermute only.
A program may use at most 64 MiB of HBM per device.

```python
import jax
import jax.numpy as jnp
from jax import lax

QUERY_HEADS = 48
KEY_VALUE_HEADS = 8
HEAD_SIZE = 128
GROUP_QUERY_TOKS = 192
NB = 2
BLK = 32
QDEV = 16
MAXS = 14
NOISY_TOKENS = 3072
CLEAN_TOKENS = 1024
N_CTX = 16


def drawn_pair(key):
    queries_raw = jnp.clip(1.5 * jax.random.normal(jax.random.fold_in(key, 101), (NOISY_TOKENS, QUERY_HEADS * HEAD_SIZE), jnp.float32), -9.0, 9.0)
    unshaped_keys = jnp.clip(1.5 * jax.random.normal(jax.random.fold_in(key, 202), (NOISY_TOKENS, KEY_VALUE_HEADS * HEAD_SIZE), jnp.float32), -9.0, 9.0)
    return (queries_raw, unshaped_keys)


def draw_queries(key, part):
    return drawn_pair(key)[0].astype(jnp.bfloat16)


def draw_noisy_token_keys(key, part):
    return drawn_pair(key)[1].astype(jnp.bfloat16)


def draw_history_list(key, part):
    row_ids = jnp.arange(QDEV, dtype=jnp.int32)
    allowed = (row_ids // 2)[None, :] < (row_ids // 2)[:, None]
    allowed_count = jnp.sum(allowed.astype(jnp.int32), 1)
    wanted = jax.random.randint(jax.random.fold_in(key, 1), (QDEV,), MAXS // 2, MAXS + 1, dtype=jnp.int32)
    wanted = jnp.where(row_ids == QDEV - 1, MAXS, wanted)
    wanted = jnp.minimum(wanted, allowed_count)
    priority = jax.random.randint(jax.random.fold_in(key, 2), (QDEV, QDEV), 0, 2 ** 20, dtype=jnp.int32) * QDEV + row_ids[None, :]
    priority = jnp.where(allowed, priority, 2 ** 30 + row_ids[None, :])
    ranking = jnp.argsort(jnp.argsort(priority, axis=1), axis=1).astype(jnp.int32)
    selected = allowed & (ranking < wanted[:, None])
    block_pick = jax.random.randint(jax.random.fold_in(key, 3), (QDEV, QDEV), 0, NB, dtype=jnp.int32)
    return jnp.where(selected, block_pick, -1).astype(jnp.int32)


def block_scale(own_key, extent, shards, low, high):
    def one(dim, blocks):
        heights = jax.random.uniform(jax.random.fold_in(jax.random.fold_in(own_key, 6), dim), (blocks,), jnp.float32, low / len(shards), high / len(shards))
        return jnp.repeat(jnp.exp(heights), extent[dim] // blocks).reshape((-1,) + (1,) * (len(extent) - dim - 1))

    loudness = one(*shards[0])
    for cut in shards[1:]:
        loudness = loudness * one(*cut)
    return loudness


def gaussian(rng, extent, spread, limit, shards=(), kind=jnp.bfloat16):
    entries = spread * jax.random.normal(rng, extent, jnp.float32)
    if shards:
        entries = entries * block_scale(rng, extent, shards, -0.22, 0.18)
    return jnp.clip(entries, -limit, limit).astype(kind)


def setup_inputs(seed: int = 0) -> dict:
    arg_keys = jax.random.split(jax.random.key(seed), 8)
    return {
        "queries": draw_queries(jax.random.fold_in(arg_keys[7], 71), 0),
        "noisy_token_keys": draw_noisy_token_keys(jax.random.fold_in(arg_keys[7], 71), 0),
        "noisy_token_values": gaussian(arg_keys[2], (NOISY_TOKENS, KEY_VALUE_HEADS * HEAD_SIZE), 1.0, 6.0, ((0, 32),)),
        "clean_token_keys": gaussian(arg_keys[3], (CLEAN_TOKENS, KEY_VALUE_HEADS * HEAD_SIZE), 1.5, 9.0, ((0, 32),)),
        "clean_token_values": gaussian(arg_keys[4], (CLEAN_TOKENS, KEY_VALUE_HEADS * HEAD_SIZE), 1.0, 6.0, ((0, 32),)),
        "output_gradient": gaussian(arg_keys[5], (NOISY_TOKENS, QUERY_HEADS * HEAD_SIZE), 1.0, 6.0, ((0, 32),)),
        "history_list": draw_history_list(jax.random.fold_in(arg_keys[7], 71), 0),
    }


NEG_FILL = -1.0e30


def rounded(values):
    return lax.optimization_barrier(values.astype(jnp.bfloat16)).astype(jnp.float32)


def reference(queries, noisy_token_keys, noisy_token_values, clean_token_keys, clean_token_values, output_gradient, history_list):
    heads_per_group = QUERY_HEADS // KEY_VALUE_HEADS
    logit_scale = HEAD_SIZE ** -0.5
    block_offsets = jnp.arange(BLK, dtype=jnp.int32)

    def one_group(running, query_group_index):
        clean_key_grad, clean_value_grad = running
        query_matrix_rows = lax.dynamic_slice_in_dim(queries, query_group_index * GROUP_QUERY_TOKS, GROUP_QUERY_TOKS, 0).astype(jnp.float32).reshape(GROUP_QUERY_TOKS, KEY_VALUE_HEADS, heads_per_group, HEAD_SIZE)
        incoming_gradient = lax.dynamic_slice_in_dim(output_gradient, query_group_index * GROUP_QUERY_TOKS, GROUP_QUERY_TOKS, 0).astype(jnp.float32).reshape(GROUP_QUERY_TOKS, KEY_VALUE_HEADS, heads_per_group, HEAD_SIZE)
        span_begin_index = (query_group_index // 2) * (2 * GROUP_QUERY_TOKS)
        keys_in_span = lax.dynamic_slice_in_dim(noisy_token_keys, span_begin_index, 2 * GROUP_QUERY_TOKS, 0).astype(jnp.float32).reshape(2 * GROUP_QUERY_TOKS, KEY_VALUE_HEADS, HEAD_SIZE)
        values_in_span = lax.dynamic_slice_in_dim(noisy_token_values, span_begin_index, 2 * GROUP_QUERY_TOKS, 0).astype(jnp.float32).reshape(2 * GROUP_QUERY_TOKS, KEY_VALUE_HEADS, HEAD_SIZE)
        listed = history_list[query_group_index]
        slot_order = jnp.argsort((listed < 0).astype(jnp.int32), stable=True)[:MAXS].astype(jnp.int32)
        chosen = listed[slot_order]
        chosen_live = chosen >= 0
        query_row_index = ((slot_order * NB + jnp.maximum(chosen, 0)) * BLK)[:, None] + block_offsets[None, :]
        query_row_index = query_row_index.reshape(-1).astype(jnp.int32)
        clean_history_keys = clean_token_keys[query_row_index].astype(jnp.float32).reshape(-1, KEY_VALUE_HEADS, HEAD_SIZE)
        clean_history_values = clean_token_values[query_row_index].astype(jnp.float32).reshape(-1, KEY_VALUE_HEADS, HEAD_SIZE)
        all_keys = jnp.concatenate([keys_in_span, clean_history_keys], 0)
        all_values = jnp.concatenate([values_in_span, clean_history_values], 0)
        live_keys = jnp.concatenate([jnp.ones((2 * GROUP_QUERY_TOKS,), jnp.bool_), jnp.repeat(chosen_live, BLK)], 0)
        scores = jnp.einsum('qgrd,kgd->gqrk', query_matrix_rows, all_keys) * logit_scale
        scores = jnp.where(live_keys, scores, NEG_FILL)
        row_max = jnp.max(scores, -1, keepdims=True)
        log_total = row_max + jnp.log(jnp.sum(jnp.exp(scores - row_max), -1, keepdims=True))
        probabilities = jnp.exp(scores - log_total)
        softmax_weights = rounded(probabilities)
        attended = jnp.einsum('gqrk,kgd->qgrd', softmax_weights, all_values).astype(jnp.bfloat16)
        row_dot = jnp.sum(incoming_gradient * attended.astype(jnp.float32), -1).transpose(1, 0, 2)[..., None]
        dprobs = jnp.einsum('qgrd,kgd->gqrk', incoming_gradient, all_values)
        score_gradient = rounded(probabilities * (dprobs - row_dot))
        query_grad = (logit_scale * jnp.einsum('gqrk,kgd->qgrd', score_gradient, all_keys)).astype(jnp.bfloat16)
        key_gradient_terms = (logit_scale * jnp.einsum('xtlv,txlh->vxh', score_gradient, query_matrix_rows)).reshape(-1, KEY_VALUE_HEADS * HEAD_SIZE)
        value_gradient_terms = jnp.einsum('xtlv,txlh->vxh', softmax_weights, incoming_gradient).reshape(-1, KEY_VALUE_HEADS * HEAD_SIZE)
        clean_key_grad = clean_key_grad.at[query_row_index].add(key_gradient_terms[2 * GROUP_QUERY_TOKS:])
        clean_value_grad = clean_value_grad.at[query_row_index].add(value_gradient_terms[2 * GROUP_QUERY_TOKS:])
        produced = (attended.reshape(GROUP_QUERY_TOKS, QUERY_HEADS * HEAD_SIZE), query_grad.reshape(GROUP_QUERY_TOKS, QUERY_HEADS * HEAD_SIZE), key_gradient_terms[:2 * GROUP_QUERY_TOKS], value_gradient_terms[:2 * GROUP_QUERY_TOKS])
        return (clean_key_grad, clean_value_grad), produced

    initial_gradients = jnp.zeros((CLEAN_TOKENS, KEY_VALUE_HEADS * HEAD_SIZE), jnp.float32)
    finals, produced = lax.scan(one_group, (initial_gradients, initial_gradients), jnp.arange(N_CTX, dtype=jnp.int32))
    attended_all, query_grads, key_segments, value_segments = produced
    attn_out = attended_all.reshape(NOISY_TOKENS, QUERY_HEADS * HEAD_SIZE)
    grad_query = query_grads.reshape(NOISY_TOKENS, QUERY_HEADS * HEAD_SIZE)
    noisy_key_gradient = key_segments.reshape(N_CTX // 2, 2, 2 * GROUP_QUERY_TOKS, KEY_VALUE_HEADS * HEAD_SIZE).sum(1).reshape(NOISY_TOKENS, KEY_VALUE_HEADS * HEAD_SIZE).astype(jnp.bfloat16)
    noisy_value_gradient = value_segments.reshape(N_CTX // 2, 2, 2 * GROUP_QUERY_TOKS, KEY_VALUE_HEADS * HEAD_SIZE).sum(1).reshape(NOISY_TOKENS, KEY_VALUE_HEADS * HEAD_SIZE).astype(jnp.bfloat16)
    return (attn_out, grad_query, noisy_key_gradient, noisy_value_gradient, finals[0].astype(jnp.bfloat16), finals[1].astype(jnp.bfloat16))
```

```python
import functools

import jax
import jax.numpy as jnp
from jax import lax
from jax.experimental import pallas as pl
from jax.experimental.pallas import tpu as pltpu
from jax.sharding import PartitionSpec as P

QUERY_HEADS = 48
KEY_VALUE_HEADS = 8
HEAD_SIZE = 128
BLK = 32
HEADS_PER_GROUP = QUERY_HEADS // KEY_VALUE_HEADS
SCALE = HEAD_SIZE**-0.5
LOG2E = 1.4426950408889634

NEG_FILL = -1e30


def swapped(block, axis, bit):
    count = lax.axis_size(axis)
    route = []
    for low in range(count):
        high = low | 1 << bit
        if high != low and high < count:
            route += [(low, high), (high, low)]
    return lax.ppermute(block, axis, route)


def shifted(block, axis, step):
    count = lax.axis_size(axis)
    return lax.ppermute(block, axis, [(i, (i + step) % count) for i in range(count)])


def dot(a, b, contract):
    return lax.dot_general(
        a, b, ((contract[:1], contract[1:]), ((), ())), preferred_element_type=jnp.float32
    )


def attention_kernel(
    noisy_parts, slots, blocks_per_store, listed, q_ref, g_ref, *refs
):
    noisy_keys = refs[:noisy_parts]
    noisy_values = refs[noisy_parts : 2 * noisy_parts]
    clean_k, clean_v, o_ref, gq_ref, gn_ref, gc_ref, k_all, v_all = refs[2 * noisy_parts :]
    rows = q_ref.shape[0]
    width = HEAD_SIZE

    at = 0
    for key_part, value_part in zip(noisy_keys, noisy_values):
        k_all[at : at + key_part.shape[0], :] = key_part[...]
        v_all[at : at + key_part.shape[0], :] = value_part[...]
        at += key_part.shape[0]
    span = at
    for slot in range(slots):
        block = slot * blocks_per_store + jnp.maximum(listed[slot], 0)
        source = pl.ds(pl.multiple_of(block * BLK, BLK), BLK)
        k_all[at : at + BLK, :] = clean_k[source, :]
        v_all[at : at + BLK, :] = clean_v[source, :]
        at += BLK

    keys = k_all[...]
    values = v_all[...]
    query = jnp.concatenate(
        [q_ref[:, r * width : (r + 1) * width] for r in range(HEADS_PER_GROUP)], 0
    )
    upstream = jnp.concatenate(
        [g_ref[:, r * width : (r + 1) * width] for r in range(HEADS_PER_GROUP)], 0
    )
    keys_t = keys.T
    values_t = values.T
    upstream_t = upstream.T

    scores = dot(keys, query, (1, 1)) * (SCALE * LOG2E)
    pieces = [scores[:span]]
    for slot in range(slots):
        low = span + slot * BLK
        bias = jnp.where(listed[slot] >= 0, 0.0, NEG_FILL).astype(jnp.float32)
        pieces.append(scores[low : low + BLK] + bias)
    scores = jnp.concatenate(pieces, 0)
    top = jnp.max(scores, 0, keepdims=True)
    unscaled = jnp.exp2(scores - top)
    prob = unscaled * (1.0 / jnp.sum(unscaled, 0, keepdims=True))
    weights = prob.astype(jnp.bfloat16)
    attended_t = dot(values_t, weights, (1, 0)).astype(jnp.bfloat16)
    row_dot = jnp.sum(
        attended_t.astype(jnp.float32) * upstream_t.astype(jnp.float32), 0, keepdims=True
    )
    dprob = dot(values, upstream, (1, 1))
    dscore = (prob * (dprob - row_dot)).astype(jnp.bfloat16)
    gq_t = (dot(keys_t, dscore, (1, 0)) * SCALE).astype(jnp.bfloat16)
    attended = attended_t.T
    gq = gq_t.T
    for r in range(HEADS_PER_GROUP):
        o_ref[:, r * width : (r + 1) * width] = attended[r * rows : (r + 1) * rows]
        gq_ref[:, r * width : (r + 1) * width] = gq[r * rows : (r + 1) * rows]
    gk = (dot(dscore, query, (1, 0)) * SCALE).astype(jnp.bfloat16)
    gv = dot(weights, upstream, (1, 0)).astype(jnp.bfloat16)
    gn_ref[:, :width] = gk[:span]
    gn_ref[:, width:] = gv[:span]
    gc_ref[...] = jnp.zeros_like(gc_ref)
    for slot in range(slots):
        low = span + slot * BLK

        @pl.when(listed[slot] >= 0)
        def _():
            block = slot * blocks_per_store + listed[slot]
            target = pl.ds(pl.multiple_of(block * BLK, BLK), BLK)
            gc_ref[target, :width] = gk[low : low + BLK]
            gc_ref[target, width:] = gv[low : low + BLK]


def attention(listed, queries, upstream, noisy_keys, noisy_values, clean, slots, blocks_per_store):
    rows = queries.shape[0]
    clean_rows = clean.shape[0]
    span = sum(part.shape[0] for part in noisy_keys)
    total = span + slots * BLK
    group_width = HEADS_PER_GROUP * HEAD_SIZE

    def column(width, first=0):
        return lambda h, listed: (0, first + h)

    wide = pl.BlockSpec((rows, group_width), column(group_width))
    noisy_specs = [pl.BlockSpec((part.shape[0], HEAD_SIZE), column(HEAD_SIZE)) for part in noisy_keys]
    return pl.pallas_call(
        functools.partial(attention_kernel, len(noisy_keys), slots, blocks_per_store),
        grid_spec=pltpu.PrefetchScalarGridSpec(
            num_scalar_prefetch=1,
            grid=(KEY_VALUE_HEADS,),
            in_specs=[
                wide,
                wide,
                *noisy_specs,
                *noisy_specs,
                pl.BlockSpec((clean_rows, HEAD_SIZE), column(HEAD_SIZE)),
                pl.BlockSpec((clean_rows, HEAD_SIZE), column(HEAD_SIZE, KEY_VALUE_HEADS)),
            ],
            out_specs=[
                wide,
                wide,
                pl.BlockSpec((span, 2 * HEAD_SIZE), column(2 * HEAD_SIZE)),
                pl.BlockSpec((clean_rows, 2 * HEAD_SIZE), column(2 * HEAD_SIZE)),
            ],
            scratch_shapes=[
                pltpu.VMEM((total, HEAD_SIZE), jnp.bfloat16),
                pltpu.VMEM((total, HEAD_SIZE), jnp.bfloat16),
            ],
        ),
        out_shape=[
            jax.ShapeDtypeStruct(queries.shape, jnp.bfloat16),
            jax.ShapeDtypeStruct(queries.shape, jnp.bfloat16),
            jax.ShapeDtypeStruct((span, 2 * KEY_VALUE_HEADS * HEAD_SIZE), jnp.bfloat16),
            jax.ShapeDtypeStruct((clean_rows, 2 * KEY_VALUE_HEADS * HEAD_SIZE), jnp.bfloat16),
        ],
        compiler_params=pltpu.CompilerParams(vmem_limit_bytes=56 * 2**20),
        cost_estimate=pl.CostEstimate(
            flops=12 * rows * QUERY_HEADS * HEAD_SIZE * total,
            bytes_accessed=8 * rows * QUERY_HEADS * HEAD_SIZE,
            transcendentals=rows * QUERY_HEADS * total,
        ),
        name="span_attention",
    )(listed, queries, upstream, *noisy_keys, *noisy_values, clean, clean)


def unpaired(pairs):
    split = pairs.reshape(pairs.shape[0], KEY_VALUE_HEADS, 2, HEAD_SIZE)
    width = KEY_VALUE_HEADS * HEAD_SIZE
    return (split[:, :, 0].reshape(-1, width), split[:, :, 1].reshape(-1, width))


def shards(
    queries,
    noisy_token_keys,
    noisy_token_values,
    clean_token_keys,
    clean_token_values,
    output_gradient,
    history_list,
):
    ctx_count = lax.axis_size("ctx")
    head_count = lax.axis_size("head")
    position = lax.axis_index("ctx")
    rows = queries.shape[0]
    blocks_per_store = clean_token_keys.shape[0] * head_count // BLK
    slots = ctx_count - 2
    listed = lax.dynamic_index_in_dim(history_list, position, 0, keepdims=False)

    clean = lax.all_gather(
        jnp.concatenate([clean_token_keys, clean_token_values], 1),
        ("ctx", "head"),
        axis=0,
        tiled=True,
    )

    own_keys = [noisy_token_keys] + [
        shifted(noisy_token_keys, "head", step) for step in range(1, head_count)
    ]
    own_values = [noisy_token_values] + [
        shifted(noisy_token_values, "head", step) for step in range(1, head_count)
    ]
    noisy_keys = own_keys + [swapped(part, "ctx", 0) for part in own_keys]
    noisy_values = own_values + [swapped(part, "ctx", 0) for part in own_values]

    attended, query_grad, noisy_grad, clean_grad = attention(
        listed,
        queries,
        output_gradient,
        noisy_keys,
        noisy_values,
        clean,
        slots,
        blocks_per_store,
    )

    clean_total = lax.psum_scatter(clean_grad, ("ctx", "head"), scatter_dimension=0, tiled=True)

    half = head_count * rows
    group_grad = noisy_grad[:half].astype(jnp.float32) + swapped(
        noisy_grad[half:], "ctx", 0
    ).astype(jnp.float32)
    noisy_total = group_grad[:rows]
    for step in range(1, head_count):
        part = group_grad[step * rows : (step + 1) * rows].astype(jnp.bfloat16)
        noisy_total = noisy_total + shifted(part, "head", -step).astype(jnp.float32)
    return (
        attended,
        query_grad,
        *unpaired(noisy_total.astype(jnp.bfloat16)),
        *unpaired(clean_total.astype(jnp.bfloat16)),
    )


def solution(mesh):
    split = P(("ctx", "head"), None)
    return jax.shard_map(
        shards,
        mesh=mesh,
        in_specs=(split, split, split, split, split, split, P()),
        out_specs=(split,) * 6,
        check_vma=False,
    )
```

```python
import functools

import jax
import jax.numpy as jnp
from jax import lax
from jax.experimental import pallas as pl
from jax.experimental.pallas import tpu as pltpu
from jax.sharding import PartitionSpec as P

QUERY_HEADS = 48
KEY_VALUE_HEADS = 8
HEAD_SIZE = 128
BLK = 32
HEADS_PER_GROUP = QUERY_HEADS // KEY_VALUE_HEADS
GROUP_WIDTH = HEADS_PER_GROUP * HEAD_SIZE
SCALE = HEAD_SIZE**-0.5
LOG2E = 1.4426950408889634
CHUNKS = 2

NEG_FILL = -1e30


def flipped(block, bits):
    count = lax.axis_size("ctx")
    return lax.ppermute(block, "ctx", [(i, i ^ bits) for i in range(count)])


def shifted(block, step):
    count = lax.axis_size("head")
    return lax.ppermute(block, "head", [(i, (i + step) % count) for i in range(count)])


def dot(a, b, contract):
    return lax.dot_general(
        a, b, ((contract[:1], contract[1:]), ((), ())), preferred_element_type=jnp.float32
    )


def lanes(start, size):
    return pl.ds(pl.multiple_of(start, HEAD_SIZE), size)


def pack_kernel(head_count, chunks, place, k_noisy, v_noisy, k_clean, v_clean, *outs):
    rows = k_noisy.shape[0]
    half = k_noisy.shape[1] // head_count
    width = half // chunks
    for chunk in range(chunks):
        for step in range(head_count):
            out = outs[chunk * head_count + step]
            target = lax.rem(place[1] + step, head_count)
            source = lanes(target * half + chunk * width, width)
            out[:rows, :width] = k_noisy[:, source]
            out[:rows, width:] = v_noisy[:, source]
            out[rows:, :width] = k_clean[:, source]
            out[rows:, width:] = v_clean[:, source]


def packed(place, head_count, chunks, k_noisy, v_noisy, k_clean, v_clean):
    rows = k_noisy.shape[0] + k_clean.shape[0]
    width = 2 * k_noisy.shape[1] // head_count // chunks
    vmem = pl.BlockSpec(memory_space=pltpu.VMEM)
    outs = pl.pallas_call(
        functools.partial(pack_kernel, head_count, chunks),
        in_specs=[pl.BlockSpec(memory_space=pltpu.SMEM)] + [vmem] * 4,
        out_specs=[vmem] * (chunks * head_count),
        out_shape=[jax.ShapeDtypeStruct((rows, width), jnp.bfloat16)] * (chunks * head_count),
        name="pack_keys_values",
    )(place, k_noisy, v_noisy, k_clean, v_clean)
    return [outs[c * head_count : (c + 1) * head_count] for c in range(chunks)]


def attention_kernel(shape, listed, place, *refs):
    head_count, group_rows, store_rows, clean_rows, slots, aliased = shape
    q_parts, g_parts = refs[:head_count], refs[head_count : 2 * head_count]
    near, far = refs[2 * head_count : 2 * head_count + 2]
    o_own, gq_own, *sends = refs[2 * head_count + 2 + aliased : -4]
    near_grad, far_grad, k_all, v_all = refs[-4:]
    width = HEAD_SIZE
    rows = q_parts[0].shape[0]
    position, head = place[0], place[1]
    member = pl.program_id(0)
    half = near.shape[1] // 2
    k_cols = lanes(member * width, width)
    v_cols = lanes(half + member * width, width)
    depth = lax.div(near.shape[0] - group_rows, 2 * store_rows)

    def placed(slot):
        apart = lax.bitwise_xor(position, slot)
        store = lax.bitwise_and(lax.shift_right_logical(apart, 1), 1) * depth
        store = store + lax.shift_right_logical(apart, 2)
        block = jnp.maximum(listed[position, slot], 0)
        if clean_rows >= BLK:
            owner = lax.div(block * BLK, clean_rows)
            step = lax.rem(head - owner + head_count, head_count)
            inside = step * clean_rows + block * BLK - owner * clean_rows
        else:
            inside = block * BLK
        start = pl.multiple_of(group_rows + store * store_rows + inside, BLK)
        return lax.bitwise_and(apart, 1), pl.ds(start, BLK)

    k_all[:group_rows, :] = near[:group_rows, k_cols]
    v_all[:group_rows, :] = near[:group_rows, v_cols]
    k_all[group_rows : 2 * group_rows, :] = far[:group_rows, k_cols]
    v_all[group_rows : 2 * group_rows, :] = far[:group_rows, v_cols]
    span = 2 * group_rows
    for slot in range(slots):
        other, source = placed(slot)
        to = slice(span + slot * BLK, span + (slot + 1) * BLK)
        k_all[to, :] = jnp.where(other == 1, far[source, k_cols], near[source, k_cols])
        v_all[to, :] = jnp.where(other == 1, far[source, v_cols], near[source, v_cols])

    keys = k_all[...]
    values = v_all[...]

    def stacked(parts):
        return jnp.concatenate(
            [
                part[:, r * width : (r + 1) * width]
                for r in range(HEADS_PER_GROUP)
                for part in parts
            ],
            0,
        )

    query = stacked(q_parts)
    upstream = stacked(g_parts)
    keys_t = keys.T
    values_t = values.T
    upstream_t = upstream.T

    scores = dot(keys, query, (1, 1)) * (SCALE * LOG2E)
    pieces = [scores[:span]]
    for slot in range(slots):
        low = span + slot * BLK
        bias = jnp.where(listed[position, slot] >= 0, 0.0, NEG_FILL).astype(jnp.float32)
        pieces.append(scores[low : low + BLK] + bias)
    scores = jnp.concatenate(pieces, 0)
    top = jnp.max(scores, 0, keepdims=True)
    unscaled = jnp.exp2(scores - top)
    prob = unscaled * (1.0 / jnp.sum(unscaled, 0, keepdims=True))
    weights = prob.astype(jnp.bfloat16)
    attended_t = dot(values_t, weights, (1, 0)).astype(jnp.bfloat16)
    row_dot = jnp.sum(
        attended_t.astype(jnp.float32) * upstream_t.astype(jnp.float32), 0, keepdims=True
    )
    dprob = dot(values, upstream, (1, 1))
    dscore = (prob * (dprob - row_dot)).astype(jnp.bfloat16)
    gq_t = (dot(keys_t, dscore, (1, 0)) * SCALE).astype(jnp.bfloat16)
    attended = attended_t.T
    gq = gq_t.T
    at = 0
    for r in range(HEADS_PER_GROUP):
        to = slice(r * width, (r + 1) * width)
        for part in range(head_count):
            if part:
                sends[part - 1][:rows, to] = attended[at : at + rows]
                sends[part - 1][rows:, to] = gq[at : at + rows]
            else:
                o_own[:, to] = attended[at : at + rows]
                gq_own[:, to] = gq[at : at + rows]
            at += rows
    gk = (dot(dscore, query, (1, 0)) * SCALE).astype(jnp.bfloat16)
    gv = dot(weights, upstream, (1, 0)).astype(jnp.bfloat16)
    for index, grad in enumerate((near_grad, far_grad)):
        here = slice(index * group_rows, (index + 1) * group_rows)
        grad[:group_rows, k_cols] = gk[here]
        grad[:group_rows, v_cols] = gv[here]
        rest = grad.shape[0] - group_rows
        grad[group_rows:, k_cols] = jnp.zeros((rest, width), jnp.bfloat16)
        grad[group_rows:, v_cols] = jnp.zeros((rest, width), jnp.bfloat16)
    for slot in range(slots):
        other, target = placed(slot)
        low = span + slot * BLK
        for index, grad in enumerate((near_grad, far_grad)):

            @pl.when(jnp.logical_and(listed[position, slot] >= 0, other == index))
            def _():
                grad[target, k_cols] = gk[low : low + BLK]
                grad[target, v_cols] = gv[low : low + BLK]


def attention(listed, place, chunk, members, q_parts, g_parts, near, far, carried, shape):
    head_count, group_rows, store_rows, clean_rows, slots = shape
    rows, full_width = q_parts[0].shape
    per_device = KEY_VALUE_HEADS // head_count
    total = 2 * group_rows + slots * BLK

    own = pl.BlockSpec(
        (rows, GROUP_WIDTH), lambda m, l, place: (0, place[1] * per_device + chunk * members + m)
    )
    part = pl.BlockSpec((rows, GROUP_WIDTH), lambda m, l, place: (0, m))
    pair = pl.BlockSpec((2 * rows, GROUP_WIDTH), lambda m, l, place: (0, m))
    whole = pl.BlockSpec(near.shape, lambda m, l, place: (0, 0))
    others = head_count - 1
    first_carried = 2 + 2 * head_count + 2
    return pl.pallas_call(
        functools.partial(attention_kernel, (*shape, len(carried))),
        grid_spec=pltpu.PrefetchScalarGridSpec(
            num_scalar_prefetch=2,
            grid=(members,),
            in_specs=[own, *[part] * others, own, *[part] * others, whole, whole]
            + [pl.BlockSpec(memory_space=pl.ANY)] * len(carried),
            out_specs=[own, own, *[pair] * others, whole, whole],
            scratch_shapes=[
                pltpu.VMEM((total, HEAD_SIZE), jnp.bfloat16),
                pltpu.VMEM((total, HEAD_SIZE), jnp.bfloat16),
            ],
        ),
        out_shape=[
            jax.ShapeDtypeStruct((rows, full_width), jnp.bfloat16),
            jax.ShapeDtypeStruct((rows, full_width), jnp.bfloat16),
            *[jax.ShapeDtypeStruct((2 * rows, members * GROUP_WIDTH), jnp.bfloat16)] * others,
            jax.ShapeDtypeStruct(near.shape, jnp.bfloat16),
            jax.ShapeDtypeStruct(near.shape, jnp.bfloat16),
        ],
        input_output_aliases={first_carried + i: i for i in range(len(carried))},
        compiler_params=pltpu.CompilerParams(vmem_limit_bytes=56 * 2**20),
        cost_estimate=pl.CostEstimate(
            flops=24 * group_rows * members * HEADS_PER_GROUP * HEAD_SIZE * total,
            bytes_accessed=16 * group_rows * members * GROUP_WIDTH,
            transcendentals=group_rows * members * HEADS_PER_GROUP * total,
        ),
        name="span_attention",
    )(listed, place, *q_parts, *g_parts, near, far, *carried)


def canonical(parts, head):
    count = len(parts)
    if count == 1:
        return parts[0]
    if count == 2:
        return jnp.where(
            head == 0, jnp.concatenate(parts, 1), jnp.concatenate(parts[::-1], 1)
        )
    stack = jnp.stack(parts)
    order = lax.rem(head - jnp.arange(count, dtype=jnp.int32) + count, count)
    return jnp.concatenate(list(stack[order]), 1)


def shards(
    queries,
    noisy_token_keys,
    noisy_token_values,
    clean_token_keys,
    clean_token_values,
    output_gradient,
    history_list,
):
    ctx_count = lax.axis_size("ctx")
    head_count = lax.axis_size("head")
    head = lax.axis_index("head")
    place = jnp.stack([lax.axis_index("ctx"), head]).astype(jnp.int32)
    rows = queries.shape[0]
    clean_rows = clean_token_keys.shape[0]
    store_rows = clean_rows * head_count
    group_rows = rows * head_count
    slots = ctx_count - 2
    per_device = KEY_VALUE_HEADS // head_count
    chunks = CHUNKS if per_device % CHUNKS == 0 else 1
    members = per_device // chunks
    depth = ctx_count // 4
    steps = range(1, head_count)
    row_order = lax.rem(head - jnp.arange(head_count, dtype=jnp.int32) + head_count, head_count)

    def by_block(store):
        if clean_rows >= BLK:
            return store
        return store.reshape(head_count, clean_rows, -1)[row_order].reshape(store.shape)

    packs = packed(
        place,
        head_count,
        chunks,
        noisy_token_keys,
        noisy_token_values,
        clean_token_keys,
        clean_token_values,
    )
    arrived = [
        [packs[c][0]] + [shifted(packs[c][step], step) for step in steps] for c in range(chunks)
    ]

    def columns(array, chunk, step):
        target = lax.rem(head + step, head_count)
        start = (target * per_device + chunk * members) * GROUP_WIDTH
        return lax.dynamic_slice_in_dim(array, start, members * GROUP_WIDTH, 1)

    q_parts = [
        [queries] + [shifted(columns(queries, c, step), step) for step in steps]
        for c in range(chunks)
    ]
    g_parts = [
        [output_gradient] + [shifted(columns(output_gradient, c, step), step) for step in steps]
        for c in range(chunks)
    ]

    carried = ()
    sent = []
    grads = []
    for c in range(chunks):
        noisy = [part[:rows] for part in arrived[c]]
        store = by_block(jnp.concatenate([part[rows:] for part in arrived[c]], 0))
        line = jnp.concatenate([store] + [flipped(store, z << 2) for z in range(1, depth)], 0)
        near = jnp.concatenate(noisy + [line, flipped(line, 2)], 0)
        far = flipped(near, 1)
        *carried, near_grad, far_grad = attention(
            history_list,
            place,
            c,
            members,
            q_parts[c],
            g_parts[c],
            near,
            far,
            carried,
            (head_count, group_rows, store_rows, clean_rows, slots),
        )
        sends = carried[2:]
        carried = carried[:2]
        sent.append([shifted(block, -step) for step, block in zip(steps, sends)])

        line_rows = depth * store_rows
        total = near_grad.astype(jnp.float32) + flipped(far_grad, 1).astype(jnp.float32)
        noisy_sum = total[:group_rows]
        keep = total[group_rows : group_rows + line_rows]
        give = total[group_rows + line_rows :].astype(jnp.bfloat16)
        line_sum = keep + flipped(give, 2).astype(jnp.float32)
        store_sum = line_sum[:store_rows]
        for z in range(1, depth):
            give = line_sum[z * store_rows : (z + 1) * store_rows].astype(jnp.bfloat16)
            store_sum = store_sum + flipped(give, z << 2).astype(jnp.float32)
        if clean_rows < BLK:
            store_sum = store_sum.reshape(head_count, clean_rows, -1)[row_order].reshape(
                store_sum.shape
            )
        store_sum = store_sum.astype(jnp.bfloat16)
        noisy_sum = noisy_sum.astype(jnp.bfloat16)
        mixed = [
            jnp.concatenate(
                [
                    noisy_sum[step * rows : (step + 1) * rows],
                    store_sum[step * clean_rows : (step + 1) * clean_rows],
                ],
                0,
            )
            for step in range(head_count)
        ]
        grads.append([mixed[0]] + [shifted(mixed[step], -step) for step in steps])

    attended, query_grad = carried
    for c in range(chunks):
        for step, block in zip(steps, sent[c]):
            source = lax.rem(head + step, head_count)
            start = (source * per_device + c * members) * GROUP_WIDTH
            attended = lax.dynamic_update_slice_in_dim(attended, block[:rows], start, 1)
            query_grad = lax.dynamic_update_slice_in_dim(query_grad, block[rows:], start, 1)

    width = members * HEAD_SIZE
    finished = []
    for first in (0, width):
        joined = [
            jnp.concatenate([grads[c][step][:, first : first + width] for c in range(chunks)], 1)
            for step in range(head_count)
        ]
        joined = joined[:1] + joined[:0:-1]
        finished.append(canonical(joined, head))
    return (
        attended,
        query_grad,
        finished[0][:rows],
        finished[1][:rows],
        finished[0][rows:],
        finished[1][rows:],
    )


def solution(mesh):
    split = P(("ctx", "head"), None)
    return jax.shard_map(
        shards,
        mesh=mesh,
        in_specs=(split, split, split, split, split, split, P()),
        out_specs=(split,) * 6,
        check_vma=False,
    )
```

```python
import functools

import jax
import jax.numpy as jnp
from jax import lax
from jax.experimental import pallas as pl
from jax.experimental.pallas import tpu as pltpu
from jax.sharding import PartitionSpec as P

QUERY_HEADS = 48
KEY_VALUE_HEADS = 8
HEAD_SIZE = 128
BLK = 32
HEADS_PER_GROUP = QUERY_HEADS // KEY_VALUE_HEADS
GROUP_WIDTH = HEADS_PER_GROUP * HEAD_SIZE
SCALE = HEAD_SIZE**-0.5
LOG2E = 1.4426950408889634
CHUNKS = 2
SLICE_HEADS = 2

NEG_FILL = -1e30


def flipped(block, bits):
    count = lax.axis_size("ctx")
    return lax.ppermute(block, "ctx", [(i, i ^ bits) for i in range(count)])


def shifted(block, step):
    count = lax.axis_size("head")
    return lax.ppermute(block, "head", [(i, (i + step) % count) for i in range(count)])


def dot(a, b, contract):
    return lax.dot_general(
        a, b, ((contract[:1], contract[1:]), ((), ())), preferred_element_type=jnp.float32
    )


def lanes(start, size):
    return pl.ds(pl.multiple_of(start, HEAD_SIZE), size)


def pack_kernel(head_count, chunks, place, k_noisy, v_noisy, k_clean, v_clean, *outs):
    rows = k_noisy.shape[0]
    half = k_noisy.shape[1] // head_count
    width = half // chunks
    for chunk in range(chunks):
        for step in range(head_count):
            out = outs[chunk * head_count + step]
            target = lax.rem(place[1] + step, head_count)
            source = lanes(target * half + chunk * width, width)
            out[:rows, :width] = k_noisy[:, source]
            out[:rows, width:] = v_noisy[:, source]
            out[rows:, :width] = k_clean[:, source]
            out[rows:, width:] = v_clean[:, source]


def packed(place, head_count, chunks, k_noisy, v_noisy, k_clean, v_clean):
    rows = k_noisy.shape[0] + k_clean.shape[0]
    width = 2 * k_noisy.shape[1] // head_count // chunks
    vmem = pl.BlockSpec(memory_space=pltpu.VMEM)
    outs = pl.pallas_call(
        functools.partial(pack_kernel, head_count, chunks),
        in_specs=[pl.BlockSpec(memory_space=pltpu.SMEM)] + [vmem] * 4,
        out_specs=[vmem] * (chunks * head_count),
        out_shape=[jax.ShapeDtypeStruct((rows, width), jnp.bfloat16)] * (chunks * head_count),
        name="pack_keys_values",
    )(place, k_noisy, v_noisy, k_clean, v_clean)
    return [outs[c * head_count : (c + 1) * head_count] for c in range(chunks)]


def attention_kernel(shape, listed, place, *refs):
    head_count, group_rows, store_rows, clean_rows, slots, aliased = shape
    q_parts, g_parts = refs[:head_count], refs[head_count : 2 * head_count]
    near, far = refs[2 * head_count : 2 * head_count + 2]
    o_own, gq_own, *sends = refs[2 * head_count + 2 + aliased : -4]
    near_grad, far_grad, k_all, v_all = refs[-4:]
    width = HEAD_SIZE
    rows = q_parts[0].shape[0]
    position, head = place[0], place[1]
    member = pl.program_id(0)
    half = near.shape[1] // 2
    k_cols = lanes(member * width, width)
    v_cols = lanes(half + member * width, width)
    depth = lax.div(near.shape[0] - group_rows, 2 * store_rows)

    def placed(slot):
        apart = lax.bitwise_xor(position, slot)
        store = lax.bitwise_and(lax.shift_right_logical(apart, 1), 1) * depth
        store = store + lax.shift_right_logical(apart, 2)
        block = jnp.maximum(listed[position, slot], 0)
        if clean_rows >= BLK:
            owner = lax.div(block * BLK, clean_rows)
            step = lax.rem(head - owner + head_count, head_count)
            inside = step * clean_rows + block * BLK - owner * clean_rows
        else:
            inside = block * BLK
        start = pl.multiple_of(group_rows + store * store_rows + inside, BLK)
        return lax.bitwise_and(apart, 1), pl.ds(start, BLK)

    k_all[:group_rows, :] = near[:group_rows, k_cols]
    v_all[:group_rows, :] = near[:group_rows, v_cols]
    k_all[group_rows : 2 * group_rows, :] = far[:group_rows, k_cols]
    v_all[group_rows : 2 * group_rows, :] = far[:group_rows, v_cols]
    span = 2 * group_rows
    total = span + slots * BLK
    for slot in range(slots):
        other, source = placed(slot)
        to = slice(span + slot * BLK, span + (slot + 1) * BLK)
        k_all[to, :] = jnp.where(other == 1, far[source, k_cols], near[source, k_cols])
        v_all[to, :] = jnp.where(other == 1, far[source, v_cols], near[source, v_cols])

    keys = k_all[...]
    values = v_all[...]

    keys_t = keys.T
    values_t = values.T
    biases = [
        jnp.where(listed[position, slot] >= 0, 0.0, NEG_FILL).astype(jnp.float32)
        for slot in range(slots)
    ]
    gk = jnp.zeros((total, width), jnp.float32)
    gv = jnp.zeros((total, width), jnp.float32)
    for first in range(0, HEADS_PER_GROUP, SLICE_HEADS):
        heads = range(first, first + SLICE_HEADS)

        def stacked(parts):
            return jnp.concatenate(
                [part[:, r * width : (r + 1) * width] for r in heads for part in parts], 0
            )

        query = stacked(q_parts)
        upstream = stacked(g_parts)
        upstream_t = upstream.T
        scores = dot(keys, query, (1, 1)) * (SCALE * LOG2E)
        pieces = [scores[:span]]
        for slot in range(slots):
            low = span + slot * BLK
            pieces.append(scores[low : low + BLK] + biases[slot])
        scores = jnp.concatenate(pieces, 0)
        top = jnp.max(scores, 0, keepdims=True)
        unscaled = jnp.exp2(scores - top)
        prob = unscaled * (1.0 / jnp.sum(unscaled, 0, keepdims=True))
        weights = prob.astype(jnp.bfloat16)
        attended_t = dot(values_t, weights, (1, 0)).astype(jnp.bfloat16)
        row_dot = jnp.sum(
            attended_t.astype(jnp.float32) * upstream_t.astype(jnp.float32), 0, keepdims=True
        )
        dprob = dot(values, upstream, (1, 1))
        dscore = (prob * (dprob - row_dot)).astype(jnp.bfloat16)
        gq_t = (dot(keys_t, dscore, (1, 0)) * SCALE).astype(jnp.bfloat16)
        gk = gk + dot(dscore, query, (1, 0))
        gv = gv + dot(weights, upstream, (1, 0))
        attended = attended_t.T
        gq = gq_t.T
        at = 0
        for r in heads:
            to = slice(r * width, (r + 1) * width)
            for part in range(head_count):
                if part:
                    sends[part - 1][:rows, to] = attended[at : at + rows]
                    sends[part - 1][rows:, to] = gq[at : at + rows]
                else:
                    o_own[:, to] = attended[at : at + rows]
                    gq_own[:, to] = gq[at : at + rows]
                at += rows
    gk = (gk * SCALE).astype(jnp.bfloat16)
    gv = gv.astype(jnp.bfloat16)
    for index, grad in enumerate((near_grad, far_grad)):
        here = slice(index * group_rows, (index + 1) * group_rows)
        grad[:group_rows, k_cols] = gk[here]
        grad[:group_rows, v_cols] = gv[here]
        rest = grad.shape[0] - group_rows
        grad[group_rows:, k_cols] = jnp.zeros((rest, width), jnp.bfloat16)
        grad[group_rows:, v_cols] = jnp.zeros((rest, width), jnp.bfloat16)
    for slot in range(slots):
        other, target = placed(slot)
        low = span + slot * BLK
        for index, grad in enumerate((near_grad, far_grad)):

            @pl.when(jnp.logical_and(listed[position, slot] >= 0, other == index))
            def _():
                grad[target, k_cols] = gk[low : low + BLK]
                grad[target, v_cols] = gv[low : low + BLK]


def attention(listed, place, chunk, members, q_parts, g_parts, near, far, carried, shape):
    head_count, group_rows, store_rows, clean_rows, slots = shape
    rows, full_width = q_parts[0].shape
    per_device = KEY_VALUE_HEADS // head_count
    total = 2 * group_rows + slots * BLK

    own = pl.BlockSpec(
        (rows, GROUP_WIDTH), lambda m, l, place: (0, place[1] * per_device + chunk * members + m)
    )
    part = pl.BlockSpec((rows, GROUP_WIDTH), lambda m, l, place: (0, m))
    pair = pl.BlockSpec((2 * rows, GROUP_WIDTH), lambda m, l, place: (0, m))
    whole = pl.BlockSpec(near.shape, lambda m, l, place: (0, 0))
    others = head_count - 1
    first_carried = 2 + 2 * head_count + 2
    return pl.pallas_call(
        functools.partial(attention_kernel, (*shape, len(carried))),
        grid_spec=pltpu.PrefetchScalarGridSpec(
            num_scalar_prefetch=2,
            grid=(members,),
            in_specs=[own, *[part] * others, own, *[part] * others, whole, whole]
            + [pl.BlockSpec(memory_space=pl.ANY)] * len(carried),
            out_specs=[own, own, *[pair] * others, whole, whole],
            scratch_shapes=[
                pltpu.VMEM((total, HEAD_SIZE), jnp.bfloat16),
                pltpu.VMEM((total, HEAD_SIZE), jnp.bfloat16),
            ],
        ),
        out_shape=[
            jax.ShapeDtypeStruct((rows, full_width), jnp.bfloat16),
            jax.ShapeDtypeStruct((rows, full_width), jnp.bfloat16),
            *[jax.ShapeDtypeStruct((2 * rows, members * GROUP_WIDTH), jnp.bfloat16)] * others,
            jax.ShapeDtypeStruct(near.shape, jnp.bfloat16),
            jax.ShapeDtypeStruct(near.shape, jnp.bfloat16),
        ],
        input_output_aliases={first_carried + i: i for i in range(len(carried))},
        compiler_params=pltpu.CompilerParams(vmem_limit_bytes=56 * 2**20),
        cost_estimate=pl.CostEstimate(
            flops=24 * group_rows * members * HEADS_PER_GROUP * HEAD_SIZE * total,
            bytes_accessed=16 * group_rows * members * GROUP_WIDTH,
            transcendentals=group_rows * members * HEADS_PER_GROUP * total,
        ),
        name="span_attention",
    )(listed, place, *q_parts, *g_parts, near, far, *carried)


def canonical(parts, head):
    count = len(parts)
    if count == 1:
        return parts[0]
    if count == 2:
        return jnp.where(
            head == 0, jnp.concatenate(parts, 1), jnp.concatenate(parts[::-1], 1)
        )
    stack = jnp.stack(parts)
    order = lax.rem(head - jnp.arange(count, dtype=jnp.int32) + count, count)
    return jnp.concatenate(list(stack[order]), 1)


def shards(
    queries,
    noisy_token_keys,
    noisy_token_values,
    clean_token_keys,
    clean_token_values,
    output_gradient,
    history_list,
):
    ctx_count = lax.axis_size("ctx")
    head_count = lax.axis_size("head")
    head = lax.axis_index("head")
    place = jnp.stack([lax.axis_index("ctx"), head]).astype(jnp.int32)
    rows = queries.shape[0]
    clean_rows = clean_token_keys.shape[0]
    store_rows = clean_rows * head_count
    group_rows = rows * head_count
    slots = ctx_count - 2
    per_device = KEY_VALUE_HEADS // head_count
    chunks = CHUNKS if per_device % CHUNKS == 0 else 1
    members = per_device // chunks
    depth = ctx_count // 4
    steps = range(1, head_count)
    row_order = lax.rem(head - jnp.arange(head_count, dtype=jnp.int32) + head_count, head_count)

    def by_block(store):
        if clean_rows >= BLK:
            return store
        return store.reshape(head_count, clean_rows, -1)[row_order].reshape(store.shape)

    packs = packed(
        place,
        head_count,
        chunks,
        noisy_token_keys,
        noisy_token_values,
        clean_token_keys,
        clean_token_values,
    )
    arrived = [
        [packs[c][0]] + [shifted(packs[c][step], step) for step in steps] for c in range(chunks)
    ]

    def columns(array, chunk, step):
        target = lax.rem(head + step, head_count)
        start = (target * per_device + chunk * members) * GROUP_WIDTH
        return lax.dynamic_slice_in_dim(array, start, members * GROUP_WIDTH, 1)

    q_parts = [
        [queries] + [shifted(columns(queries, c, step), step) for step in steps]
        for c in range(chunks)
    ]
    g_parts = [
        [output_gradient] + [shifted(columns(output_gradient, c, step), step) for step in steps]
        for c in range(chunks)
    ]

    carried = ()
    sent = []
    grads = []
    for c in range(chunks):
        noisy = [part[:rows] for part in arrived[c]]
        store = by_block(jnp.concatenate([part[rows:] for part in arrived[c]], 0))
        line = jnp.concatenate([store] + [flipped(store, z << 2) for z in range(1, depth)], 0)
        near = jnp.concatenate(noisy + [line, flipped(line, 2)], 0)
        far = flipped(near, 1)
        *carried, near_grad, far_grad = attention(
            history_list,
            place,
            c,
            members,
            q_parts[c],
            g_parts[c],
            near,
            far,
            carried,
            (head_count, group_rows, store_rows, clean_rows, slots),
        )
        sends = carried[2:]
        carried = carried[:2]
        sent.append([shifted(block, -step) for step, block in zip(steps, sends)])

        line_rows = depth * store_rows
        total = near_grad.astype(jnp.float32) + flipped(far_grad, 1).astype(jnp.float32)
        noisy_sum = total[:group_rows]
        keep = total[group_rows : group_rows + line_rows]
        give = total[group_rows + line_rows :].astype(jnp.bfloat16)
        line_sum = keep + flipped(give, 2).astype(jnp.float32)
        store_sum = line_sum[:store_rows]
        for z in range(1, depth):
            give = line_sum[z * store_rows : (z + 1) * store_rows].astype(jnp.bfloat16)
            store_sum = store_sum + flipped(give, z << 2).astype(jnp.float32)
        if clean_rows < BLK:
            store_sum = store_sum.reshape(head_count, clean_rows, -1)[row_order].reshape(
                store_sum.shape
            )
        store_sum = store_sum.astype(jnp.bfloat16)
        noisy_sum = noisy_sum.astype(jnp.bfloat16)
        mixed = [
            jnp.concatenate(
                [
                    noisy_sum[step * rows : (step + 1) * rows],
                    store_sum[step * clean_rows : (step + 1) * clean_rows],
                ],
                0,
            )
            for step in range(head_count)
        ]
        grads.append([mixed[0]] + [shifted(mixed[step], -step) for step in steps])

    attended, query_grad = carried
    for c in range(chunks):
        for step, block in zip(steps, sent[c]):
            source = lax.rem(head + step, head_count)
            start = (source * per_device + c * members) * GROUP_WIDTH
            attended = lax.dynamic_update_slice_in_dim(attended, block[:rows], start, 1)
            query_grad = lax.dynamic_update_slice_in_dim(query_grad, block[rows:], start, 1)

    width = members * HEAD_SIZE
    finished = []
    for first in (0, width):
        joined = [
            jnp.concatenate([grads[c][step][:, first : first + width] for c in range(chunks)], 1)
            for step in range(head_count)
        ]
        joined = joined[:1] + joined[:0:-1]
        finished.append(canonical(joined, head))
    return (
        attended,
        query_grad,
        finished[0][:rows],
        finished[1][:rows],
        finished[0][rows:],
        finished[1][rows:],
    )


def solution(mesh):
    split = P(("ctx", "head"), None)
    return jax.shard_map(
        shards,
        mesh=mesh,
        in_specs=(split, split, split, split, split, split, P()),
        out_specs=(split,) * 6,
        check_vma=False,
    )
```

```python
import functools

import jax
import jax.numpy as jnp
from jax import lax
from jax.experimental import pallas as pl
from jax.experimental.pallas import tpu as pltpu
from jax.sharding import PartitionSpec as P

QUERY_HEADS = 48
KEY_VALUE_HEADS = 8
HEAD_SIZE = 128
BLK = 32
HEADS_PER_GROUP = QUERY_HEADS // KEY_VALUE_HEADS
GROUP_WIDTH = HEADS_PER_GROUP * HEAD_SIZE
SCALE = HEAD_SIZE**-0.5
LOG2E = 1.4426950408889634
CHUNKS = 2

NEG_FILL = -1e30


def flipped(block, bits):
    count = lax.axis_size("ctx")
    return lax.ppermute(block, "ctx", [(i, i ^ bits) for i in range(count)])


def shifted(block, step):
    count = lax.axis_size("head")
    return lax.ppermute(block, "head", [(i, (i + step) % count) for i in range(count)])


def dot(a, b, contract):
    return lax.dot_general(
        a, b, ((contract[:1], contract[1:]), ((), ())), preferred_element_type=jnp.float32
    )


def lanes(start, size):
    return pl.ds(pl.multiple_of(start, HEAD_SIZE), size)


def pack_kernel(head_count, pieces, place, q, g, k_noisy, v_noisy, k_clean, v_clean, *refs):
    outs, (copied,) = refs[:-1], refs[-1:]
    rows = q.shape[0]
    full = q.shape[1] // head_count
    half = k_noisy.shape[1] // head_count
    moves = []

    def move(source, start, out, to_rows, to_columns):
        size = to_columns.stop - to_columns.start
        moves.append(
            pltpu.make_async_copy(
                source.at[:, lanes(start, size)], out.at[to_rows, to_columns], copied.at[len(moves)]
            )
        )
        moves[-1].start()

    width = HEAD_SIZE
    for step in range(head_count):
        target = lax.rem(place[1] + step, head_count)
        for member in range(half // width):
            start = target * half + member * width
            for index, (noisy, clean) in enumerate(((k_noisy, k_clean), (v_noisy, v_clean))):
                to = slice((2 * member + index) * width, (2 * member + index + 1) * width)
                move(noisy, start, outs[step], slice(0, rows), to)
                move(clean, start, outs[step], slice(rows, outs[step].shape[0]), to)
    at = head_count
    start = 0
    for wide in pieces:
        for step in range(1, head_count):
            target = lax.rem(place[1] + step, head_count)
            move(q, target * full + start, outs[at], slice(0, rows), slice(0, wide))
            move(g, target * full + start, outs[at], slice(rows, 2 * rows), slice(0, wide))
            at += 1
        start += wide
    for copy in moves:
        copy.wait()


def packed(place, head_count, pieces, q, g, k_noisy, v_noisy, k_clean, v_clean):
    rows = q.shape[0]
    far = pl.BlockSpec(memory_space=pl.ANY)
    width = 2 * k_noisy.shape[1] // head_count
    kinds = [((rows + k_clean.shape[0], width), head_count)]
    kinds += [((2 * rows, wide), head_count - 1) for wide in pieces]
    shapes = [jax.ShapeDtypeStruct(k, jnp.bfloat16) for k, count in kinds for _ in range(count)]
    copies = 4 * KEY_VALUE_HEADS + len(pieces) * (head_count - 1) * 2
    outs = pl.pallas_call(
        functools.partial(pack_kernel, head_count, pieces),
        in_specs=[pl.BlockSpec(memory_space=pltpu.SMEM)] + [far] * 6,
        out_specs=[far] * len(shapes),
        out_shape=shapes,
        scratch_shapes=[pltpu.SemaphoreType.DMA((copies,))],
        name="pack_by_head",
    )(place, q, g, k_noisy, v_noisy, k_clean, v_clean)
    wide = outs[head_count:]
    others = head_count - 1
    return outs[:head_count], [wide[i * others : (i + 1) * others] for i in range(len(pieces))]


def attention_kernel(shape, listed, place, *refs):
    head_count, group_rows, store_rows, clean_rows, slots, aliased = shape
    rows = refs[0].shape[0]
    received = refs[2 : head_count + 1]
    q_parts = [refs[0]] + [pair.at[:rows] for pair in received]
    g_parts = [refs[1]] + [pair.at[rows:] for pair in received]
    near, far = refs[head_count + 1 : head_count + 3]
    o_own, gq_own, *sends = refs[head_count + 3 + aliased : -4]
    near_grad, far_grad, k_all, v_all = refs[-4:]
    width = HEAD_SIZE
    position, head = place[0], place[1]
    k_cols = slice(0, width)
    v_cols = slice(width, 2 * width)
    depth = lax.div(near.shape[0] - group_rows, 2 * store_rows)

    def placed(slot):
        apart = lax.bitwise_xor(position, slot)
        store = lax.bitwise_and(lax.shift_right_logical(apart, 1), 1) * depth
        store = store + lax.shift_right_logical(apart, 2)
        block = jnp.maximum(listed[position, slot], 0)
        if clean_rows >= BLK:
            owner = lax.div(block * BLK, clean_rows)
            step = lax.rem(head - owner + head_count, head_count)
            inside = step * clean_rows + block * BLK - owner * clean_rows
        else:
            inside = block * BLK
        start = pl.multiple_of(group_rows + store * store_rows + inside, BLK)
        return lax.bitwise_and(apart, 1), pl.ds(start, BLK)

    k_all[:group_rows, :] = near[:group_rows, k_cols]
    v_all[:group_rows, :] = near[:group_rows, v_cols]
    k_all[group_rows : 2 * group_rows, :] = far[:group_rows, k_cols]
    v_all[group_rows : 2 * group_rows, :] = far[:group_rows, v_cols]
    span = 2 * group_rows
    for slot in range(slots):
        other, source = placed(slot)
        to = slice(span + slot * BLK, span + (slot + 1) * BLK)
        k_all[to, :] = jnp.where(other == 1, far[source, k_cols], near[source, k_cols])
        v_all[to, :] = jnp.where(other == 1, far[source, v_cols], near[source, v_cols])

    keys = k_all[...]
    values = v_all[...]

    def stacked(parts):
        return jnp.concatenate(
            [
                part[:, r * width : (r + 1) * width]
                for r in range(HEADS_PER_GROUP)
                for part in parts
            ],
            0,
        )

    query = stacked(q_parts)
    upstream = stacked(g_parts)
    keys_t = keys.T
    values_t = values.T
    upstream_t = upstream.T

    scores = dot(keys, query, (1, 1)) * (SCALE * LOG2E)
    pieces = [scores[:span]]
    for slot in range(slots):
        low = span + slot * BLK
        bias = jnp.where(listed[position, slot] >= 0, 0.0, NEG_FILL).astype(jnp.float32)
        pieces.append(scores[low : low + BLK] + bias)
    scores = jnp.concatenate(pieces, 0)
    top = jnp.max(scores, 0, keepdims=True)
    unscaled = jnp.exp2(scores - top)
    prob = unscaled * (1.0 / jnp.sum(unscaled, 0, keepdims=True))
    weights = prob.astype(jnp.bfloat16)
    attended_t = dot(values_t, weights, (1, 0)).astype(jnp.bfloat16)
    row_dot = jnp.sum(
        attended_t.astype(jnp.float32) * upstream_t.astype(jnp.float32), 0, keepdims=True
    )
    dprob = dot(values, upstream, (1, 1))
    dscore = (prob * (dprob - row_dot)).astype(jnp.bfloat16)
    gq_t = (dot(keys_t, dscore, (1, 0)) * SCALE).astype(jnp.bfloat16)
    attended = attended_t.T
    gq = gq_t.T
    at = 0
    for r in range(HEADS_PER_GROUP):
        to = slice(r * width, (r + 1) * width)
        for part in range(head_count):
            if part:
                sends[part - 1][:rows, to] = attended[at : at + rows]
                sends[part - 1][rows:, to] = gq[at : at + rows]
            else:
                o_own[:, to] = attended[at : at + rows]
                gq_own[:, to] = gq[at : at + rows]
            at += rows
    gk = (dot(dscore, query, (1, 0)) * SCALE).astype(jnp.bfloat16)
    gv = dot(weights, upstream, (1, 0)).astype(jnp.bfloat16)
    for index, grad in enumerate((near_grad, far_grad)):
        here = slice(index * group_rows, (index + 1) * group_rows)
        grad[:group_rows, k_cols] = gk[here]
        grad[:group_rows, v_cols] = gv[here]
        rest = grad.shape[0] - group_rows
        grad[group_rows:, k_cols] = jnp.zeros((rest, width), jnp.bfloat16)
        grad[group_rows:, v_cols] = jnp.zeros((rest, width), jnp.bfloat16)
    for slot in range(slots):
        other, target = placed(slot)
        low = span + slot * BLK
        for index, grad in enumerate((near_grad, far_grad)):

            @pl.when(jnp.logical_and(listed[position, slot] >= 0, other == index))
            def _():
                grad[target, k_cols] = gk[low : low + BLK]
                grad[target, v_cols] = gv[low : low + BLK]


def attention(listed, place, q, g, received, near, far, carried, shape, head_of_chunk, chunk, within):
    head_count, group_rows, store_rows, clean_rows, slots = shape
    rows, full_width = q.shape
    per_device = KEY_VALUE_HEADS // head_count
    members = near.shape[1] // (2 * HEAD_SIZE)
    total = 2 * group_rows + slots * BLK
    column = chunk * members + head_of_chunk

    own = pl.BlockSpec((rows, GROUP_WIDTH), lambda i, l, place: (0, place[1] * per_device + column))
    arrived = pl.BlockSpec((2 * rows, GROUP_WIDTH), lambda i, l, place: (0, within))
    pair = pl.BlockSpec((2 * rows, GROUP_WIDTH), lambda i, l, place: (0, head_of_chunk))
    keys = pl.BlockSpec((near.shape[0], 2 * HEAD_SIZE), lambda i, l, place: (0, head_of_chunk))
    others = head_count - 1
    first_carried = 2 + head_count + 3
    out_shape = [
        jax.ShapeDtypeStruct((rows, full_width), jnp.bfloat16),
        jax.ShapeDtypeStruct((rows, full_width), jnp.bfloat16),
        *[jax.ShapeDtypeStruct((2 * rows, members * GROUP_WIDTH), jnp.bfloat16)] * others,
        jax.ShapeDtypeStruct(near.shape, jnp.bfloat16),
        jax.ShapeDtypeStruct(near.shape, jnp.bfloat16),
    ]
    return pl.pallas_call(
        functools.partial(attention_kernel, (*shape, len(carried))),
        grid_spec=pltpu.PrefetchScalarGridSpec(
            num_scalar_prefetch=2,
            grid=(1,),
            in_specs=[own, own, *[arrived] * others, keys, keys]
            + [pl.BlockSpec(memory_space=pl.ANY)] * len(carried),
            out_specs=[own, own, *[pair] * others, keys, keys],
            scratch_shapes=[
                pltpu.VMEM((total, HEAD_SIZE), jnp.bfloat16),
                pltpu.VMEM((total, HEAD_SIZE), jnp.bfloat16),
            ],
        ),
        out_shape=out_shape,
        input_output_aliases={first_carried + i: i for i in range(len(carried))},
        compiler_params=pltpu.CompilerParams(vmem_limit_bytes=56 * 2**20),
        cost_estimate=pl.CostEstimate(
            flops=24 * group_rows * HEADS_PER_GROUP * HEAD_SIZE * total,
            bytes_accessed=16 * group_rows * GROUP_WIDTH,
            transcendentals=group_rows * HEADS_PER_GROUP * total,
        ),
        name="span_attention",
    )(listed, place, q, g, *received, near, far, *carried)


def unpack_kernel(head_count, chunks, place, *refs):
    parts, outs = refs[:-4], refs[-4:]
    rows = outs[0].shape[0]
    half = outs[0].shape[1] // head_count
    width = HEAD_SIZE
    members = half // chunks // width
    for step in range(head_count):
        source = lax.rem(place[1] + step, head_count)
        for chunk in range(chunks):
            part = parts[chunk * head_count + step]
            for member in range(members):
                to = lanes(source * half + (chunk * members + member) * width, width)
                for index in range(2):
                    at = (2 * member + index) * width
                    outs[index][:, to] = part[:rows, at : at + width]
                    outs[2 + index][:, to] = part[rows:, at : at + width]


def unpacked(place, head_count, grads, rows, clean_rows):
    vmem = pl.BlockSpec(memory_space=pltpu.VMEM)
    parts = [part for chunk in grads for part in chunk]
    width = KEY_VALUE_HEADS * HEAD_SIZE
    return pl.pallas_call(
        functools.partial(unpack_kernel, head_count, len(grads)),
        in_specs=[pl.BlockSpec(memory_space=pltpu.SMEM)] + [vmem] * len(parts),
        out_specs=[vmem] * 4,
        out_shape=[jax.ShapeDtypeStruct((rows, width), jnp.bfloat16)] * 2
        + [jax.ShapeDtypeStruct((clean_rows, width), jnp.bfloat16)] * 2,
        name="unpack_gradients",
    )(place, *parts)


def shards(
    queries,
    noisy_token_keys,
    noisy_token_values,
    clean_token_keys,
    clean_token_values,
    output_gradient,
    history_list,
):
    ctx_count = lax.axis_size("ctx")
    head_count = lax.axis_size("head")
    head = lax.axis_index("head")
    place = jnp.stack([lax.axis_index("ctx"), head]).astype(jnp.int32)
    rows = queries.shape[0]
    clean_rows = clean_token_keys.shape[0]
    store_rows = clean_rows * head_count
    group_rows = rows * head_count
    slots = ctx_count - 2
    per_device = KEY_VALUE_HEADS // head_count
    chunks = CHUNKS if per_device % CHUNKS == 0 else 1
    members = per_device // chunks
    depth = ctx_count // 4
    steps = range(1, head_count)
    row_order = lax.rem(head - jnp.arange(head_count, dtype=jnp.int32) + head_count, head_count)

    def by_block(store):
        if clean_rows >= BLK:
            return store
        return store.reshape(head_count, clean_rows, -1)[row_order].reshape(store.shape)

    pieces = [members * GROUP_WIDTH] + [GROUP_WIDTH] * (members * (chunks - 1))
    pairs, wide = packed(
        place,
        head_count,
        pieces,
        queries,
        output_gradient,
        noisy_token_keys,
        noisy_token_values,
        clean_token_keys,
        clean_token_values,
    )
    arrived = [pairs[0]] + [shifted(pairs[step], step) for step in steps]
    store = by_block(jnp.concatenate([part[rows:] for part in arrived], 0))
    line = [store] + [flipped(store, z << 2) for z in range(1, depth)]
    part_width = 2 * members * HEAD_SIZE

    def cut(array, chunk):
        return array[:, chunk * part_width : (chunk + 1) * part_width]

    noisy = [part[:rows] for part in arrived]
    lines = [jnp.concatenate([cut(part, c) for part in line], 0) for c in range(chunks)]
    before = arrived[-1]
    received = []
    for block_set in wide[:2]:
        *blocks, before = lax.optimization_barrier((*block_set, before))
        received.append([shifted(block, step) for step, block in zip(steps, blocks)])
        before = received[-1][-1] if head_count > 1 else before

    def met(chunk):
        return flipped(lines[chunk], 2)

    def joined(chunk, crossed):
        return jnp.concatenate([cut(part, chunk) for part in noisy] + [lines[chunk], crossed], 0)

    def summed(near_grad, from_core):
        total = near_grad.astype(jnp.float32) + from_core.astype(jnp.float32)
        middle = group_rows + depth * store_rows
        return total[:group_rows], total[group_rows:middle], total[middle:].astype(jnp.bfloat16)

    def along_line(line_sum):
        gives = [
            line_sum[z * store_rows : (z + 1) * store_rows].astype(jnp.bfloat16)
            for z in range(1, depth)
        ]
        return line_sum[:store_rows], [flipped(g, z << 2) for z, g in enumerate(gives, 1)]

    def swap_heads(noisy_sum, store_sum):
        if clean_rows < BLK:
            store_sum = store_sum.reshape(head_count, clean_rows, -1)[row_order].reshape(
                store_sum.shape
            )
        store_sum = store_sum.astype(jnp.bfloat16)
        noisy_sum = noisy_sum.astype(jnp.bfloat16)
        mixed = [
            jnp.concatenate(
                [
                    noisy_sum[step * rows : (step + 1) * rows],
                    store_sum[step * clean_rows : (step + 1) * clean_rows],
                ],
                0,
            )
            for step in range(head_count)
        ]
        return [mixed[0]] + [shifted(mixed[step], -step) for step in steps]

    shape = (head_count, group_rows, store_rows, clean_rows, slots)
    outputs = ()
    sent = []
    grads = []
    crossing = met(0)
    waiting = None
    for c in range(chunks):
        near = joined(c, crossing)
        if c == 0:
            near, *received[0] = lax.optimization_barrier((near, *received[0]))
        far = flipped(near, 1)
        if c + 1 < chunks:
            crossing = met(c + 1)
        carried = outputs
        for m in range(members):
            piece = 0 if c == 0 else 1 + (c - 1) * members + m
            if m == 1 and c + 1 < chunks:
                ahead = received[1 + c * members]
                crossing, carried, ahead = lax.optimization_barrier((crossing, carried, ahead))
                received[1 + c * members] = ahead
                for later in wide[2 + c * members : 1 + (c + 1) * members]:
                    *blocks, carried = lax.optimization_barrier((*later, carried))
                    received.append([shifted(block, step) for step, block in zip(steps, blocks)])
            if m == 1 and waiting:
                noisy_sum, line_sum = waiting
                line_sum, carried = lax.optimization_barrier((line_sum, carried))
                waiting = (noisy_sum, *along_line(line_sum))
            carried = attention(
                history_list,
                place,
                queries,
                output_gradient,
                received[piece],
                near,
                far,
                carried,
                shape,
                m,
                c,
                0 if c else m,
            )
        *outputs, near_grad, far_grad = carried
        sends, outputs = outputs[2:], outputs[:2]
        if c + 1 < chunks and members > 1:
            ahead = received[2 + c * members]
            far_grad, ahead = lax.optimization_barrier((far_grad, ahead))
            received[2 + c * members] = ahead
        sent.append([shifted(block, -step) for step, block in zip(steps, sends)])
        if waiting:
            noisy_sum, store_sum, others = waiting
            far_grad, others = lax.optimization_barrier((far_grad, others))
            for other in others:
                store_sum = store_sum + other.astype(jnp.float32)
            grads.append(swap_heads(noisy_sum, store_sum))
        noisy_sum, keep, give = summed(near_grad, flipped(far_grad, 1))
        waiting = (noisy_sum, keep + flipped(give, 2).astype(jnp.float32))
    noisy_sum, line_sum = waiting
    store_sum, others = along_line(line_sum)
    for other in others:
        store_sum = store_sum + other.astype(jnp.float32)
    grads.append(swap_heads(noisy_sum, store_sum))
    attended, query_grad = outputs
    for c in range(chunks):
        for step, block in zip(steps, sent[c]):
            source = lax.rem(head + step, head_count)
            start = (source * per_device + c * members) * GROUP_WIDTH
            attended = lax.dynamic_update_slice_in_dim(attended, block[:rows], start, 1)
            query_grad = lax.dynamic_update_slice_in_dim(query_grad, block[rows:], start, 1)
    return (attended, query_grad, *unpacked(place, head_count, grads, rows, clean_rows))


def solution(mesh):
    split = P(("ctx", "head"), None)
    return jax.shard_map(
        shards,
        mesh=mesh,
        in_specs=(split, split, split, split, split, split, P()),
        out_specs=(split,) * 6,
        check_vma=False,
    )
```

```python
import functools

import jax
import jax.numpy as jnp
from jax import lax
from jax.experimental import pallas as pl
from jax.experimental.pallas import tpu as pltpu
from jax.sharding import PartitionSpec as P

QUERY_HEADS = 48
KEY_VALUE_HEADS = 8
HEAD_SIZE = 128
BLK = 32
HEADS_PER_GROUP = QUERY_HEADS // KEY_VALUE_HEADS
GROUP_WIDTH = HEADS_PER_GROUP * HEAD_SIZE
SCALE = HEAD_SIZE**-0.5
LOG2E = 1.4426950408889634
CHUNKS = 2

NEG_FILL = -1e30


def flipped(block, bits):
    count = lax.axis_size("ctx")
    return lax.ppermute(block, "ctx", [(i, i ^ bits) for i in range(count)])


def shifted(block, step):
    count = lax.axis_size("head")
    return lax.ppermute(block, "head", [(i, (i + step) % count) for i in range(count)])


def dot(a, b, contract):
    return lax.dot_general(
        a, b, ((contract[:1], contract[1:]), ((), ())), preferred_element_type=jnp.float32
    )


def lanes(start, size):
    return pl.ds(pl.multiple_of(start, HEAD_SIZE), size)


def pack_kernel(head_count, place, k_noisy, v_noisy, k_clean, v_clean, *outs):
    rows = k_noisy.shape[0]
    half = k_noisy.shape[1] // head_count
    width = HEAD_SIZE
    for step, out in enumerate(outs):
        target = lax.rem(place[1] + step, head_count)
        for member in range(half // width):
            source = lanes(target * half + member * width, width)
            for index, (noisy, clean) in enumerate(((k_noisy, k_clean), (v_noisy, v_clean))):
                to = slice((2 * member + index) * width, (2 * member + index + 1) * width)
                out[:rows, to] = noisy[:, source]
                out[rows:, to] = clean[:, source]


def packed(place, head_count, k_noisy, v_noisy, k_clean, v_clean):
    vmem = pl.BlockSpec(memory_space=pltpu.VMEM)
    block = (k_noisy.shape[0] + k_clean.shape[0], 2 * k_noisy.shape[1] // head_count)
    return pl.pallas_call(
        functools.partial(pack_kernel, head_count),
        in_specs=[pl.BlockSpec(memory_space=pltpu.SMEM)] + [vmem] * 4,
        out_specs=[vmem] * head_count,
        out_shape=[jax.ShapeDtypeStruct(block, jnp.bfloat16)] * head_count,
        name="pack_keys_values",
    )(place, k_noisy, v_noisy, k_clean, v_clean)


def stack_kernel(place, q, g, out):
    rows = q.shape[0]
    out[:rows] = q[...]
    out[rows:] = g[...]


def query_blocks(place, head_count, step, first, count, q, g):
    rows, columns = q.shape
    per_device = columns // head_count // GROUP_WIDTH

    def source(i, place):
        return 0, lax.rem(place[1] + step, head_count) * per_device + first + i

    return pl.pallas_call(
        stack_kernel,
        grid_spec=pltpu.PrefetchScalarGridSpec(
            num_scalar_prefetch=1,
            grid=(count,),
            in_specs=[pl.BlockSpec((rows, GROUP_WIDTH), source)] * 2,
            out_specs=pl.BlockSpec((2 * rows, GROUP_WIDTH), lambda i, place: (0, i)),
        ),
        out_shape=jax.ShapeDtypeStruct((2 * rows, count * GROUP_WIDTH), jnp.bfloat16),
        name="stack_queries",
    )(place, q, g)


def attention_kernel(shape, listed, place, *refs):
    head_count, group_rows, store_rows, clean_rows, slots, aliased = shape
    rows = refs[0].shape[0]
    received = refs[2 : head_count + 1]
    q_parts = [refs[0]] + [pair.at[:rows] for pair in received]
    g_parts = [refs[1]] + [pair.at[rows:] for pair in received]
    near, far = refs[head_count + 1 : head_count + 3]
    o_own, gq_own, *sends = refs[head_count + 3 + aliased : -4]
    near_grad, far_grad, k_all, v_all = refs[-4:]
    width = HEAD_SIZE
    position, head = place[0], place[1]
    k_cols = slice(0, width)
    v_cols = slice(width, 2 * width)
    depth = lax.div(near.shape[0] - group_rows, 2 * store_rows)

    def placed(slot):
        apart = lax.bitwise_xor(position, slot)
        store = lax.bitwise_and(lax.shift_right_logical(apart, 1), 1) * depth
        store = store + lax.shift_right_logical(apart, 2)
        block = jnp.maximum(listed[position, slot], 0)
        if clean_rows >= BLK:
            owner = lax.div(block * BLK, clean_rows)
            step = lax.rem(head - owner + head_count, head_count)
            inside = step * clean_rows + block * BLK - owner * clean_rows
        else:
            inside = block * BLK
        start = pl.multiple_of(group_rows + store * store_rows + inside, BLK)
        return lax.bitwise_and(apart, 1), pl.ds(start, BLK)

    k_all[:group_rows, :] = near[:group_rows, k_cols]
    v_all[:group_rows, :] = near[:group_rows, v_cols]
    k_all[group_rows : 2 * group_rows, :] = far[:group_rows, k_cols]
    v_all[group_rows : 2 * group_rows, :] = far[:group_rows, v_cols]
    span = 2 * group_rows
    for slot in range(slots):
        other, source = placed(slot)
        to = slice(span + slot * BLK, span + (slot + 1) * BLK)
        k_all[to, :] = jnp.where(other == 1, far[source, k_cols], near[source, k_cols])
        v_all[to, :] = jnp.where(other == 1, far[source, v_cols], near[source, v_cols])

    keys = k_all[...]
    values = v_all[...]

    def stacked(parts):
        return jnp.concatenate(
            [
                part[:, r * width : (r + 1) * width]
                for r in range(HEADS_PER_GROUP)
                for part in parts
            ],
            0,
        )

    query = stacked(q_parts)
    upstream = stacked(g_parts)
    keys_t = keys.T
    values_t = values.T
    upstream_t = upstream.T

    scores = dot(keys, query, (1, 1)) * (SCALE * LOG2E)
    pieces = [scores[:span]]
    for slot in range(slots):
        low = span + slot * BLK
        bias = jnp.where(listed[position, slot] >= 0, 0.0, NEG_FILL).astype(jnp.float32)
        pieces.append(scores[low : low + BLK] + bias)
    scores = jnp.concatenate(pieces, 0)
    top = jnp.max(scores, 0, keepdims=True)
    unscaled = jnp.exp2(scores - top)
    prob = unscaled * (1.0 / jnp.sum(unscaled, 0, keepdims=True))
    weights = prob.astype(jnp.bfloat16)
    attended_t = dot(values_t, weights, (1, 0)).astype(jnp.bfloat16)
    row_dot = jnp.sum(
        attended_t.astype(jnp.float32) * upstream_t.astype(jnp.float32), 0, keepdims=True
    )
    dprob = dot(values, upstream, (1, 1))
    dscore = (prob * (dprob - row_dot)).astype(jnp.bfloat16)
    gq_t = (dot(keys_t, dscore, (1, 0)) * SCALE).astype(jnp.bfloat16)
    attended = attended_t.T
    gq = gq_t.T
    at = 0
    for r in range(HEADS_PER_GROUP):
        to = slice(r * width, (r + 1) * width)
        for part in range(head_count):
            if part:
                sends[part - 1][:rows, to] = attended[at : at + rows]
                sends[part - 1][rows:, to] = gq[at : at + rows]
            else:
                o_own[:, to] = attended[at : at + rows]
                gq_own[:, to] = gq[at : at + rows]
            at += rows
    gk = (dot(dscore, query, (1, 0)) * SCALE).astype(jnp.bfloat16)
    gv = dot(weights, upstream, (1, 0)).astype(jnp.bfloat16)
    for index, grad in enumerate((near_grad, far_grad)):
        here = slice(index * group_rows, (index + 1) * group_rows)
        grad[:group_rows, k_cols] = gk[here]
        grad[:group_rows, v_cols] = gv[here]
        rest = grad.shape[0] - group_rows
        grad[group_rows:, k_cols] = jnp.zeros((rest, width), jnp.bfloat16)
        grad[group_rows:, v_cols] = jnp.zeros((rest, width), jnp.bfloat16)
    for slot in range(slots):
        other, target = placed(slot)
        low = span + slot * BLK
        for index, grad in enumerate((near_grad, far_grad)):

            @pl.when(jnp.logical_and(listed[position, slot] >= 0, other == index))
            def _():
                grad[target, k_cols] = gk[low : low + BLK]
                grad[target, v_cols] = gv[low : low + BLK]


def attention(listed, place, q, g, received, near, far, carried, shape, head_of_chunk, chunk, within):
    head_count, group_rows, store_rows, clean_rows, slots = shape
    rows, full_width = q.shape
    per_device = KEY_VALUE_HEADS // head_count
    members = near.shape[1] // (2 * HEAD_SIZE)
    total = 2 * group_rows + slots * BLK
    column = chunk * members + head_of_chunk

    own = pl.BlockSpec((rows, GROUP_WIDTH), lambda i, l, place: (0, place[1] * per_device + column))
    arrived = pl.BlockSpec((2 * rows, GROUP_WIDTH), lambda i, l, place: (0, within))
    pair = pl.BlockSpec((2 * rows, GROUP_WIDTH), lambda i, l, place: (0, head_of_chunk))
    keys = pl.BlockSpec((near.shape[0], 2 * HEAD_SIZE), lambda i, l, place: (0, head_of_chunk))
    others = head_count - 1
    first_carried = 2 + head_count + 3
    out_shape = [
        jax.ShapeDtypeStruct((rows, full_width), jnp.bfloat16),
        jax.ShapeDtypeStruct((rows, full_width), jnp.bfloat16),
        *[jax.ShapeDtypeStruct((2 * rows, members * GROUP_WIDTH), jnp.bfloat16)] * others,
        jax.ShapeDtypeStruct(near.shape, jnp.bfloat16),
        jax.ShapeDtypeStruct(near.shape, jnp.bfloat16),
    ]
    return pl.pallas_call(
        functools.partial(attention_kernel, (*shape, len(carried))),
        grid_spec=pltpu.PrefetchScalarGridSpec(
            num_scalar_prefetch=2,
            grid=(1,),
            in_specs=[own, own, *[arrived] * others, keys, keys]
            + [pl.BlockSpec(memory_space=pl.ANY)] * len(carried),
            out_specs=[own, own, *[pair] * others, keys, keys],
            scratch_shapes=[
                pltpu.VMEM((total, HEAD_SIZE), jnp.bfloat16),
                pltpu.VMEM((total, HEAD_SIZE), jnp.bfloat16),
            ],
        ),
        out_shape=out_shape,
        input_output_aliases={first_carried + i: i for i in range(len(carried))},
        compiler_params=pltpu.CompilerParams(vmem_limit_bytes=56 * 2**20),
        cost_estimate=pl.CostEstimate(
            flops=24 * group_rows * HEADS_PER_GROUP * HEAD_SIZE * total,
            bytes_accessed=16 * group_rows * GROUP_WIDTH,
            transcendentals=group_rows * HEADS_PER_GROUP * total,
        ),
        name="span_attention",
    )(listed, place, q, g, *received, near, far, *carried)


def unpack_kernel(head_count, chunks, place, *refs):
    parts, outs = refs[:-4], refs[-4:]
    rows = outs[0].shape[0]
    half = outs[0].shape[1] // head_count
    width = HEAD_SIZE
    members = half // chunks // width
    for step in range(head_count):
        source = lax.rem(place[1] + step, head_count)
        for chunk in range(chunks):
            part = parts[chunk * head_count + step]
            for member in range(members):
                to = lanes(source * half + (chunk * members + member) * width, width)
                for index in range(2):
                    at = (2 * member + index) * width
                    outs[index][:, to] = part[:rows, at : at + width]
                    outs[2 + index][:, to] = part[rows:, at : at + width]


def unpacked(place, head_count, grads, rows, clean_rows):
    vmem = pl.BlockSpec(memory_space=pltpu.VMEM)
    parts = [part for chunk in grads for part in chunk]
    width = KEY_VALUE_HEADS * HEAD_SIZE
    return pl.pallas_call(
        functools.partial(unpack_kernel, head_count, len(grads)),
        in_specs=[pl.BlockSpec(memory_space=pltpu.SMEM)] + [vmem] * len(parts),
        out_specs=[vmem] * 4,
        out_shape=[jax.ShapeDtypeStruct((rows, width), jnp.bfloat16)] * 2
        + [jax.ShapeDtypeStruct((clean_rows, width), jnp.bfloat16)] * 2,
        name="unpack_gradients",
    )(place, *parts)


def shards(
    queries,
    noisy_token_keys,
    noisy_token_values,
    clean_token_keys,
    clean_token_values,
    output_gradient,
    history_list,
):
    ctx_count = lax.axis_size("ctx")
    head_count = lax.axis_size("head")
    head = lax.axis_index("head")
    place = jnp.stack([lax.axis_index("ctx"), head]).astype(jnp.int32)
    rows = queries.shape[0]
    clean_rows = clean_token_keys.shape[0]
    store_rows = clean_rows * head_count
    group_rows = rows * head_count
    slots = ctx_count - 2
    per_device = KEY_VALUE_HEADS // head_count
    chunks = CHUNKS if per_device % CHUNKS == 0 else 1
    members = per_device // chunks
    depth = ctx_count // 4
    steps = range(1, head_count)
    row_order = lax.rem(head - jnp.arange(head_count, dtype=jnp.int32) + head_count, head_count)

    def by_block(store):
        if clean_rows >= BLK:
            return store
        return store.reshape(head_count, clean_rows, -1)[row_order].reshape(store.shape)

    pairs = packed(
        place,
        head_count,
        noisy_token_keys,
        noisy_token_values,
        clean_token_keys,
        clean_token_values,
    )
    pieces = [(0, members)] + [(m, 1) for m in range(members, per_device)]
    wide = [
        [query_blocks(place, head_count, k, *piece, queries, output_gradient) for k in steps]
        for piece in pieces
    ]
    arrived = [pairs[0]] + [shifted(pairs[step], step) for step in steps]
    store = by_block(jnp.concatenate([part[rows:] for part in arrived], 0))
    line = [store] + [flipped(store, z << 2) for z in range(1, depth)]
    part_width = 2 * members * HEAD_SIZE

    def cut(array, chunk):
        return array[:, chunk * part_width : (chunk + 1) * part_width]

    noisy = [part[:rows] for part in arrived]
    lines = [jnp.concatenate([cut(part, c) for part in line], 0) for c in range(chunks)]
    before = arrived[-1]
    received = []
    for block_set in wide[:2]:
        *blocks, before = lax.optimization_barrier((*block_set, before))
        received.append([shifted(block, step) for step, block in zip(steps, blocks)])
        before = received[-1][-1] if head_count > 1 else before

    def met(chunk):
        return flipped(lines[chunk], 2)

    def joined(chunk, crossed):
        return jnp.concatenate([cut(part, chunk) for part in noisy] + [lines[chunk], crossed], 0)

    def summed(near_grad, from_core):
        total = near_grad.astype(jnp.float32) + from_core.astype(jnp.float32)
        middle = group_rows + depth * store_rows
        return total[:group_rows], total[group_rows:middle], total[middle:].astype(jnp.bfloat16)

    def along_line(line_sum):
        gives = [
            line_sum[z * store_rows : (z + 1) * store_rows].astype(jnp.bfloat16)
            for z in range(1, depth)
        ]
        return line_sum[:store_rows], [flipped(g, z << 2) for z, g in enumerate(gives, 1)]

    def swap_heads(noisy_sum, store_sum):
        if clean_rows < BLK:
            store_sum = store_sum.reshape(head_count, clean_rows, -1)[row_order].reshape(
                store_sum.shape
            )
        store_sum = store_sum.astype(jnp.bfloat16)
        noisy_sum = noisy_sum.astype(jnp.bfloat16)
        mixed = [
            jnp.concatenate(
                [
                    noisy_sum[step * rows : (step + 1) * rows],
                    store_sum[step * clean_rows : (step + 1) * clean_rows],
                ],
                0,
            )
            for step in range(head_count)
        ]
        return [mixed[0]] + [shifted(mixed[step], -step) for step in steps]

    shape = (head_count, group_rows, store_rows, clean_rows, slots)
    outputs = ()
    sent = []
    grads = []
    crossing = met(0)
    waiting = None
    for c in range(chunks):
        near = joined(c, crossing)
        if c == 0:
            near, *received[0] = lax.optimization_barrier((near, *received[0]))
        far = flipped(near, 1)
        if c + 1 < chunks:
            crossing = met(c + 1)
        carried = outputs
        for m in range(members):
            piece = 0 if c == 0 else 1 + (c - 1) * members + m
            if m == 1 and c + 1 < chunks:
                ahead = received[1 + c * members]
                crossing, carried, ahead = lax.optimization_barrier((crossing, carried, ahead))
                received[1 + c * members] = ahead
                for later in wide[2 + c * members : 1 + (c + 1) * members]:
                    *blocks, carried = lax.optimization_barrier((*later, carried))
                    received.append([shifted(block, step) for step, block in zip(steps, blocks)])
            if m == 1 and waiting:
                noisy_sum, line_sum = waiting
                line_sum, carried = lax.optimization_barrier((line_sum, carried))
                waiting = (noisy_sum, *along_line(line_sum))
            carried = attention(
                history_list,
                place,
                queries,
                output_gradient,
                received[piece],
                near,
                far,
                carried,
                shape,
                m,
                c,
                0 if c else m,
            )
        *outputs, near_grad, far_grad = carried
        sends, outputs = outputs[2:], outputs[:2]
        if c + 1 < chunks and members > 1:
            ahead = received[2 + c * members]
            far_grad, ahead = lax.optimization_barrier((far_grad, ahead))
            received[2 + c * members] = ahead
        sent.append([shifted(block, -step) for step, block in zip(steps, sends)])
        if waiting:
            noisy_sum, store_sum, others = waiting
            far_grad, others = lax.optimization_barrier((far_grad, others))
            for other in others:
                store_sum = store_sum + other.astype(jnp.float32)
            grads.append(swap_heads(noisy_sum, store_sum))
        noisy_sum, keep, give = summed(near_grad, flipped(far_grad, 1))
        waiting = (noisy_sum, keep + flipped(give, 2).astype(jnp.float32))
    noisy_sum, line_sum = waiting
    store_sum, others = along_line(line_sum)
    for other in others:
        store_sum = store_sum + other.astype(jnp.float32)
    grads.append(swap_heads(noisy_sum, store_sum))
    attended, query_grad = outputs
    for c in range(chunks):
        for step, block in zip(steps, sent[c]):
            source = lax.rem(head + step, head_count)
            start = (source * per_device + c * members) * GROUP_WIDTH
            attended = lax.dynamic_update_slice_in_dim(attended, block[:rows], start, 1)
            query_grad = lax.dynamic_update_slice_in_dim(query_grad, block[rows:], start, 1)
    return (attended, query_grad, *unpacked(place, head_count, grads, rows, clean_rows))


def solution(mesh):
    split = P(("ctx", "head"), None)
    return jax.shard_map(
        shards,
        mesh=mesh,
        in_specs=(split, split, split, split, split, split, P()),
        out_specs=(split,) * 6,
        check_vma=False,
    )
```

```python
import functools

import jax
import jax.numpy as jnp
from jax import lax
from jax.experimental import pallas as pl
from jax.experimental.pallas import tpu as pltpu
from jax.sharding import PartitionSpec as P

QUERY_HEADS = 48
KEY_VALUE_HEADS = 8
HEAD_SIZE = 128
BLK = 32
HEADS_PER_GROUP = QUERY_HEADS // KEY_VALUE_HEADS
GROUP_WIDTH = HEADS_PER_GROUP * HEAD_SIZE
SCALE = HEAD_SIZE**-0.5
LOG2E = 1.4426950408889634

NEG_FILL = -1e30


def flipped(block, bits):
    count = lax.axis_size("ctx")
    return lax.ppermute(block, "ctx", [(i, i ^ bits) for i in range(count)])


def shifted(block, step):
    count = lax.axis_size("head")
    return lax.ppermute(block, "head", [(i, (i + step) % count) for i in range(count)])


def dot(a, b, contract):
    return lax.dot_general(
        a, b, ((contract[:1], contract[1:]), ((), ())), preferred_element_type=jnp.float32
    )


def lanes(start, size):
    return pl.ds(pl.multiple_of(start, HEAD_SIZE), size)


def pack_kernel(head_count, k_noisy, v_noisy, k_clean, v_clean, *outs):
    rows = k_noisy.shape[0]
    half = k_noisy.shape[1] // head_count
    width = HEAD_SIZE
    for step, out in enumerate(outs):
        target = lax.rem(lax.axis_index("head") + step, head_count)
        for member in range(half // width):
            source = lanes(target * half + member * width, width)
            for index, (noisy, clean) in enumerate(((k_noisy, k_clean), (v_noisy, v_clean))):
                to = slice((2 * member + index) * width, (2 * member + index + 1) * width)
                out[:rows, to] = noisy[:, source]
                out[rows:, to] = clean[:, source]


def packed(head_count, k_noisy, v_noisy, k_clean, v_clean):
    vmem = pl.BlockSpec(memory_space=pltpu.VMEM)
    block = (k_noisy.shape[0] + k_clean.shape[0], 2 * k_noisy.shape[1] // head_count)
    return pl.pallas_call(
        functools.partial(pack_kernel, head_count),
        in_specs=[vmem] * 4,
        out_specs=[vmem] * head_count,
        out_shape=[jax.ShapeDtypeStruct(block, jnp.bfloat16)] * head_count,
        name="pack_keys_values",
    )(k_noisy, v_noisy, k_clean, v_clean)


def stack_kernel(place, q, g, out):
    rows = q.shape[0]
    out[:rows] = q[...]
    out[rows:] = g[...]


def query_blocks(place, head_count, step, first, count, q, g):
    rows, columns = q.shape
    per_device = columns // head_count // GROUP_WIDTH

    def source(i, place):
        return 0, lax.rem(place[1] + step, head_count) * per_device + first + i

    return pl.pallas_call(
        stack_kernel,
        grid_spec=pltpu.PrefetchScalarGridSpec(
            num_scalar_prefetch=1,
            grid=(count,),
            in_specs=[pl.BlockSpec((rows, GROUP_WIDTH), source)] * 2,
            out_specs=pl.BlockSpec((2 * rows, GROUP_WIDTH), lambda i, place: (0, i)),
        ),
        out_shape=jax.ShapeDtypeStruct((2 * rows, count * GROUP_WIDTH), jnp.bfloat16),
        name="stack_queries",
    )(place, q, g)


def attention_kernel(shape, listed, place, *refs):
    head_count, group_rows, store_rows, clean_rows, slots, aliased = shape
    rows = refs[0].shape[0]
    received = refs[2 : head_count + 1]
    q_parts = [refs[0]] + [pair.at[:rows] for pair in received]
    g_parts = [refs[1]] + [pair.at[rows:] for pair in received]
    near, far = refs[head_count + 1 : head_count + 3]
    o_own, gq_own, *sends = refs[head_count + 3 + aliased : -4]
    near_grad, far_grad, k_all, v_all = refs[-4:]
    width = HEAD_SIZE
    position, head = place[0], place[1]
    k_cols = slice(0, width)
    v_cols = slice(width, 2 * width)
    depth = lax.div(near.shape[0] - group_rows, 2 * store_rows)

    def placed(slot):
        apart = lax.bitwise_xor(position, slot)
        store = lax.bitwise_and(lax.shift_right_logical(apart, 1), 1) * depth
        store = store + lax.shift_right_logical(apart, 2)
        block = jnp.maximum(listed[position, slot], 0)
        if clean_rows >= BLK:
            owner = lax.div(block * BLK, clean_rows)
            step = lax.rem(head - owner + head_count, head_count)
            inside = step * clean_rows + block * BLK - owner * clean_rows
        else:
            inside = block * BLK
        start = pl.multiple_of(group_rows + store * store_rows + inside, BLK)
        return lax.bitwise_and(apart, 1), pl.ds(start, BLK)

    k_all[:group_rows, :] = near[:group_rows, k_cols]
    v_all[:group_rows, :] = near[:group_rows, v_cols]
    k_all[group_rows : 2 * group_rows, :] = far[:group_rows, k_cols]
    v_all[group_rows : 2 * group_rows, :] = far[:group_rows, v_cols]
    span = 2 * group_rows
    for slot in range(slots):
        other, source = placed(slot)
        to = slice(span + slot * BLK, span + (slot + 1) * BLK)
        k_all[to, :] = jnp.where(other == 1, far[source, k_cols], near[source, k_cols])
        v_all[to, :] = jnp.where(other == 1, far[source, v_cols], near[source, v_cols])

    keys = k_all[...]
    values = v_all[...]

    def stacked(parts):
        return jnp.concatenate(
            [
                part[:, r * width : (r + 1) * width]
                for r in range(HEADS_PER_GROUP)
                for part in parts
            ],
            0,
        )

    query = stacked(q_parts)
    upstream = stacked(g_parts)
    keys_t = keys.T
    values_t = values.T
    upstream_t = upstream.T

    scores = dot(keys, query, (1, 1)) * (SCALE * LOG2E)
    pieces = [scores[:span]]
    for slot in range(slots):
        low = span + slot * BLK
        bias = jnp.where(listed[position, slot] >= 0, 0.0, NEG_FILL).astype(jnp.float32)
        pieces.append(scores[low : low + BLK] + bias)
    scores = jnp.concatenate(pieces, 0)
    top = jnp.max(scores, 0, keepdims=True)
    unscaled = jnp.exp2(scores - top)
    prob = unscaled * (1.0 / jnp.sum(unscaled, 0, keepdims=True))
    weights = prob.astype(jnp.bfloat16)
    attended_t = dot(values_t, weights, (1, 0)).astype(jnp.bfloat16)
    row_dot = jnp.sum(
        attended_t.astype(jnp.float32) * upstream_t.astype(jnp.float32), 0, keepdims=True
    )
    dprob = dot(values, upstream, (1, 1))
    dscore = (prob * (dprob - row_dot)).astype(jnp.bfloat16)
    gq_t = (dot(keys_t, dscore, (1, 0)) * SCALE).astype(jnp.bfloat16)
    attended = attended_t.T
    gq = gq_t.T
    at = 0
    for r in range(HEADS_PER_GROUP):
        to = slice(r * width, (r + 1) * width)
        for part in range(head_count):
            if part:
                sends[part - 1][:rows, to] = attended[at : at + rows]
                sends[part - 1][rows:, to] = gq[at : at + rows]
            else:
                o_own[:, to] = attended[at : at + rows]
                gq_own[:, to] = gq[at : at + rows]
            at += rows
    gk = (dot(dscore, query, (1, 0)) * SCALE).astype(jnp.bfloat16)
    gv = dot(weights, upstream, (1, 0)).astype(jnp.bfloat16)
    for index, grad in enumerate((near_grad, far_grad)):
        here = slice(index * group_rows, (index + 1) * group_rows)
        grad[:group_rows, k_cols] = gk[here]
        grad[:group_rows, v_cols] = gv[here]
        rest = grad.shape[0] - group_rows
        grad[group_rows:, k_cols] = jnp.zeros((rest, width), jnp.bfloat16)
        grad[group_rows:, v_cols] = jnp.zeros((rest, width), jnp.bfloat16)
    for slot in range(slots):
        other, target = placed(slot)
        low = span + slot * BLK
        for index, grad in enumerate((near_grad, far_grad)):

            @pl.when(jnp.logical_and(listed[position, slot] >= 0, other == index))
            def _():
                grad[target, k_cols] = gk[low : low + BLK]
                grad[target, v_cols] = gv[low : low + BLK]


def attention(listed, place, q, g, received, near, far, carried, shape, member, columns):
    head_count, group_rows, store_rows, clean_rows, slots = shape
    rows = q.shape[0]
    per_device = KEY_VALUE_HEADS // head_count
    total = 2 * group_rows + slots * BLK
    from_queries, from_keys, to_sends, to_grads = columns

    own = pl.BlockSpec((rows, GROUP_WIDTH), lambda i, l, place: (0, place[1] * per_device + member))

    def block(height, width, column):
        return pl.BlockSpec((height, width), lambda i, l, place: (0, column))

    others = head_count - 1
    keys = 2 * HEAD_SIZE
    kept = [i for i, array in enumerate(carried) if not isinstance(array, jax.ShapeDtypeStruct)]
    first_carried = 2 + head_count + 3
    return pl.pallas_call(
        functools.partial(attention_kernel, (*shape, len(kept))),
        grid_spec=pltpu.PrefetchScalarGridSpec(
            num_scalar_prefetch=2,
            grid=(1,),
            in_specs=[own, own]
            + [block(2 * rows, GROUP_WIDTH, from_queries)] * others
            + [block(near.shape[0], keys, from_keys)] * 2
            + [pl.BlockSpec(memory_space=pl.ANY)] * len(kept),
            out_specs=[own, own]
            + [block(2 * rows, GROUP_WIDTH, to_sends)] * others
            + [block(near.shape[0], keys, to_grads)] * 2,
            scratch_shapes=[
                pltpu.VMEM((total, HEAD_SIZE), jnp.bfloat16),
                pltpu.VMEM((total, HEAD_SIZE), jnp.bfloat16),
            ],
        ),
        out_shape=[jax.ShapeDtypeStruct(array.shape, jnp.bfloat16) for array in carried],
        input_output_aliases={first_carried + n: i for n, i in enumerate(kept)},
        compiler_params=pltpu.CompilerParams(vmem_limit_bytes=56 * 2**20),
        cost_estimate=pl.CostEstimate(
            flops=24 * group_rows * HEADS_PER_GROUP * HEAD_SIZE * total,
            bytes_accessed=16 * group_rows * GROUP_WIDTH,
            transcendentals=group_rows * HEADS_PER_GROUP * total,
        ),
        name="span_attention",
    )(listed, place, q, g, *received, near, far, *[carried[i] for i in kept])


def unpack_kernel(head_count, groups, *refs):
    parts, outs = refs[:-4], refs[-4:]
    rows = outs[0].shape[0]
    half = outs[0].shape[1] // head_count
    width = HEAD_SIZE
    for step in range(head_count):
        source = lax.rem(lax.axis_index("head") + step, head_count)
        for group, members in enumerate(groups):
            part = parts[group * head_count + step]
            for at, member in enumerate(members):
                to = lanes(source * half + member * width, width)
                for index in range(2):
                    here = slice((2 * at + index) * width, (2 * at + index + 1) * width)
                    outs[index][:, to] = part[:rows, here]
                    outs[2 + index][:, to] = part[rows:, here]


def unpacked(head_count, groups, grads, rows, clean_rows):
    vmem = pl.BlockSpec(memory_space=pltpu.VMEM)
    parts = [part for chunk in grads for part in chunk]
    width = KEY_VALUE_HEADS * HEAD_SIZE
    return pl.pallas_call(
        functools.partial(unpack_kernel, head_count, groups),
        in_specs=[vmem] * len(parts),
        out_specs=[vmem] * 4,
        out_shape=[jax.ShapeDtypeStruct((rows, width), jnp.bfloat16)] * 2
        + [jax.ShapeDtypeStruct((clean_rows, width), jnp.bfloat16)] * 2,
        name="unpack_gradients",
    )(*parts)


def shards(
    queries,
    noisy_token_keys,
    noisy_token_values,
    clean_token_keys,
    clean_token_values,
    output_gradient,
    history_list,
):
    ctx_count = lax.axis_size("ctx")
    head_count = lax.axis_size("head")
    head = lax.axis_index("head")
    place = jnp.stack([lax.axis_index("ctx"), head]).astype(jnp.int32)
    rows = queries.shape[0]
    clean_rows = clean_token_keys.shape[0]
    store_rows = clean_rows * head_count
    group_rows = rows * head_count
    slots = ctx_count - 2
    per_device = KEY_VALUE_HEADS // head_count
    everything = list(range(per_device))
    half = max(1, per_device // 2)
    key_groups = [g for g in (everything[:half], everything[half:]) if g]
    ask_groups = [[m] for m in everything]
    send_groups = ask_groups
    grad_groups = [g for g in (everything[:-1], everything[-1:]) if g]
    depth = ctx_count // 4
    steps = range(1, head_count)
    row_order = lax.rem(head - jnp.arange(head_count, dtype=jnp.int32) + head_count, head_count)

    def by_block(store):
        if clean_rows >= BLK:
            return store
        return store.reshape(head_count, clean_rows, -1)[row_order].reshape(store.shape)

    pairs = packed(
        head_count,
        noisy_token_keys,
        noisy_token_values,
        clean_token_keys,
        clean_token_values,
    )
    wide = [
        [
            query_blocks(place, head_count, k, group[0], len(group), queries, output_gradient)
            for k in steps
        ]
        for group in ask_groups
    ]
    arrived = [pairs[0]] + [shifted(pairs[step], step) for step in steps]
    store = by_block(jnp.concatenate([part[rows:] for part in arrived], 0))
    line = [store] + [flipped(store, z << 2) for z in range(1, depth)]
    key_width = 2 * HEAD_SIZE

    def cut(array, group):
        return array[:, group[0] * key_width : (group[-1] + 1) * key_width]

    noisy = [part[:rows] for part in arrived]
    lines = [jnp.concatenate([cut(part, group) for part in line], 0) for group in key_groups]

    def swap_queries(index, *after):
        *blocks, after = lax.optimization_barrier((*wide[index], after))
        return [shifted(block, step) for step, block in zip(steps, blocks)], after

    def joined(index, crossed):
        own = [cut(part, key_groups[index]) for part in noisy]
        return jnp.concatenate(own + [lines[index], crossed], 0)

    def summed(near_grad, from_core):
        total = near_grad.astype(jnp.float32) + from_core.astype(jnp.float32)
        middle = group_rows + depth * store_rows
        return total[:group_rows], total[group_rows:middle], total[middle:].astype(jnp.bfloat16)

    def along_line(line_sum):
        gives = [
            line_sum[z * store_rows : (z + 1) * store_rows].astype(jnp.bfloat16)
            for z in range(1, depth)
        ]
        return line_sum[:store_rows], [flipped(g, z << 2) for z, g in enumerate(gives, 1)]

    def swap_heads(noisy_sum, store_sum):
        if clean_rows < BLK:
            store_sum = store_sum.reshape(head_count, clean_rows, -1)[row_order].reshape(
                store_sum.shape
            )
        store_sum = store_sum.astype(jnp.bfloat16)
        noisy_sum = noisy_sum.astype(jnp.bfloat16)
        mixed = [
            jnp.concatenate(
                [
                    noisy_sum[step * rows : (step + 1) * rows],
                    store_sum[step * clean_rows : (step + 1) * clean_rows],
                ],
                0,
            )
            for step in range(head_count)
        ]
        return [mixed[0]] + [shifted(mixed[step], -step) for step in steps]

    shape = (head_count, group_rows, store_rows, clean_rows, slots)
    received = {}
    received[0], _ = swap_queries(0, arrived[-1])
    lines[0], received[0], wide = lax.optimization_barrier((lines[0], received[0], wide))
    near = joined(0, flipped(lines[0], 2))
    if half > 1:
        received[1], _ = swap_queries(1, received[0])
        near, received[1] = lax.optimization_barrier((near, received[1]))
    keys = {0: (near, flipped(near, 1))}
    if len(key_groups) > 1:
        received[half], _ = swap_queries(half, received[half - 1])
        crossing = flipped(lines[1], 2)

    outputs = [jax.ShapeDtypeStruct(queries.shape, jnp.bfloat16)] * 2
    sent = []
    grads = []
    waiting = []

    def group_of(groups, member):
        return next(i for i, group in enumerate(groups) if member in group)

    for member in everything:
        k, s, r = (group_of(g, member) for g in (key_groups, send_groups, grad_groups))
        if member == send_groups[s][0]:
            width = len(send_groups[s]) * GROUP_WIDTH
            sends = [jax.ShapeDtypeStruct((2 * rows, width), jnp.bfloat16)] * (head_count - 1)
        if member == grad_groups[r][0]:
            width = len(grad_groups[r]) * key_width
            pair = [jax.ShapeDtypeStruct((near.shape[0], width), jnp.bfloat16)] * 2
        columns = [
            groups[i].index(member)
            for groups, i in (
                (ask_groups, member),
                (key_groups, k),
                (send_groups, s),
                (grad_groups, r),
            )
        ]
        outputs[0], outputs[1], *rest = attention(
            history_list,
            place,
            queries,
            output_gradient,
            received[member],
            *keys[k],
            [*outputs, *sends, *pair],
            shape,
            member,
            columns,
        )
        sends, pair = rest[:-2], rest[-2:]
        if member == 0 and len(key_groups) > 1:
            crossing, received[half], outputs = lax.optimization_barrier(
                (crossing, received[half], outputs)
            )
            near = joined(1, crossing)
            keys[1] = (near, flipped(near, 1))
            for later in range(half + 1, per_device):
                received[later], (outputs,) = swap_queries(later, outputs)
        if member == half - 1 and half + 1 in received:
            outputs, received[half + 1] = lax.optimization_barrier((outputs, received[half + 1]))
        if member == send_groups[s][-1]:
            sent.append([shifted(block, -step) for step, block in zip(steps, sends)])
        if member == grad_groups[r][-1]:
            if waiting:
                pair, waiting[-1], sent[:half] = lax.optimization_barrier(
                    (pair, waiting[-1], sent[:half])
                )
            elif half > 1:
                pair, sent[0] = lax.optimization_barrier((pair, sent[0]))
            from_core = flipped(pair[1], 1)
            if waiting:
                from_core, waiting[-1] = lax.optimization_barrier((from_core, waiting[-1]))
            noisy_sum, keep, give = summed(pair[0], from_core)
            if member != everything[-1]:
                noisy_sum, keep, give, outputs = lax.optimization_barrier(
                    (noisy_sum, keep, give, outputs)
                )
            waiting.append((noisy_sum, keep + flipped(give, 2).astype(jnp.float32)))
    for noisy_sum, line_sum in waiting:
        store_sum, others = along_line(line_sum)
        if len(grads) + 1 == len(grad_groups) > 1:
            others, sent[half:] = lax.optimization_barrier((others, sent[half:]))
        for other in others:
            store_sum = store_sum + other.astype(jnp.float32)
        grads.append(swap_heads(noisy_sum, store_sum))
    attended, query_grad = outputs
    for group, blocks in zip(send_groups, sent):
        for step, block in zip(steps, blocks):
            source = lax.rem(head + step, head_count)
            start = (source * per_device + group[0]) * GROUP_WIDTH
            attended = lax.dynamic_update_slice_in_dim(attended, block[:rows], start, 1)
            query_grad = lax.dynamic_update_slice_in_dim(query_grad, block[rows:], start, 1)
    finished = unpacked(head_count, grad_groups, grads, rows, clean_rows)
    return (attended, query_grad, *finished)


def solution(mesh):
    split = P(("ctx", "head"), None)
    return jax.shard_map(
        shards,
        mesh=mesh,
        in_specs=(split, split, split, split, split, split, P()),
        out_specs=(split,) * 6,
        check_vma=False,
    )
```

```python
import functools

import jax
import jax.numpy as jnp
from jax import lax
from jax.experimental import pallas as pl
from jax.experimental.pallas import tpu as pltpu
from jax.sharding import PartitionSpec as P

QUERY_HEADS = 48
KEY_VALUE_HEADS = 8
HEAD_SIZE = 128
BLK = 32
HEADS_PER_GROUP = QUERY_HEADS // KEY_VALUE_HEADS
GROUP_WIDTH = HEADS_PER_GROUP * HEAD_SIZE
SCALE = HEAD_SIZE**-0.5
LOG2E = 1.4426950408889634

NEG_FILL = -1e30


def flipped(block, bits):
    count = lax.axis_size("ctx")
    return lax.ppermute(block, "ctx", [(i, i ^ bits) for i in range(count)])


def shifted(block, step):
    count = lax.axis_size("head")
    return lax.ppermute(block, "head", [(i, (i + step) % count) for i in range(count)])


def dot(a, b, contract):
    return lax.dot_general(
        a, b, ((contract[:1], contract[1:]), ((), ())), preferred_element_type=jnp.float32
    )


def lanes(start, size):
    return pl.ds(pl.multiple_of(start, HEAD_SIZE), size)


def pack_kernel(head_count, groups, k_noisy, v_noisy, k_clean, v_clean, *outs):
    rows = k_noisy.shape[0]
    half = k_noisy.shape[1] // head_count
    width = HEAD_SIZE
    for index, group in enumerate(groups):
        for step in range(head_count):
            out = outs[index * head_count + step]
            target = lax.rem(lax.axis_index("head") + step, head_count)
            for at, member in enumerate(group):
                source = lanes(target * half + member * width, width)
                for n, (noisy, clean) in enumerate(((k_noisy, k_clean), (v_noisy, v_clean))):
                    to = slice((2 * at + n) * width, (2 * at + n + 1) * width)
                    out[:rows, to] = noisy[:, source]
                    out[rows:, to] = clean[:, source]


def packed(head_count, groups, k_noisy, v_noisy, k_clean, v_clean):
    vmem = pl.BlockSpec(memory_space=pltpu.VMEM)
    rows = k_noisy.shape[0] + k_clean.shape[0]
    shapes = [
        jax.ShapeDtypeStruct((rows, 2 * HEAD_SIZE * len(group)), jnp.bfloat16)
        for group in groups
        for _ in range(head_count)
    ]
    outs = pl.pallas_call(
        functools.partial(pack_kernel, head_count, groups),
        in_specs=[vmem] * 4,
        out_specs=[vmem] * len(shapes),
        out_shape=shapes,
        name="pack_keys_values",
    )(k_noisy, v_noisy, k_clean, v_clean)
    return [outs[i * head_count : (i + 1) * head_count] for i in range(len(groups))]


def attention_kernel(shape, listed, place, *refs):
    head_count, group_rows, store_rows, clean_rows, slots, aliased = shape
    rows = refs[0].shape[0]
    received = refs[2 : head_count + 1]
    q_parts = [refs[0]] + [pair.at[:rows] for pair in received]
    g_parts = [refs[1]] + [pair.at[rows:] for pair in received]
    near, far = refs[head_count + 1 : head_count + 3]
    o_own, gq_own, *sends = refs[head_count + 3 + aliased : -4]
    near_grad, far_grad, k_all, v_all = refs[-4:]
    width = HEAD_SIZE
    position, head = place[0], place[1]
    k_cols = slice(0, width)
    v_cols = slice(width, 2 * width)
    levels = ((near.shape[0] - group_rows) // store_rows).bit_length() - 1

    def placed(slot):
        apart = lax.bitwise_xor(position, slot)
        store = jnp.int32(0)
        for bit in range(1, levels + 1):
            store = store + (lax.bitwise_and(lax.shift_right_logical(apart, bit), 1) << (levels - bit))
        block = jnp.maximum(listed[position, slot], 0)
        if clean_rows >= BLK:
            owner = lax.div(block * BLK, clean_rows)
            step = lax.rem(head - owner + head_count, head_count)
            inside = step * clean_rows + block * BLK - owner * clean_rows
        else:
            inside = block * BLK
        start = pl.multiple_of(group_rows + store * store_rows + inside, BLK)
        return lax.bitwise_and(apart, 1), pl.ds(start, BLK)

    k_all[:group_rows, :] = near[:group_rows, k_cols]
    v_all[:group_rows, :] = near[:group_rows, v_cols]
    k_all[group_rows : 2 * group_rows, :] = far[:group_rows, k_cols]
    v_all[group_rows : 2 * group_rows, :] = far[:group_rows, v_cols]
    span = 2 * group_rows
    for slot in range(slots):
        other, source = placed(slot)
        to = slice(span + slot * BLK, span + (slot + 1) * BLK)
        k_all[to, :] = jnp.where(other == 1, far[source, k_cols], near[source, k_cols])
        v_all[to, :] = jnp.where(other == 1, far[source, v_cols], near[source, v_cols])

    keys = k_all[...]
    values = v_all[...]

    def stacked(parts):
        return jnp.concatenate(
            [
                part[:, r * width : (r + 1) * width]
                for r in range(HEADS_PER_GROUP)
                for part in parts
            ],
            0,
        )

    query = stacked(q_parts)
    upstream = stacked(g_parts)
    keys_t = keys.T
    values_t = values.T
    upstream_t = upstream.T

    scores = dot(keys, query, (1, 1)) * (SCALE * LOG2E)
    pieces = [scores[:span]]
    for slot in range(slots):
        low = span + slot * BLK
        bias = jnp.where(listed[position, slot] >= 0, 0.0, NEG_FILL).astype(jnp.float32)
        pieces.append(scores[low : low + BLK] + bias)
    scores = jnp.concatenate(pieces, 0)
    top = jnp.max(scores, 0, keepdims=True)
    unscaled = jnp.exp2(scores - top)
    prob = unscaled * (1.0 / jnp.sum(unscaled, 0, keepdims=True))
    weights = prob.astype(jnp.bfloat16)
    attended_t = dot(values_t, weights, (1, 0)).astype(jnp.bfloat16)
    row_dot = jnp.sum(
        attended_t.astype(jnp.float32) * upstream_t.astype(jnp.float32), 0, keepdims=True
    )
    dprob = dot(values, upstream, (1, 1))
    dscore = (prob * (dprob - row_dot)).astype(jnp.bfloat16)
    gq_t = (dot(keys_t, dscore, (1, 0)) * SCALE).astype(jnp.bfloat16)
    attended = attended_t.T
    gq = gq_t.T
    at = 0
    for r in range(HEADS_PER_GROUP):
        to = slice(r * width, (r + 1) * width)
        for part in range(head_count):
            if part:
                sends[part - 1][:rows, to] = attended[at : at + rows]
                sends[part - 1][rows:, to] = gq[at : at + rows]
            else:
                o_own[:, to] = attended[at : at + rows]
                gq_own[:, to] = gq[at : at + rows]
            at += rows
    gk = (dot(dscore, query, (1, 0)) * SCALE).astype(jnp.bfloat16)
    gv = dot(weights, upstream, (1, 0)).astype(jnp.bfloat16)
    for index, grad in enumerate((near_grad, far_grad)):
        here = slice(index * group_rows, (index + 1) * group_rows)
        grad[:group_rows, k_cols] = gk[here]
        grad[:group_rows, v_cols] = gv[here]
        rest = grad.shape[0] - group_rows
        grad[group_rows:, k_cols] = jnp.zeros((rest, width), jnp.bfloat16)
        grad[group_rows:, v_cols] = jnp.zeros((rest, width), jnp.bfloat16)
    for slot in range(slots):
        other, target = placed(slot)
        low = span + slot * BLK
        for index, grad in enumerate((near_grad, far_grad)):

            @pl.when(jnp.logical_and(listed[position, slot] >= 0, other == index))
            def _():
                grad[target, k_cols] = gk[low : low + BLK]
                grad[target, v_cols] = gv[low : low + BLK]


def attention(listed, place, q, g, received, near, far, carried, shape, member, columns):
    head_count, group_rows, store_rows, clean_rows, slots = shape
    rows = q.shape[0]
    per_device = KEY_VALUE_HEADS // head_count
    total = 2 * group_rows + slots * BLK
    from_queries, from_keys, to_sends, to_grads = columns

    own = pl.BlockSpec((rows, GROUP_WIDTH), lambda i, l, place: (0, place[1] * per_device + member))

    def block(height, width, column):
        return pl.BlockSpec((height, width), lambda i, l, place: (0, column))

    others = head_count - 1
    keys = 2 * HEAD_SIZE
    kept = [i for i, array in enumerate(carried) if not isinstance(array, jax.ShapeDtypeStruct)]
    first_carried = 2 + head_count + 3
    return pl.pallas_call(
        functools.partial(attention_kernel, (*shape, len(kept))),
        grid_spec=pltpu.PrefetchScalarGridSpec(
            num_scalar_prefetch=2,
            grid=(1,),
            in_specs=[own, own]
            + [block(2 * rows, GROUP_WIDTH, from_queries)] * others
            + [block(near.shape[0], keys, from_keys)] * 2
            + [pl.BlockSpec(memory_space=pl.ANY)] * len(kept),
            out_specs=[own, own]
            + [block(2 * rows, GROUP_WIDTH, to_sends)] * others
            + [block(near.shape[0], keys, to_grads)] * 2,
            scratch_shapes=[
                pltpu.VMEM((total, HEAD_SIZE), jnp.bfloat16),
                pltpu.VMEM((total, HEAD_SIZE), jnp.bfloat16),
            ],
        ),
        out_shape=[jax.ShapeDtypeStruct(array.shape, jnp.bfloat16) for array in carried],
        input_output_aliases={first_carried + n: i for n, i in enumerate(kept)},
        compiler_params=pltpu.CompilerParams(vmem_limit_bytes=56 * 2**20),
        cost_estimate=pl.CostEstimate(
            flops=24 * group_rows * HEADS_PER_GROUP * HEAD_SIZE * total,
            bytes_accessed=16 * group_rows * GROUP_WIDTH,
            transcendentals=group_rows * HEADS_PER_GROUP * total,
        ),
        name="span_attention",
    )(listed, place, q, g, *received, near, far, *[carried[i] for i in kept])


def unpack_kernel(head_count, groups, *refs):
    parts, outs = refs[:-4], refs[-4:]
    rows = outs[0].shape[0]
    half = outs[0].shape[1] // head_count
    width = HEAD_SIZE
    for step in range(head_count):
        source = lax.rem(lax.axis_index("head") + step, head_count)
        for group, members in enumerate(groups):
            part = parts[group * head_count + step]
            for at, member in enumerate(members):
                to = lanes(source * half + member * width, width)
                for index in range(2):
                    here = slice((2 * at + index) * width, (2 * at + index + 1) * width)
                    outs[index][:, to] = part[:rows, here]
                    outs[2 + index][:, to] = part[rows:, here]


def unpacked(head_count, groups, grads, rows, clean_rows):
    vmem = pl.BlockSpec(memory_space=pltpu.VMEM)
    parts = [part for chunk in grads for part in chunk]
    width = KEY_VALUE_HEADS * HEAD_SIZE
    return pl.pallas_call(
        functools.partial(unpack_kernel, head_count, groups),
        in_specs=[vmem] * len(parts),
        out_specs=[vmem] * 4,
        out_shape=[jax.ShapeDtypeStruct((rows, width), jnp.bfloat16)] * 2
        + [jax.ShapeDtypeStruct((clean_rows, width), jnp.bfloat16)] * 2,
        name="unpack_gradients",
    )(*parts)


def shards(
    queries,
    noisy_token_keys,
    noisy_token_values,
    clean_token_keys,
    clean_token_values,
    output_gradient,
    history_list,
):
    ctx_count = lax.axis_size("ctx")
    head_count = lax.axis_size("head")
    head = lax.axis_index("head")
    place = jnp.stack([lax.axis_index("ctx"), head]).astype(jnp.int32)
    rows = queries.shape[0]
    clean_rows = clean_token_keys.shape[0]
    store_rows = clean_rows * head_count
    group_rows = rows * head_count
    slots = ctx_count - 2
    per_device = KEY_VALUE_HEADS // head_count
    everything = list(range(per_device))
    half = max(1, per_device // 2)
    key_groups = [g for g in (everything[:half], everything[half:]) if g]
    grad_groups = key_groups
    ask_groups = send_groups = [[m] for m in everything]
    top = ctx_count.bit_length() - 2
    steps = range(1, head_count)
    row_order = lax.rem(head - jnp.arange(head_count, dtype=jnp.int32) + head_count, head_count)

    def by_block(store):
        if clean_rows >= BLK:
            return store
        return store.reshape(head_count, clean_rows, -1)[row_order].reshape(store.shape)

    packs = packed(
        head_count,
        key_groups,
        noisy_token_keys,
        noisy_token_values,
        clean_token_keys,
        clean_token_values,
    )

    def own_columns(array, member, step):
        start = (lax.rem(head + step, head_count) * per_device + member) * GROUP_WIDTH
        return lax.dynamic_slice_in_dim(array, start, GROUP_WIDTH, 1)

    def swap_keys(index):
        return [packs[index][0]] + [shifted(packs[index][step], step) for step in steps]

    def swap_queries(member):
        return [
            shifted(
                jnp.concatenate(
                    [own_columns(array, member, step) for array in (queries, output_gradient)], 0
                ),
                step,
            )
            for step in steps
        ]

    def stored(parts):
        return by_block(jnp.concatenate([part[rows:] for part in parts], 0))

    def doubled(line, bit):
        return jnp.concatenate([line, flipped(line, 1 << bit)], 0)

    def joined(parts, line):
        return jnp.concatenate([part[:rows] for part in parts] + [line], 0)

    def summed(near_grad, from_core):
        total = near_grad.astype(jnp.float32) + from_core.astype(jnp.float32)
        return total[:group_rows], total[group_rows:]

    def halved(line, bit):
        middle = line.shape[0] // 2
        return line[:middle], flipped(line[middle:].astype(jnp.bfloat16), 1 << bit)

    together = lax.optimization_barrier
    def swap_heads(noisy_sum, store_sum):
        if clean_rows < BLK:
            store_sum = store_sum.reshape(head_count, clean_rows, -1)[row_order].reshape(
                store_sum.shape
            )
        store_sum = store_sum.astype(jnp.bfloat16)
        noisy_sum = noisy_sum.astype(jnp.bfloat16)
        mixed = [
            jnp.concatenate(
                [
                    noisy_sum[step * rows : (step + 1) * rows],
                    store_sum[step * clean_rows : (step + 1) * clean_rows],
                ],
                0,
            )
            for step in range(head_count)
        ]
        return [mixed[0]] + [shifted(mixed[step], -step) for step in steps]

    shape = (head_count, group_rows, store_rows, clean_rows, slots)
    received = {}
    two = len(key_groups) > 1
    parts = swap_keys(0)
    line = stored(parts)
    if two:
        packs[1], parts = together((packs[1], parts))
        later_parts = swap_keys(1)
    asked = 0
    for bit in range(top, 0, -1):
        line = doubled(line, bit)
        if two and bit == top:
            line, later_parts = together((line, later_parts))
            later_line = stored(later_parts)
            received[0] = swap_queries(0)
        elif two and bit == 1:
            line, later_line, received[0] = together((line, later_line, received[0]))
        elif two:
            line, later_line = together((line, later_line))
        if two and bit > 1:
            later_line = doubled(later_line, bit)
    if not two:
        received[0] = swap_queries(0)
    near = joined(parts, line)
    near, received[0] = together((near, received[0]))
    keys = {0: (near, flipped(near, 1))}
    if two:
        crossing = flipped(later_line, 2)
    for member in everything[1:]:
        received[member] = swap_queries(member)

    outputs = [jax.ShapeDtypeStruct(queries.shape, jnp.bfloat16)] * 2
    sent = []
    waiting = []

    def group_of(groups, member):
        return next(i for i, group in enumerate(groups) if member in group)

    for member in everything:
        k = group_of(key_groups, member)
        first = member == key_groups[k][0]
        last = member == key_groups[k][-1]
        sends = [jax.ShapeDtypeStruct((2 * rows, GROUP_WIDTH), jnp.bfloat16)] * (head_count - 1)
        if first:
            width = len(key_groups[k]) * 2 * HEAD_SIZE
            pair = [jax.ShapeDtypeStruct((near.shape[0], width), jnp.bfloat16)] * 2
        column = key_groups[k].index(member)
        outputs[0], outputs[1], *rest = attention(
            history_list,
            place,
            queries,
            output_gradient,
            received[member],
            *keys[k],
            [*outputs, *sends, *pair],
            shape,
            member,
            (0, column, 0, column),
        )
        sends, pair = rest[:-2], rest[-2:]
        sent.append([shifted(block, -step) for step, block in zip(steps, sends)])
        if two and member == 0:
            outputs, crossing, received = together((outputs, crossing, received))
            near = joined(later_parts, jnp.concatenate([later_line, crossing], 0))
            keys[1] = (near, flipped(near, 1))
        elif two and member == half - 1:
            pair, sent[: half - 1] = together((pair, sent[: half - 1]))
        if waiting and not last:
            noisy_sum, line = summed(*waiting[0])
            line, outputs, sent[half - 1] = together((line, outputs, sent[half - 1]))
            waiting[0] = (noisy_sum, *halved(line, 1))
        if last:
            if waiting:
                waiting[0], pair, sent[:-1] = together((waiting[0], pair, sent[:-1]))
            from_core = flipped(pair[1], 1)
            if waiting:
                from_core, waiting[0] = together((from_core, waiting[0]))
            waiting.append((pair[0], from_core))
    grads = []
    for index, state in enumerate(waiting):
        if len(state) == 2:
            noisy_sum, line = summed(*state)
            keep, other = halved(line, 1)
        else:
            noisy_sum, keep, other = state
        line = keep + other.astype(jnp.float32)
        for bit in range(2, top + 1):
            keep, other = halved(line, bit)
            line = keep + other.astype(jnp.float32)
        if index:
            line, sent[-1] = together((line, sent[-1]))
        grads.append(swap_heads(noisy_sum, line))
    attended, query_grad = outputs
    for group, blocks in zip(send_groups, sent):
        for step, block in zip(steps, blocks):
            source = lax.rem(head + step, head_count)
            start = (source * per_device + group[0]) * GROUP_WIDTH
            attended = lax.dynamic_update_slice_in_dim(attended, block[:rows], start, 1)
            query_grad = lax.dynamic_update_slice_in_dim(query_grad, block[rows:], start, 1)
    finished = unpacked(head_count, grad_groups, grads, rows, clean_rows)
    return (attended, query_grad, *finished)


def solution(mesh):
    split = P(("ctx", "head"), None)
    return jax.shard_map(
        shards,
        mesh=mesh,
        in_specs=(split, split, split, split, split, split, P()),
        out_specs=(split,) * 6,
        check_vma=False,
    )
```

```python
import functools

import jax
import jax.numpy as jnp
from jax import lax
from jax.experimental import pallas as pl
from jax.experimental.pallas import tpu as pltpu
from jax.sharding import PartitionSpec as P

QUERY_HEADS = 48
KEY_VALUE_HEADS = 8
HEAD_SIZE = 128
BLK = 32
HEADS_PER_GROUP = QUERY_HEADS // KEY_VALUE_HEADS
GROUP_WIDTH = HEADS_PER_GROUP * HEAD_SIZE
SCALE = HEAD_SIZE**-0.5
LOG2E = 1.4426950408889634

NEG_FILL = -1e30
SLICE_ROWS = 256
KERNEL_VMEM = 32 * 2**20


def flipped(block, bits):
    count = lax.axis_size("ctx")
    return lax.ppermute(block, "ctx", [(i, i ^ bits) for i in range(count)])


def shifted(block, step):
    count = lax.axis_size("head")
    return lax.ppermute(block, "head", [(i, (i + step) % count) for i in range(count)])


def dot(a, b, contract):
    return lax.dot_general(
        a, b, ((contract[:1], contract[1:]), ((), ())), preferred_element_type=jnp.float32
    )


def lanes(start, size):
    return pl.ds(pl.multiple_of(start, HEAD_SIZE), size)


def pack_kernel(head_count, groups, k_noisy, v_noisy, k_clean, v_clean, *outs):
    rows = k_noisy.shape[0]
    half = k_noisy.shape[1] // head_count
    width = HEAD_SIZE
    for index, group in enumerate(groups):
        for step in range(head_count):
            out = outs[index * head_count + step]
            target = lax.rem(lax.axis_index("head") + step, head_count)
            for at, member in enumerate(group):
                source = lanes(target * half + member * width, width)
                for n, (noisy, clean) in enumerate(((k_noisy, k_clean), (v_noisy, v_clean))):
                    to = slice((2 * at + n) * width, (2 * at + n + 1) * width)
                    out[:rows, to] = noisy[:, source]
                    out[rows:, to] = clean[:, source]


def packed(head_count, groups, k_noisy, v_noisy, k_clean, v_clean):
    vmem = pl.BlockSpec(memory_space=pltpu.VMEM)
    rows = k_noisy.shape[0] + k_clean.shape[0]
    shapes = [
        jax.ShapeDtypeStruct((rows, 2 * HEAD_SIZE * len(group)), jnp.bfloat16)
        for group in groups
        for _ in range(head_count)
    ]
    outs = pl.pallas_call(
        functools.partial(pack_kernel, head_count, groups),
        in_specs=[vmem] * 4,
        out_specs=[vmem] * len(shapes),
        out_shape=shapes,
        name="pack_keys_values",
    )(k_noisy, v_noisy, k_clean, v_clean)
    return [outs[i * head_count : (i + 1) * head_count] for i in range(len(groups))]


def attention_kernel(shape, column, kept, listed, place, own, *refs):
    head_count, group_rows, store_rows, clean_rows, slots = shape
    received, refs = refs[: head_count - 1], refs[head_count - 1 :]
    near, far, *refs = refs
    o_all, gq_all, *refs = refs[kept:]
    sends, refs = refs[: head_count - 1], refs[head_count - 1 :]
    near_grad, far_grad, k_all, v_all, q_all, g_all, o_out, gq_out, o_own, gq_own, copied = refs
    rows = own.shape[0] // 2
    width = HEAD_SIZE
    position, head = place[0], place[1]
    k_cols = slice(2 * column * width, (2 * column + 1) * width)
    v_cols = slice((2 * column + 1) * width, (2 * column + 2) * width)
    levels = ((near.shape[0] - group_rows) // store_rows).bit_length() - 1

    def placed(slot):
        apart = lax.bitwise_xor(position, slot)
        store = jnp.int32(0)
        for bit in range(1, levels + 1):
            bit_set = lax.bitwise_and(lax.shift_right_logical(apart, bit), 1)
            store = store + (bit_set << (levels - bit))
        block = jnp.maximum(listed[position, slot], 0)
        if clean_rows >= BLK:
            owner = lax.div(block * BLK, clean_rows)
            step = lax.rem(head - owner + head_count, head_count)
            inside = step * clean_rows + block * BLK - owner * clean_rows
        else:
            inside = block * BLK
        start = pl.multiple_of(group_rows + store * store_rows + inside, BLK)
        return lax.bitwise_and(apart, 1), pl.ds(start, BLK)

    k_all[:group_rows, :] = near[:group_rows, k_cols]
    v_all[:group_rows, :] = near[:group_rows, v_cols]
    k_all[group_rows : 2 * group_rows, :] = far[:group_rows, k_cols]
    v_all[group_rows : 2 * group_rows, :] = far[:group_rows, v_cols]
    span = 2 * group_rows
    total = span + slots * BLK
    for slot in range(slots):
        other, source = placed(slot)
        to = slice(span + slot * BLK, span + (slot + 1) * BLK)
        k_all[to, :] = jnp.where(other == 1, far[source, k_cols], near[source, k_cols])
        v_all[to, :] = jnp.where(other == 1, far[source, v_cols], near[source, v_cols])
    at = 0
    for r in range(HEADS_PER_GROUP):
        for part in (own, *received):
            q_all[at : at + rows, :] = part[:rows, r * width : (r + 1) * width]
            g_all[at : at + rows, :] = part[rows:, r * width : (r + 1) * width]
            at += rows

    keys = k_all[...]
    values = v_all[...]
    keys_t = keys.T
    values_t = values.T
    biases = [
        jnp.where(listed[position, slot] >= 0, 0.0, NEG_FILL).astype(jnp.float32)
        for slot in range(slots)
    ]
    cuts = list(range(0, at - SLICE_ROWS + 1, SLICE_ROWS)) + [at]
    slices = [slice(low, high) for low, high in zip(cuts, cuts[1:])]

    def products(piece):
        query, upstream = q_all[piece, :], g_all[piece, :]
        return query, upstream, dot(keys, query, (1, 1)), dot(values, upstream, (1, 1))

    def softmax(scores, dprob):
        scores = scores * (SCALE * LOG2E)
        pieces = [scores[:span]]
        for slot in range(slots):
            low = span + slot * BLK
            pieces.append(scores[low : low + BLK] + biases[slot])
        scores = jnp.concatenate(pieces, 0)
        top = jnp.max(scores, 0, keepdims=True)
        unscaled = jnp.exp2(scores - top)
        prob = unscaled * (1.0 / jnp.sum(unscaled, 0, keepdims=True))
        row_dot = jnp.sum(prob * dprob, 0, keepdims=True)
        return prob.astype(jnp.bfloat16), (prob * (dprob - row_dot)).astype(jnp.bfloat16)

    gk = jnp.zeros((total, width), jnp.float32)
    gv = jnp.zeros((total, width), jnp.float32)
    ahead = products(slices[0])
    for index, piece in enumerate(slices):
        query, upstream, scores, dprob = ahead
        if index + 1 < len(slices):
            ahead = products(slices[index + 1])
        weights, dscore = softmax(scores, dprob)
        o_out[piece, :] = dot(values_t, weights, (1, 0)).astype(jnp.bfloat16).T
        gq_out[piece, :] = (dot(keys_t, dscore, (1, 0)) * SCALE).astype(jnp.bfloat16).T
        gk = gk + dot(dscore, query, (1, 0))
        gv = gv + dot(weights, upstream, (1, 0))
    at = 0
    for r in range(HEADS_PER_GROUP):
        to = slice(r * width, (r + 1) * width)
        for part in (None, *sends):
            attended, gq = o_out[at : at + rows, :], gq_out[at : at + rows, :]
            if part is None:
                o_own[:, to] = attended
                gq_own[:, to] = gq
            else:
                part[:rows, to] = attended
                part[rows:, to] = gq
            at += rows
    start = (head * (KEY_VALUE_HEADS // head_count) + place[2]) * GROUP_WIDTH
    target = lanes(start, GROUP_WIDTH)
    copies = [
        pltpu.make_async_copy(o_own, o_all.at[:, target], copied.at[0]),
        pltpu.make_async_copy(gq_own, gq_all.at[:, target], copied.at[1]),
    ]
    for copy in copies:
        copy.start()
    gk = (gk * SCALE).astype(jnp.bfloat16)
    gv = gv.astype(jnp.bfloat16)
    for index, grad in enumerate((near_grad, far_grad)):
        here = slice(index * group_rows, (index + 1) * group_rows)
        grad[:group_rows, k_cols] = gk[here]
        grad[:group_rows, v_cols] = gv[here]
        rest = grad.shape[0] - group_rows
        grad[group_rows:, k_cols] = jnp.zeros((rest, width), jnp.bfloat16)
        grad[group_rows:, v_cols] = jnp.zeros((rest, width), jnp.bfloat16)
    for slot in range(slots):
        other, target = placed(slot)
        low = span + slot * BLK
        for index, grad in enumerate((near_grad, far_grad)):

            @pl.when(jnp.logical_and(listed[position, slot] >= 0, other == index))
            def _():
                grad[target, k_cols] = gk[low : low + BLK]
                grad[target, v_cols] = gv[low : low + BLK]

    for copy in copies:
        copy.wait()


def attention(listed, place, own, received, near, far, carried, shape, column):
    head_count, group_rows, store_rows, clean_rows, slots = shape
    rows = own.shape[0] // 2
    total = 2 * group_rows + slots * BLK
    stacked = HEADS_PER_GROUP * group_rows
    smem = pl.BlockSpec(memory_space=pltpu.SMEM)
    vmem = pl.BlockSpec(memory_space=pltpu.VMEM)
    hbm = pl.BlockSpec(memory_space=pl.ANY)
    kept = [i for i, array in enumerate(carried) if not isinstance(array, jax.ShapeDtypeStruct)]
    first_carried = 3 + len(received) + 2
    spaces = [hbm, hbm] + [vmem] * (len(carried) - 2)
    return pl.pallas_call(
        functools.partial(attention_kernel, shape, column, len(kept)),
        in_specs=[smem, smem] + [vmem] * (3 + len(received)) + [spaces[i] for i in kept],
        out_specs=spaces,
        scratch_shapes=[pltpu.VMEM((total, HEAD_SIZE), jnp.bfloat16)] * 2
        + [pltpu.VMEM((stacked, HEAD_SIZE), jnp.bfloat16)] * 4
        + [pltpu.VMEM((rows, GROUP_WIDTH), jnp.bfloat16)] * 2
        + [pltpu.SemaphoreType.DMA((2,))],
        out_shape=[jax.ShapeDtypeStruct(array.shape, jnp.bfloat16) for array in carried],
        input_output_aliases={first_carried + n: i for n, i in enumerate(kept)},
        compiler_params=pltpu.CompilerParams(vmem_limit_bytes=KERNEL_VMEM),
        cost_estimate=pl.CostEstimate(
            flops=24 * group_rows * HEADS_PER_GROUP * HEAD_SIZE * total,
            bytes_accessed=16 * group_rows * GROUP_WIDTH,
            transcendentals=group_rows * HEADS_PER_GROUP * total,
        ),
        name="span_attention",
    )(listed, place, own, *received, near, far, *[carried[i] for i in kept])


def unpack_kernel(head_count, groups, *refs):
    parts, outs = refs[:-4], refs[-4:]
    rows = outs[0].shape[0]
    half = outs[0].shape[1] // head_count
    width = HEAD_SIZE
    for step in range(head_count):
        source = lax.rem(lax.axis_index("head") + step, head_count)
        for group, members in enumerate(groups):
            part = parts[group * head_count + step]
            for at, member in enumerate(members):
                to = lanes(source * half + member * width, width)
                for index in range(2):
                    here = slice((2 * at + index) * width, (2 * at + index + 1) * width)
                    outs[index][:, to] = part[:rows, here]
                    outs[2 + index][:, to] = part[rows:, here]


def unpacked(head_count, groups, grads, rows, clean_rows):
    vmem = pl.BlockSpec(memory_space=pltpu.VMEM)
    parts = [part for chunk in grads for part in chunk]
    width = KEY_VALUE_HEADS * HEAD_SIZE
    return pl.pallas_call(
        functools.partial(unpack_kernel, head_count, groups),
        in_specs=[vmem] * len(parts),
        out_specs=[vmem] * 4,
        out_shape=[jax.ShapeDtypeStruct((rows, width), jnp.bfloat16)] * 2
        + [jax.ShapeDtypeStruct((clean_rows, width), jnp.bfloat16)] * 2,
        name="unpack_gradients",
    )(*parts)


def shards(
    queries,
    noisy_token_keys,
    noisy_token_values,
    clean_token_keys,
    clean_token_values,
    output_gradient,
    history_list,
):
    ctx_count = lax.axis_size("ctx")
    head_count = lax.axis_size("head")
    head = lax.axis_index("head")
    place = jnp.stack([lax.axis_index("ctx"), head]).astype(jnp.int32)
    rows = queries.shape[0]
    clean_rows = clean_token_keys.shape[0]
    store_rows = clean_rows * head_count
    group_rows = rows * head_count
    slots = ctx_count - 2
    per_device = KEY_VALUE_HEADS // head_count
    everything = list(range(per_device))
    half = max(1, per_device // 2)
    key_groups = [g for g in (everything[:half], everything[half:]) if g]
    grad_groups = key_groups
    ask_groups = send_groups = [[m] for m in everything]
    top = ctx_count.bit_length() - 2
    steps = range(1, head_count)
    row_order = lax.rem(head - jnp.arange(head_count, dtype=jnp.int32) + head_count, head_count)

    def by_block(store):
        if clean_rows >= BLK:
            return store
        return store.reshape(head_count, clean_rows, -1)[row_order].reshape(store.shape)

    packs = packed(
        head_count,
        key_groups,
        noisy_token_keys,
        noisy_token_values,
        clean_token_keys,
        clean_token_values,
    )

    def own_columns(array, member, step):
        start = (lax.rem(head + step, head_count) * per_device + member) * GROUP_WIDTH
        return lax.dynamic_slice_in_dim(array, start, GROUP_WIDTH, 1)

    def swap_keys(index):
        return [packs[index][0]] + [shifted(packs[index][step], step) for step in steps]

    def query_block(member, step):
        return jnp.concatenate(
            [own_columns(array, member, step) for array in (queries, output_gradient)], 0
        )

    asks = [[query_block(member, step) for step in range(head_count)] for member in everything]

    def swap_queries(member):
        return [shifted(asks[member][step], step) for step in steps]

    def stored(parts):
        return by_block(jnp.concatenate([part[rows:] for part in parts], 0))

    def doubled(line, bit):
        return jnp.concatenate([line, flipped(line, 1 << bit)], 0)

    def joined(parts, line):
        return jnp.concatenate([part[:rows] for part in parts] + [line], 0)

    def summed(near_grad, from_core):
        total = near_grad.astype(jnp.float32) + from_core.astype(jnp.float32)
        return total[:group_rows], total[group_rows:]

    def halved(line, bit):
        middle = line.shape[0] // 2
        return line[:middle], flipped(line[middle:].astype(jnp.bfloat16), 1 << bit)

    together = lax.optimization_barrier
    def swap_heads(noisy_sum, store_sum):
        if clean_rows < BLK:
            store_sum = store_sum.reshape(head_count, clean_rows, -1)[row_order].reshape(
                store_sum.shape
            )
        store_sum = store_sum.astype(jnp.bfloat16)
        noisy_sum = noisy_sum.astype(jnp.bfloat16)
        mixed = [
            jnp.concatenate(
                [
                    noisy_sum[step * rows : (step + 1) * rows],
                    store_sum[step * clean_rows : (step + 1) * clean_rows],
                ],
                0,
            )
            for step in range(head_count)
        ]
        return [mixed[0]] + [shifted(mixed[step], -step) for step in steps]

    shape = (head_count, group_rows, store_rows, clean_rows, slots)
    received = {}
    two = len(key_groups) > 1
    parts = swap_keys(0)
    line = stored(parts)
    if two:
        packs[1], parts, asks = together((packs[1], parts, asks))
        later_parts = swap_keys(1)
    asked = 0
    for bit in range(top, 0, -1):
        line = doubled(line, bit)
        if two and bit == top:
            line, later_parts = together((line, later_parts))
            later_line = stored(later_parts)
            received[0] = swap_queries(0)
        elif two and bit <= 2:
            line, later_line, received[2 - bit] = together((line, later_line, received[2 - bit]))
            asks, _ = together((asks, received[2 - bit]))
            received[3 - bit] = swap_queries(3 - bit)
        elif two:
            line, later_line = together((line, later_line))
        if two and bit > 1:
            later_line = doubled(later_line, bit)
    if not two:
        received[0] = swap_queries(0)
    near = joined(parts, line)
    keys = {0: (near, flipped(near, 1))}
    if two:
        crossing = flipped(later_line, 2)

    outputs = [jax.ShapeDtypeStruct(queries.shape, jnp.bfloat16)] * 2
    sent = []
    waiting = []

    def group_of(groups, member):
        return next(i for i, group in enumerate(groups) if member in group)

    for member in everything:
        k = group_of(key_groups, member)
        first = member == key_groups[k][0]
        last = member == key_groups[k][-1]
        sends = [jax.ShapeDtypeStruct((2 * rows, GROUP_WIDTH), jnp.bfloat16)] * (head_count - 1)
        if first:
            width = len(key_groups[k]) * 2 * HEAD_SIZE
            pair = [jax.ShapeDtypeStruct((near.shape[0], width), jnp.bfloat16)] * 2
        column = key_groups[k].index(member)
        outputs[0], outputs[1], *rest = attention(
            history_list,
            jnp.concatenate([place, jnp.array([member], jnp.int32)]),
            asks[member][0],
            received[member],
            *keys[k],
            [*outputs, *sends, *pair],
            shape,
            column,
        )
        sends, pair = rest[:-2], rest[-2:]
        for later in range(3, per_device):
            if member == later - 3:
                asks, outputs = together((asks, outputs))
                received[later] = swap_queries(later)
            if member == later - 2:
                pair, received[later] = together((pair, received[later]))
        sent.append([shifted(block, -step) for step, block in zip(steps, sends)])
        if two and member == 0:
            outputs, crossing, received[2] = together((outputs, crossing, received[2]))
            near = joined(later_parts, jnp.concatenate([later_line, crossing], 0))
            keys[1] = (near, flipped(near, 1))
        if waiting and not last:
            noisy_sum, line = summed(*waiting[0])
            line, outputs, sent[: half - 1] = together((line, outputs, sent[: half - 1]))
            waiting[0] = (noisy_sum, *halved(line, 1))
        if last:
            if waiting:
                waiting[0], pair, sent[:half] = together((waiting[0], pair, sent[:half]))
            from_core = flipped(pair[1], 1)
            if waiting:
                from_core, waiting[0] = together((from_core, waiting[0]))
            waiting.append((pair[0], from_core))
    grads = []
    for index, state in enumerate(waiting):
        if len(state) == 2:
            noisy_sum, line = summed(*state)
            keep, other = halved(line, 1)
        else:
            noisy_sum, keep, other = state
        line = keep + other.astype(jnp.float32)
        for bit in range(2, top + 1):
            keep, other = halved(line, bit)
            line = keep + other.astype(jnp.float32)
        if index:
            line, sent[half:] = together((line, sent[half:]))
        grads.append(swap_heads(noisy_sum, line))
    attended, query_grad = outputs
    for group, blocks in zip(send_groups, sent):
        for step, block in zip(steps, blocks):
            source = lax.rem(head + step, head_count)
            start = (source * per_device + group[0]) * GROUP_WIDTH
            attended = lax.dynamic_update_slice_in_dim(attended, block[:rows], start, 1)
            query_grad = lax.dynamic_update_slice_in_dim(query_grad, block[rows:], start, 1)
    finished = unpacked(head_count, grad_groups, grads, rows, clean_rows)
    return (attended, query_grad, *finished)


def solution(mesh):
    split = P(("ctx", "head"), None)
    return jax.shard_map(
        shards,
        mesh=mesh,
        in_specs=(split, split, split, split, split, split, P()),
        out_specs=(split,) * 6,
        check_vma=False,
    )
```

```python
import functools

import jax
import jax.numpy as jnp
from jax import lax
from jax.experimental import pallas as pl
from jax.experimental.pallas import tpu as pltpu
from jax.sharding import PartitionSpec as P

QUERY_HEADS = 48
KEY_VALUE_HEADS = 8
HEAD_SIZE = 128
BLK = 32
HEADS_PER_GROUP = QUERY_HEADS // KEY_VALUE_HEADS
GROUP_WIDTH = HEADS_PER_GROUP * HEAD_SIZE
SCALE = HEAD_SIZE**-0.5
LOG2E = 1.4426950408889634

NEG_FILL = -1e30
SLICE_ROWS = 256
KERNEL_VMEM = 32 * 2**20


def flipped(block, bits):
    count = lax.axis_size("ctx")
    return lax.ppermute(block, "ctx", [(i, i ^ bits) for i in range(count)])


def shifted(block, step):
    count = lax.axis_size("head")
    return lax.ppermute(block, "head", [(i, (i + step) % count) for i in range(count)])


def dot(a, b, contract):
    return lax.dot_general(
        a, b, ((contract[:1], contract[1:]), ((), ())), preferred_element_type=jnp.float32
    )


def lanes(start, size):
    return pl.ds(pl.multiple_of(start, HEAD_SIZE), size)


def pack_kernel(head_count, groups, k_noisy, v_noisy, k_clean, v_clean, *outs):
    rows = k_noisy.shape[0]
    half = k_noisy.shape[1] // head_count
    width = HEAD_SIZE
    for index, group in enumerate(groups):
        for step in range(head_count):
            out = outs[index * head_count + step]
            target = lax.rem(lax.axis_index("head") + step, head_count)
            for at, member in enumerate(group):
                source = lanes(target * half + member * width, width)
                for n, (noisy, clean) in enumerate(((k_noisy, k_clean), (v_noisy, v_clean))):
                    to = slice((2 * at + n) * width, (2 * at + n + 1) * width)
                    out[:rows, to] = noisy[:, source]
                    out[rows:, to] = clean[:, source]


def packed(head_count, groups, k_noisy, v_noisy, k_clean, v_clean):
    vmem = pl.BlockSpec(memory_space=pltpu.VMEM)
    rows = k_noisy.shape[0] + k_clean.shape[0]
    shapes = [
        jax.ShapeDtypeStruct((rows, 2 * HEAD_SIZE * len(group)), jnp.bfloat16)
        for group in groups
        for _ in range(head_count)
    ]
    outs = pl.pallas_call(
        functools.partial(pack_kernel, head_count, groups),
        in_specs=[vmem] * 4,
        out_specs=[vmem] * len(shapes),
        out_shape=shapes,
        name="pack_keys_values",
    )(k_noisy, v_noisy, k_clean, v_clean)
    return [outs[i * head_count : (i + 1) * head_count] for i in range(len(groups))]


def attention_kernel(shape, column, kept, listed, place, own, *refs):
    head_count, group_rows, store_rows, clean_rows, slots = shape
    received, refs = refs[: head_count - 1], refs[head_count - 1 :]
    near, far, *refs = refs
    o_all, gq_all, *refs = refs[kept:]
    sends, refs = refs[: head_count - 1], refs[head_count - 1 :]
    near_grad, far_grad, k_all, v_all, q_all, g_all, o_out, gq_out, o_own, gq_own, copied = refs
    rows = own.shape[0] // 2
    width = HEAD_SIZE
    position, head = place[0], place[1]
    k_cols = slice(2 * column * width, (2 * column + 1) * width)
    v_cols = slice((2 * column + 1) * width, (2 * column + 2) * width)
    levels = ((near.shape[0] - group_rows) // store_rows).bit_length() - 1

    def placed(slot):
        apart = lax.bitwise_xor(position, slot)
        store = jnp.int32(0)
        for bit in range(1, levels + 1):
            bit_set = lax.bitwise_and(lax.shift_right_logical(apart, bit), 1)
            store = store + (bit_set << (levels - bit))
        block = jnp.maximum(listed[position, slot], 0)
        if clean_rows >= BLK:
            owner = lax.div(block * BLK, clean_rows)
            step = lax.rem(head - owner + head_count, head_count)
            inside = step * clean_rows + block * BLK - owner * clean_rows
        else:
            inside = block * BLK
        start = pl.multiple_of(group_rows + store * store_rows + inside, BLK)
        return lax.bitwise_and(apart, 1), pl.ds(start, BLK)

    k_all[:group_rows, :] = near[:group_rows, k_cols]
    v_all[:group_rows, :] = near[:group_rows, v_cols]
    k_all[group_rows : 2 * group_rows, :] = far[:group_rows, k_cols]
    v_all[group_rows : 2 * group_rows, :] = far[:group_rows, v_cols]
    span = 2 * group_rows
    total = span + slots * BLK
    for slot in range(slots):
        other, source = placed(slot)
        to = slice(span + slot * BLK, span + (slot + 1) * BLK)
        k_all[to, :] = jnp.where(other == 1, far[source, k_cols], near[source, k_cols])
        v_all[to, :] = jnp.where(other == 1, far[source, v_cols], near[source, v_cols])
    at = 0
    for r in range(HEADS_PER_GROUP):
        for part in (own, *received):
            q_all[at : at + rows, :] = part[:rows, r * width : (r + 1) * width]
            g_all[at : at + rows, :] = part[rows:, r * width : (r + 1) * width]
            at += rows

    keys = k_all[...]
    values = v_all[...]
    keys_t = keys.T
    values_t = values.T
    biases = [
        jnp.where(listed[position, slot] >= 0, 0.0, NEG_FILL).astype(jnp.float32)
        for slot in range(slots)
    ]
    cuts = list(range(0, at - SLICE_ROWS + 1, SLICE_ROWS)) + [at]
    slices = [slice(low, high) for low, high in zip(cuts, cuts[1:])]

    def products(piece):
        query, upstream = q_all[piece, :], g_all[piece, :]
        return query, upstream, dot(keys, query, (1, 1)), dot(values, upstream, (1, 1))

    def softmax(scores, dprob):
        scores = scores * (SCALE * LOG2E)
        pieces = [scores[:span]]
        for slot in range(slots):
            low = span + slot * BLK
            pieces.append(scores[low : low + BLK] + biases[slot])
        scores = jnp.concatenate(pieces, 0)
        top = jnp.max(scores, 0, keepdims=True)
        unscaled = jnp.exp2(scores - top)
        prob = unscaled * (1.0 / jnp.sum(unscaled, 0, keepdims=True))
        row_dot = jnp.sum(prob * dprob, 0, keepdims=True)
        return prob.astype(jnp.bfloat16), (prob * (dprob - row_dot)).astype(jnp.bfloat16)

    gk = jnp.zeros((total, width), jnp.float32)
    gv = jnp.zeros((total, width), jnp.float32)
    ahead = products(slices[0])
    for index, piece in enumerate(slices):
        query, upstream, scores, dprob = ahead
        if index + 1 < len(slices):
            ahead = products(slices[index + 1])
        weights, dscore = softmax(scores, dprob)
        o_out[piece, :] = dot(values_t, weights, (1, 0)).astype(jnp.bfloat16).T
        gq_out[piece, :] = (dot(keys_t, dscore, (1, 0)) * SCALE).astype(jnp.bfloat16).T
        gk = gk + dot(dscore, query, (1, 0))
        gv = gv + dot(weights, upstream, (1, 0))
    at = 0
    for r in range(HEADS_PER_GROUP):
        to = slice(r * width, (r + 1) * width)
        for part in (None, *sends):
            attended, gq = o_out[at : at + rows, :], gq_out[at : at + rows, :]
            if part is None:
                o_own[:, to] = attended
                gq_own[:, to] = gq
            else:
                part[:rows, to] = attended
                part[rows:, to] = gq
            at += rows
    start = (head * (KEY_VALUE_HEADS // head_count) + place[2]) * GROUP_WIDTH
    target = lanes(start, GROUP_WIDTH)
    copies = [
        pltpu.make_async_copy(o_own, o_all.at[:, target], copied.at[0]),
        pltpu.make_async_copy(gq_own, gq_all.at[:, target], copied.at[1]),
    ]
    for copy in copies:
        copy.start()
    gk = (gk * SCALE).astype(jnp.bfloat16)
    gv = gv.astype(jnp.bfloat16)
    for index, grad in enumerate((near_grad, far_grad)):
        here = slice(index * group_rows, (index + 1) * group_rows)
        grad[:group_rows, k_cols] = gk[here]
        grad[:group_rows, v_cols] = gv[here]
        rest = grad.shape[0] - group_rows
        grad[group_rows:, k_cols] = jnp.zeros((rest, width), jnp.bfloat16)
        grad[group_rows:, v_cols] = jnp.zeros((rest, width), jnp.bfloat16)
    for slot in range(slots):
        other, target = placed(slot)
        low = span + slot * BLK
        for index, grad in enumerate((near_grad, far_grad)):

            @pl.when(jnp.logical_and(listed[position, slot] >= 0, other == index))
            def _():
                grad[target, k_cols] = gk[low : low + BLK]
                grad[target, v_cols] = gv[low : low + BLK]

    for copy in copies:
        copy.wait()


def attention(listed, place, own, received, near, far, carried, shape, column):
    head_count, group_rows, store_rows, clean_rows, slots = shape
    rows = own.shape[0] // 2
    total = 2 * group_rows + slots * BLK
    stacked = HEADS_PER_GROUP * group_rows
    smem = pl.BlockSpec(memory_space=pltpu.SMEM)
    vmem = pl.BlockSpec(memory_space=pltpu.VMEM)
    hbm = pl.BlockSpec(memory_space=pl.ANY)
    kept = [i for i, array in enumerate(carried) if not isinstance(array, jax.ShapeDtypeStruct)]
    first_carried = 3 + len(received) + 2
    spaces = [hbm, hbm] + [vmem] * (len(carried) - 2)
    return pl.pallas_call(
        functools.partial(attention_kernel, shape, column, len(kept)),
        in_specs=[smem, smem] + [vmem] * (3 + len(received)) + [spaces[i] for i in kept],
        out_specs=spaces,
        scratch_shapes=[pltpu.VMEM((total, HEAD_SIZE), jnp.bfloat16)] * 2
        + [pltpu.VMEM((stacked, HEAD_SIZE), jnp.bfloat16)] * 4
        + [pltpu.VMEM((rows, GROUP_WIDTH), jnp.bfloat16)] * 2
        + [pltpu.SemaphoreType.DMA((2,))],
        out_shape=[jax.ShapeDtypeStruct(array.shape, jnp.bfloat16) for array in carried],
        input_output_aliases={first_carried + n: i for n, i in enumerate(kept)},
        compiler_params=pltpu.CompilerParams(vmem_limit_bytes=KERNEL_VMEM),
        cost_estimate=pl.CostEstimate(
            flops=8 * group_rows * HEADS_PER_GROUP * HEAD_SIZE * total,
            bytes_accessed=16 * group_rows * GROUP_WIDTH,
            transcendentals=group_rows * HEADS_PER_GROUP * total,
        ),
        name="span_attention",
    )(listed, place, own, *received, near, far, *[carried[i] for i in kept])


def unpack_kernel(head_count, groups, *refs):
    parts, outs = refs[:-4], refs[-4:]
    rows = outs[0].shape[0]
    half = outs[0].shape[1] // head_count
    width = HEAD_SIZE
    for step in range(head_count):
        source = lax.rem(lax.axis_index("head") + step, head_count)
        for group, members in enumerate(groups):
            part = parts[group * head_count + step]
            for at, member in enumerate(members):
                to = lanes(source * half + member * width, width)
                for index in range(2):
                    here = slice((2 * at + index) * width, (2 * at + index + 1) * width)
                    outs[index][:, to] = part[:rows, here]
                    outs[2 + index][:, to] = part[rows:, here]


def unpacked(head_count, groups, grads, rows, clean_rows):
    vmem = pl.BlockSpec(memory_space=pltpu.VMEM)
    parts = [part for chunk in grads for part in chunk]
    width = KEY_VALUE_HEADS * HEAD_SIZE
    return pl.pallas_call(
        functools.partial(unpack_kernel, head_count, groups),
        in_specs=[vmem] * len(parts),
        out_specs=[vmem] * 4,
        out_shape=[jax.ShapeDtypeStruct((rows, width), jnp.bfloat16)] * 2
        + [jax.ShapeDtypeStruct((clean_rows, width), jnp.bfloat16)] * 2,
        name="unpack_gradients",
    )(*parts)


def shards(
    queries,
    noisy_token_keys,
    noisy_token_values,
    clean_token_keys,
    clean_token_values,
    output_gradient,
    history_list,
):
    ctx_count = lax.axis_size("ctx")
    head_count = lax.axis_size("head")
    head = lax.axis_index("head")
    place = jnp.stack([lax.axis_index("ctx"), head]).astype(jnp.int32)
    rows = queries.shape[0]
    clean_rows = clean_token_keys.shape[0]
    store_rows = clean_rows * head_count
    group_rows = rows * head_count
    slots = ctx_count - 2
    per_device = KEY_VALUE_HEADS // head_count
    everything = list(range(per_device))
    half = max(1, per_device // 2)
    key_groups = [g for g in (everything[:half], everything[half:]) if g]
    grad_groups = key_groups
    ask_groups = send_groups = [[m] for m in everything]
    top = ctx_count.bit_length() - 2
    steps = range(1, head_count)
    row_order = lax.rem(head - jnp.arange(head_count, dtype=jnp.int32) + head_count, head_count)

    def by_block(store):
        if clean_rows >= BLK:
            return store
        return store.reshape(head_count, clean_rows, -1)[row_order].reshape(store.shape)

    packs = packed(
        head_count,
        key_groups,
        noisy_token_keys,
        noisy_token_values,
        clean_token_keys,
        clean_token_values,
    )

    def own_columns(array, member, step):
        start = (lax.rem(head + step, head_count) * per_device + member) * GROUP_WIDTH
        return lax.dynamic_slice_in_dim(array, start, GROUP_WIDTH, 1)

    def swap_keys(index):
        return [packs[index][0]] + [shifted(packs[index][step], step) for step in steps]

    def query_block(member, step):
        return jnp.concatenate(
            [own_columns(array, member, step) for array in (queries, output_gradient)], 0
        )

    asks = [[query_block(member, step) for step in range(head_count)] for member in everything]

    def swap_queries(member):
        return [shifted(asks[member][step], step) for step in steps]

    def stored(parts):
        return by_block(jnp.concatenate([part[rows:] for part in parts], 0))

    def doubled(line, bit):
        return jnp.concatenate([line, flipped(line, 1 << bit)], 0)

    def joined(parts, line):
        return jnp.concatenate([part[:rows] for part in parts] + [line], 0)

    def summed(near_grad, from_core):
        total = near_grad.astype(jnp.float32) + from_core.astype(jnp.float32)
        return total[:group_rows], total[group_rows:]

    def halved(line, bit):
        middle = line.shape[0] // 2
        return line[:middle], flipped(line[middle:].astype(jnp.bfloat16), 1 << bit)

    together = lax.optimization_barrier
    def swap_heads(noisy_sum, store_sum):
        if clean_rows < BLK:
            store_sum = store_sum.reshape(head_count, clean_rows, -1)[row_order].reshape(
                store_sum.shape
            )
        store_sum = store_sum.astype(jnp.bfloat16)
        noisy_sum = noisy_sum.astype(jnp.bfloat16)
        mixed = [
            jnp.concatenate(
                [
                    noisy_sum[step * rows : (step + 1) * rows],
                    store_sum[step * clean_rows : (step + 1) * clean_rows],
                ],
                0,
            )
            for step in range(head_count)
        ]
        return [mixed[0]] + [shifted(mixed[step], -step) for step in steps]

    shape = (head_count, group_rows, store_rows, clean_rows, slots)
    received = {}
    two = len(key_groups) > 1
    parts = swap_keys(0)
    line = stored(parts)
    if two:
        packs[1], parts = together((packs[1], parts))
        later_parts = swap_keys(1)
    for bit in range(top, 0, -1):
        other = flipped(line, 1 << bit)
        if two and bit == top - 1:
            other, later_parts = together((other, later_parts))
            later_line = stored(later_parts)
            later_other = flipped(later_line, 1 << top)
            asks, other = together((asks, other))
            received[0] = swap_queries(0)
        elif two and bit < top - 1:
            other, later_other = together((other, later_other))
            later_line = jnp.concatenate([later_line, later_other], 0)
            later_other = flipped(later_line, 1 << (bit + 1))
        line = jnp.concatenate([line, other], 0)
    near = joined(parts, line)
    if two:
        near, asks, received[0] = together((near, asks, received[0]))
        received[1] = swap_queries(1)
    else:
        received[0] = swap_queries(0)
    keys = {0: (near, flipped(near, 1))}
    outputs = [jax.ShapeDtypeStruct(queries.shape, jnp.bfloat16)] * 2
    sent = []
    held = []
    waiting = []

    def group_of(groups, member):
        return next(i for i, group in enumerate(groups) if member in group)

    for member in everything:
        k = group_of(key_groups, member)
        first = member == key_groups[k][0]
        last = member == key_groups[k][-1]
        sends = [jax.ShapeDtypeStruct((2 * rows, GROUP_WIDTH), jnp.bfloat16)] * (head_count - 1)
        if first:
            width = len(key_groups[k]) * 2 * HEAD_SIZE
            pair = [jax.ShapeDtypeStruct((near.shape[0], width), jnp.bfloat16)] * 2
        column = key_groups[k].index(member)
        outputs[0], outputs[1], *rest = attention(
            history_list,
            jnp.concatenate([place, jnp.array([member], jnp.int32)]),
            asks[member][0],
            received[member],
            *keys[k],
            [*outputs, *sends, *pair],
            shape,
            column,
        )
        sends, pair = rest[:-2], rest[-2:]
        if two and member == 0:
            outputs, later_other, received[1] = together((outputs, later_other, received[1]))
            later_line = jnp.concatenate([later_line, later_other], 0)
            crossing = flipped(later_line, 2)
        if two and member == 1:
            outputs, crossing = together((outputs, crossing))
            near = joined(later_parts, jnp.concatenate([later_line, crossing], 0))
            keys[1] = (near, flipped(near, 1))
        if member + 2 < per_device:
            asks, outputs = together((asks, outputs))
            received[member + 2] = swap_queries(member + 2)
        if member == 1 and two:
            pair, received[2] = together((pair, received[2]))
        elif 1 < member < everything[-1]:
            outputs, received[member + 1] = together((outputs, received[member + 1]))
        held.append(sends)
        if two and member == half:
            held[half - 1], outputs = together((held[half - 1], outputs))
        if not two or member >= half - 1:
            later = len(held) if member == everything[-1] else len(held) - 1
            for block_set in held[len(sent) : later]:
                sent.append([shifted(block, -step) for step, block in zip(steps, block_set)])
        if waiting and not last:
            noisy_sum, line = summed(*waiting[0])
            line, outputs, sent[0] = together((line, outputs, sent[0]))
            waiting[0] = (noisy_sum, *halved(line, 1))
        if last:
            if waiting:
                waiting[0], pair, sent[:half] = together((waiting[0], pair, sent[:half]))
            waiting.append((pair[0], flipped(pair[1], 1)))
    grads = []
    noisy_sum, line = summed(*waiting[-1])
    if two:
        first_noisy, keep, other = waiting[0]
        first_line = keep + other.astype(jnp.float32)
        first_keep, first_other = halved(first_line, 2)
    for bit in range(1, top + 1):
        keep, other = halved(line, bit)
        if two:
            other, first_other, sent[:half] = together((other, first_other, sent[:half]))
            if bit < top:
                first_line = first_keep + first_other.astype(jnp.float32)
            if bit + 2 <= top:
                first_keep, first_other = halved(first_line, bit + 2)
            elif bit + 1 == top:
                grads.append(swap_heads(first_noisy, first_line))
        line = keep + other.astype(jnp.float32)
    if two:
        line, sent[half:] = together((line, sent[half:]))
    grads.append(swap_heads(noisy_sum, line))
    attended, query_grad = outputs
    for group, blocks in zip(send_groups, sent):
        for step, block in zip(steps, blocks):
            source = lax.rem(head + step, head_count)
            start = (source * per_device + group[0]) * GROUP_WIDTH
            attended = lax.dynamic_update_slice_in_dim(attended, block[:rows], start, 1)
            query_grad = lax.dynamic_update_slice_in_dim(query_grad, block[rows:], start, 1)
    finished = unpacked(head_count, grad_groups, grads, rows, clean_rows)
    return (attended, query_grad, *finished)


def solution(mesh):
    split = P(("ctx", "head"), None)
    return jax.shard_map(
        shards,
        mesh=mesh,
        in_specs=(split, split, split, split, split, split, P()),
        out_specs=(split,) * 6,
        check_vma=False,
    )
```

```python
import functools

import jax
import jax.numpy as jnp
from jax import lax
from jax.experimental import pallas as pl
from jax.experimental.pallas import tpu as pltpu
from jax.sharding import PartitionSpec as P

QUERY_HEADS = 48
KEY_VALUE_HEADS = 8
HEAD_SIZE = 128
BLK = 32
HEADS_PER_GROUP = QUERY_HEADS // KEY_VALUE_HEADS
GROUP_WIDTH = HEADS_PER_GROUP * HEAD_SIZE
SCALE = HEAD_SIZE**-0.5
LOG2E = 1.4426950408889634

NEG_FILL = -1e30
SLICE_ROWS = 256
KERNEL_VMEM = 32 * 2**20


def flipped(block, bits):
    count = lax.axis_size("ctx")
    return lax.ppermute(block, "ctx", [(i, i ^ bits) for i in range(count)])


def shifted(block, step):
    count = lax.axis_size("head")
    return lax.ppermute(block, "head", [(i, (i + step) % count) for i in range(count)])


def dot(a, b, contract):
    return lax.dot_general(
        a, b, ((contract[:1], contract[1:]), ((), ())), preferred_element_type=jnp.float32
    )


def lanes(start, size):
    return pl.ds(pl.multiple_of(start, HEAD_SIZE), size)


def pack_kernel(head_count, groups, k_noisy, v_noisy, k_clean, v_clean, *outs):
    rows = k_noisy.shape[0]
    half = k_noisy.shape[1] // head_count
    width = HEAD_SIZE
    for index, group in enumerate(groups):
        for step in range(head_count):
            out = outs[index * head_count + step]
            target = lax.rem(lax.axis_index("head") + step, head_count)
            for at, member in enumerate(group):
                source = lanes(target * half + member * width, width)
                for n, (noisy, clean) in enumerate(((k_noisy, k_clean), (v_noisy, v_clean))):
                    to = slice((2 * at + n) * width, (2 * at + n + 1) * width)
                    out[:rows, to] = noisy[:, source]
                    out[rows:, to] = clean[:, source]


def packed(head_count, groups, k_noisy, v_noisy, k_clean, v_clean):
    vmem = pl.BlockSpec(memory_space=pltpu.VMEM)
    rows = k_noisy.shape[0] + k_clean.shape[0]
    shapes = [
        jax.ShapeDtypeStruct((rows, 2 * HEAD_SIZE * len(group)), jnp.bfloat16)
        for group in groups
        for _ in range(head_count)
    ]
    outs = pl.pallas_call(
        functools.partial(pack_kernel, head_count, groups),
        in_specs=[vmem] * 4,
        out_specs=[vmem] * len(shapes),
        out_shape=shapes,
        name="pack_keys_values",
    )(k_noisy, v_noisy, k_clean, v_clean)
    return [outs[i * head_count : (i + 1) * head_count] for i in range(len(groups))]


def attention_kernel(shape, column, kept, listed, place, own, *refs):
    head_count, group_rows, store_rows, clean_rows, slots = shape
    received, refs = refs[: head_count - 1], refs[head_count - 1 :]
    near, far, *refs = refs
    o_all, gq_all, *refs = refs[kept:]
    sends, refs = refs[: head_count - 1], refs[head_count - 1 :]
    near_grad, far_grad, k_all, v_all, q_all, g_all, o_out, gq_out, o_own, gq_own, copied = refs
    rows = own.shape[0] // 2
    width = HEAD_SIZE
    position, head = place[0], place[1]
    k_cols = slice(2 * column * width, (2 * column + 1) * width)
    v_cols = slice((2 * column + 1) * width, (2 * column + 2) * width)
    levels = ((near.shape[0] - group_rows) // store_rows).bit_length() - 1

    def placed(slot):
        apart = lax.bitwise_xor(position, slot)
        store = jnp.int32(0)
        for bit in range(1, levels + 1):
            bit_set = lax.bitwise_and(lax.shift_right_logical(apart, bit), 1)
            store = store + (bit_set << (levels - bit))
        block = jnp.maximum(listed[position, slot], 0)
        if clean_rows >= BLK:
            owner = lax.div(block * BLK, clean_rows)
            step = lax.rem(head - owner + head_count, head_count)
            inside = step * clean_rows + block * BLK - owner * clean_rows
        else:
            inside = block * BLK
        start = pl.multiple_of(group_rows + store * store_rows + inside, BLK)
        return lax.bitwise_and(apart, 1), pl.ds(start, BLK)

    k_all[:group_rows, :] = near[:group_rows, k_cols]
    v_all[:group_rows, :] = near[:group_rows, v_cols]
    k_all[group_rows : 2 * group_rows, :] = far[:group_rows, k_cols]
    v_all[group_rows : 2 * group_rows, :] = far[:group_rows, v_cols]
    span = 2 * group_rows
    total = span + slots * BLK
    for slot in range(slots):
        other, source = placed(slot)
        to = slice(span + slot * BLK, span + (slot + 1) * BLK)
        k_all[to, :] = jnp.where(other == 1, far[source, k_cols], near[source, k_cols])
        v_all[to, :] = jnp.where(other == 1, far[source, v_cols], near[source, v_cols])
    at = 0
    for r in range(HEADS_PER_GROUP):
        for part in (own, *received):
            q_all[at : at + rows, :] = part[:rows, r * width : (r + 1) * width]
            g_all[at : at + rows, :] = part[rows:, r * width : (r + 1) * width]
            at += rows

    keys = k_all[...]
    values = v_all[...]
    keys_t = keys.T
    values_t = values.T
    biases = [
        jnp.where(listed[position, slot] >= 0, 0.0, NEG_FILL).astype(jnp.float32)
        for slot in range(slots)
    ]
    cuts = list(range(0, at - SLICE_ROWS + 1, SLICE_ROWS)) + [at]
    slices = [slice(low, high) for low, high in zip(cuts, cuts[1:])]

    def products(piece):
        query, upstream = q_all[piece, :], g_all[piece, :]
        return query, upstream, dot(keys, query, (1, 1)), dot(values, upstream, (1, 1))

    def softmax(scores, dprob):
        scores = scores * (SCALE * LOG2E)
        pieces = [scores[:span]]
        for slot in range(slots):
            low = span + slot * BLK
            pieces.append(scores[low : low + BLK] + biases[slot])
        scores = jnp.concatenate(pieces, 0)
        top = jnp.max(scores, 0, keepdims=True)
        unscaled = jnp.exp2(scores - top)
        prob = unscaled * (1.0 / jnp.sum(unscaled, 0, keepdims=True))
        row_dot = jnp.sum(prob * dprob, 0, keepdims=True)
        return prob.astype(jnp.bfloat16), (prob * (dprob - row_dot)).astype(jnp.bfloat16)

    gk = jnp.zeros((total, width), jnp.float32)
    gv = jnp.zeros((total, width), jnp.float32)
    ahead = products(slices[0])
    for index, piece in enumerate(slices):
        query, upstream, scores, dprob = ahead
        if index + 1 < len(slices):
            ahead = products(slices[index + 1])
        weights, dscore = softmax(scores, dprob)
        o_out[piece, :] = dot(values_t, weights, (1, 0)).astype(jnp.bfloat16).T
        gq_out[piece, :] = (dot(keys_t, dscore, (1, 0)) * SCALE).astype(jnp.bfloat16).T
        gk = gk + dot(dscore, query, (1, 0))
        gv = gv + dot(weights, upstream, (1, 0))
    at = 0
    for r in range(HEADS_PER_GROUP):
        to = slice(r * width, (r + 1) * width)
        for part in (None, *sends):
            attended, gq = o_out[at : at + rows, :], gq_out[at : at + rows, :]
            if part is None:
                o_own[:, to] = attended
                gq_own[:, to] = gq
            else:
                part[:rows, to] = attended
                part[rows:, to] = gq
            at += rows
    start = (head * (KEY_VALUE_HEADS // head_count) + place[2]) * GROUP_WIDTH
    target = lanes(start, GROUP_WIDTH)
    copies = [
        pltpu.make_async_copy(o_own, o_all.at[:, target], copied.at[0]),
        pltpu.make_async_copy(gq_own, gq_all.at[:, target], copied.at[1]),
    ]
    for copy in copies:
        copy.start()
    gk = (gk * SCALE).astype(jnp.bfloat16)
    gv = gv.astype(jnp.bfloat16)
    for index, grad in enumerate((near_grad, far_grad)):
        here = slice(index * group_rows, (index + 1) * group_rows)
        grad[:group_rows, k_cols] = gk[here]
        grad[:group_rows, v_cols] = gv[here]
        rest = grad.shape[0] - group_rows
        grad[group_rows:, k_cols] = jnp.zeros((rest, width), jnp.bfloat16)
        grad[group_rows:, v_cols] = jnp.zeros((rest, width), jnp.bfloat16)
    for slot in range(slots):
        other, target = placed(slot)
        low = span + slot * BLK
        for index, grad in enumerate((near_grad, far_grad)):

            @pl.when(jnp.logical_and(listed[position, slot] >= 0, other == index))
            def _():
                grad[target, k_cols] = gk[low : low + BLK]
                grad[target, v_cols] = gv[low : low + BLK]

    for copy in copies:
        copy.wait()


def attention(listed, place, own, received, near, far, carried, shape, column):
    head_count, group_rows, store_rows, clean_rows, slots = shape
    rows = own.shape[0] // 2
    total = 2 * group_rows + slots * BLK
    stacked = HEADS_PER_GROUP * group_rows
    smem = pl.BlockSpec(memory_space=pltpu.SMEM)
    vmem = pl.BlockSpec(memory_space=pltpu.VMEM)
    hbm = pl.BlockSpec(memory_space=pl.ANY)
    kept = [i for i, array in enumerate(carried) if not isinstance(array, jax.ShapeDtypeStruct)]
    first_carried = 3 + len(received) + 2
    spaces = [hbm, hbm] + [vmem] * (len(carried) - 2)
    return pl.pallas_call(
        functools.partial(attention_kernel, shape, column, len(kept)),
        in_specs=[smem, smem] + [vmem] * (3 + len(received)) + [spaces[i] for i in kept],
        out_specs=spaces,
        scratch_shapes=[pltpu.VMEM((total, HEAD_SIZE), jnp.bfloat16)] * 2
        + [pltpu.VMEM((stacked, HEAD_SIZE), jnp.bfloat16)] * 4
        + [pltpu.VMEM((rows, GROUP_WIDTH), jnp.bfloat16)] * 2
        + [pltpu.SemaphoreType.DMA((2,))],
        out_shape=[jax.ShapeDtypeStruct(array.shape, jnp.bfloat16) for array in carried],
        input_output_aliases={first_carried + n: i for n, i in enumerate(kept)},
        compiler_params=pltpu.CompilerParams(vmem_limit_bytes=KERNEL_VMEM),
        cost_estimate=pl.CostEstimate(
            flops=8 * group_rows * HEADS_PER_GROUP * HEAD_SIZE * total,
            bytes_accessed=16 * group_rows * GROUP_WIDTH,
            transcendentals=group_rows * HEADS_PER_GROUP * total,
        ),
        name="span_attention",
    )(listed, place, own, *received, near, far, *[carried[i] for i in kept])


def unpack_kernel(head_count, groups, *refs):
    parts, outs = refs[:-4], refs[-4:]
    rows = outs[0].shape[0]
    half = outs[0].shape[1] // head_count
    width = HEAD_SIZE
    for step in range(head_count):
        source = lax.rem(lax.axis_index("head") + step, head_count)
        for group, members in enumerate(groups):
            part = parts[group * head_count + step]
            for at, member in enumerate(members):
                to = lanes(source * half + member * width, width)
                for index in range(2):
                    here = slice((2 * at + index) * width, (2 * at + index + 1) * width)
                    outs[index][:, to] = part[:rows, here]
                    outs[2 + index][:, to] = part[rows:, here]


def unpacked(head_count, groups, grads, rows, clean_rows):
    vmem = pl.BlockSpec(memory_space=pltpu.VMEM)
    parts = [part for chunk in grads for part in chunk]
    width = KEY_VALUE_HEADS * HEAD_SIZE
    return pl.pallas_call(
        functools.partial(unpack_kernel, head_count, groups),
        in_specs=[vmem] * len(parts),
        out_specs=[vmem] * 4,
        out_shape=[jax.ShapeDtypeStruct((rows, width), jnp.bfloat16)] * 2
        + [jax.ShapeDtypeStruct((clean_rows, width), jnp.bfloat16)] * 2,
        name="unpack_gradients",
    )(*parts)


def shards(
    queries,
    noisy_token_keys,
    noisy_token_values,
    clean_token_keys,
    clean_token_values,
    output_gradient,
    history_list,
):
    ctx_count = lax.axis_size("ctx")
    head_count = lax.axis_size("head")
    head = lax.axis_index("head")
    place = jnp.stack([lax.axis_index("ctx"), head]).astype(jnp.int32)
    rows = queries.shape[0]
    clean_rows = clean_token_keys.shape[0]
    store_rows = clean_rows * head_count
    group_rows = rows * head_count
    slots = ctx_count - 2
    per_device = KEY_VALUE_HEADS // head_count
    everything = list(range(per_device))
    half = max(1, per_device // 2)
    key_groups = [g for g in (everything[:half], everything[half:]) if g]
    grad_groups = key_groups
    ask_groups = send_groups = [[m] for m in everything]
    top = ctx_count.bit_length() - 2
    steps = range(1, head_count)
    row_order = lax.rem(head - jnp.arange(head_count, dtype=jnp.int32) + head_count, head_count)

    def by_block(store):
        if clean_rows >= BLK:
            return store
        return store.reshape(head_count, clean_rows, -1)[row_order].reshape(store.shape)

    packs = packed(
        head_count,
        key_groups,
        noisy_token_keys,
        noisy_token_values,
        clean_token_keys,
        clean_token_values,
    )

    wide = [(queries, output_gradient)]

    def own_columns(array, member, step):
        start = (lax.rem(head + step, head_count) * per_device + member) * GROUP_WIDTH
        return lax.dynamic_slice_in_dim(array, start, GROUP_WIDTH, 1)

    def swap_keys(index):
        return [packs[index][0]] + [shifted(packs[index][step], step) for step in steps]

    def query_block(member, step):
        return jnp.concatenate(
            [own_columns(array, member, step) for array in wide[-1]], 0
        )

    def asked(member):
        return [query_block(member, step) for step in range(head_count)]

    asks = [asked(0)]

    def swap_queries(member):
        return [shifted(asks[member][step], step) for step in steps]

    def stored(parts):
        return by_block(jnp.concatenate([part[rows:] for part in parts], 0))

    def doubled(line, bit):
        return jnp.concatenate([line, flipped(line, 1 << bit)], 0)

    def joined(parts, line):
        return jnp.concatenate([part[:rows] for part in parts] + [line], 0)

    def summed(near_grad, from_core):
        total = near_grad.astype(jnp.float32) + from_core.astype(jnp.float32)
        return total[:group_rows], total[group_rows:]

    def halved(line, bit):
        middle = line.shape[0] // 2
        return line[:middle], flipped(line[middle:].astype(jnp.bfloat16), 1 << bit)

    together = lax.optimization_barrier
    def swap_heads(noisy_sum, store_sum):
        if clean_rows < BLK:
            store_sum = store_sum.reshape(head_count, clean_rows, -1)[row_order].reshape(
                store_sum.shape
            )
        store_sum = store_sum.astype(jnp.bfloat16)
        noisy_sum = noisy_sum.astype(jnp.bfloat16)
        mixed = [
            jnp.concatenate(
                [
                    noisy_sum[step * rows : (step + 1) * rows],
                    store_sum[step * clean_rows : (step + 1) * clean_rows],
                ],
                0,
            )
            for step in range(head_count)
        ]
        return [mixed[0]] + [shifted(mixed[step], -step) for step in steps]

    shape = (head_count, group_rows, store_rows, clean_rows, slots)
    received = {}
    two = len(key_groups) > 1
    parts = swap_keys(0)
    line = stored(parts)
    if two:
        packs[1], parts, later_wide = together((packs[1], parts, wide[-1]))
        wide.append(later_wide)
        asks.append(asked(1))
        later_parts = swap_keys(1)
    for bit in range(top, 0, -1):
        other = flipped(line, 1 << bit)
        if two and bit == top:
            other, asks[0] = together((other, asks[0]))
            received[0] = swap_queries(0)
        elif two and bit == top - 1:
            other, later_parts, later_wide = together((other, later_parts, wide[-1]))
            wide.append(later_wide)
            asks.extend(asked(member) for member in everything[2:])
            later_line = stored(later_parts)
            later_other = flipped(later_line, 1 << top)
        elif two:
            other, later_other = together((other, later_other))
            later_line = jnp.concatenate([later_line, later_other], 0)
            later_other = flipped(later_line, 1 << (bit + 1))
        if two and bit == 2:
            other, asks[1], received[0] = together((other, asks[1], received[0]))
            received[1] = swap_queries(1)
        line = jnp.concatenate([line, other], 0)
    near = joined(parts, line)
    if two:
        near, asks[2], received[1] = together((near, asks[2], received[1]))
        received[2] = swap_queries(2)
    else:
        received[0] = swap_queries(0)
    keys = {0: (near, flipped(near, 1))}
    outputs = [jax.ShapeDtypeStruct(queries.shape, jnp.bfloat16)] * 2
    sent = []
    held = []
    waiting = []

    def group_of(groups, member):
        return next(i for i, group in enumerate(groups) if member in group)

    for member in everything:
        k = group_of(key_groups, member)
        first = member == key_groups[k][0]
        last = member == key_groups[k][-1]
        sends = [jax.ShapeDtypeStruct((2 * rows, GROUP_WIDTH), jnp.bfloat16)] * (head_count - 1)
        if first:
            width = len(key_groups[k]) * 2 * HEAD_SIZE
            pair = [jax.ShapeDtypeStruct((near.shape[0], width), jnp.bfloat16)] * 2
        column = key_groups[k].index(member)
        outputs[0], outputs[1], *rest = attention(
            history_list,
            jnp.concatenate([place, jnp.array([member], jnp.int32)]),
            asks[member][0],
            received[member],
            *keys[k],
            [*outputs, *sends, *pair],
            shape,
            column,
        )
        sends, pair = rest[:-2], rest[-2:]
        if two and member == 0:
            outputs, later_other, received[2] = together((outputs, later_other, received[2]))
            later_line = jnp.concatenate([later_line, later_other], 0)
            crossing = flipped(later_line, 2)
        if two and member == 1:
            outputs, crossing = together((outputs, crossing))
            near = joined(later_parts, jnp.concatenate([later_line, crossing], 0))
            keys[1] = (near, flipped(near, 1))
        if member + 3 < per_device:
            asks, outputs = together((asks, outputs))
            received[member + 3] = swap_queries(member + 3)
        if two and member + 2 == everything[-1]:
            pair, received[member + 2] = together((pair, received[member + 2]))
        held.append(sends)
        if two and member == half:
            held[half - 1], outputs = together((held[half - 1], outputs))
        if not two or member >= half - 1:
            later = len(held) if member == everything[-1] else len(held) - 1
            for block_set in held[len(sent) : later]:
                sent.append([shifted(block, -step) for step, block in zip(steps, block_set)])
        if waiting and not last:
            noisy_sum, line = summed(*waiting[0])
            line, outputs, sent[0] = together((line, outputs, sent[0]))
            waiting[0] = (noisy_sum, *halved(line, 1))
        if last:
            if waiting:
                waiting[0], pair, sent[:half] = together((waiting[0], pair, sent[:half]))
            waiting.append((pair[0], flipped(pair[1], 1)))
    grads = []
    noisy_sum, line = summed(*waiting[-1])
    if two:
        first_noisy, keep, other = waiting[0]
        for bit in range(2, top + 1):
            keep, other = halved(keep + other.astype(jnp.float32), bit)
    for bit in range(1, top + 1):
        last_keep, last_other = halved(line, bit)
        if two and bit == 1:
            last_other, other, sent[:half] = together((last_other, other, sent[:half]))
            grads.append(swap_heads(first_noisy, keep + other.astype(jnp.float32)))
        line = last_keep + last_other.astype(jnp.float32)
    if two:
        line, sent[half:] = together((line, sent[half:]))
    grads.append(swap_heads(noisy_sum, line))
    attended, query_grad = outputs
    for group, blocks in zip(send_groups, sent):
        for step, block in zip(steps, blocks):
            source = lax.rem(head + step, head_count)
            start = (source * per_device + group[0]) * GROUP_WIDTH
            attended = lax.dynamic_update_slice_in_dim(attended, block[:rows], start, 1)
            query_grad = lax.dynamic_update_slice_in_dim(query_grad, block[rows:], start, 1)
    finished = unpacked(head_count, grad_groups, grads, rows, clean_rows)
    return (attended, query_grad, *finished)


def solution(mesh):
    split = P(("ctx", "head"), None)
    return jax.shard_map(
        shards,
        mesh=mesh,
        in_specs=(split, split, split, split, split, split, P()),
        out_specs=(split,) * 6,
        check_vma=False,
    )
```

```python
import functools

import jax
import jax.numpy as jnp
from jax import lax
from jax.experimental import pallas as pl
from jax.experimental.pallas import tpu as pltpu
from jax.sharding import PartitionSpec as P

QUERY_HEADS = 48
KEY_VALUE_HEADS = 8
HEAD_SIZE = 128
BLK = 32
HEADS_PER_GROUP = QUERY_HEADS // KEY_VALUE_HEADS
GROUP_WIDTH = HEADS_PER_GROUP * HEAD_SIZE
SCALE = HEAD_SIZE**-0.5
LOG2E = 1.4426950408889634

NEG_FILL = -1e30
SLICE_ROWS = 256
KERNEL_VMEM = 32 * 2**20


def flipped(block, bits):
    count = lax.axis_size("ctx")
    return lax.ppermute(block, "ctx", [(i, i ^ bits) for i in range(count)])


def shifted(block, step):
    count = lax.axis_size("head")
    return lax.ppermute(block, "head", [(i, (i + step) % count) for i in range(count)])


def dot(a, b, contract):
    return lax.dot_general(
        a, b, ((contract[:1], contract[1:]), ((), ())), preferred_element_type=jnp.float32
    )


def lanes(start, size):
    return pl.ds(pl.multiple_of(start, HEAD_SIZE), size)


def pack_kernel(head_count, groups, k_noisy, v_noisy, k_clean, v_clean, *outs):
    rows = k_noisy.shape[0]
    half = k_noisy.shape[1] // head_count
    width = HEAD_SIZE
    for index, group in enumerate(groups):
        for step in range(head_count):
            out = outs[index * head_count + step]
            target = lax.rem(lax.axis_index("head") + step, head_count)
            for at, member in enumerate(group):
                source = lanes(target * half + member * width, width)
                for n, (noisy, clean) in enumerate(((k_noisy, k_clean), (v_noisy, v_clean))):
                    to = slice((2 * at + n) * width, (2 * at + n + 1) * width)
                    out[:rows, to] = noisy[:, source]
                    out[rows:, to] = clean[:, source]


def packed(head_count, groups, k_noisy, v_noisy, k_clean, v_clean):
    vmem = pl.BlockSpec(memory_space=pltpu.VMEM)
    rows = k_noisy.shape[0] + k_clean.shape[0]
    shapes = [
        jax.ShapeDtypeStruct((rows, 2 * HEAD_SIZE * len(group)), jnp.bfloat16)
        for group in groups
        for _ in range(head_count)
    ]
    outs = pl.pallas_call(
        functools.partial(pack_kernel, head_count, groups),
        in_specs=[vmem] * 4,
        out_specs=[vmem] * len(shapes),
        out_shape=shapes,
        name="pack_keys_values",
    )(k_noisy, v_noisy, k_clean, v_clean)
    return [outs[i * head_count : (i + 1) * head_count] for i in range(len(groups))]


def stack_kernel(head_count, q, g, *outs):
    rows = q.shape[0]
    per_device = KEY_VALUE_HEADS // head_count
    for member in range(per_device):
        for step in range(head_count):
            out = outs[member * head_count + step]
            target = lax.rem(lax.axis_index("head") + step, head_count)
            source = lanes((target * per_device + member) * GROUP_WIDTH, GROUP_WIDTH)
            out[:rows, :] = q[:, source]
            out[rows:, :] = g[:, source]


def query_blocks(head_count, q, g):
    vmem = pl.BlockSpec(memory_space=pltpu.VMEM)
    shape = jax.ShapeDtypeStruct((2 * q.shape[0], GROUP_WIDTH), jnp.bfloat16)
    outs = pl.pallas_call(
        functools.partial(stack_kernel, head_count),
        in_specs=[vmem] * 2,
        out_specs=[vmem] * KEY_VALUE_HEADS,
        out_shape=[shape] * KEY_VALUE_HEADS,
        name="stack_queries",
    )(q, g)
    return [outs[i : i + head_count] for i in range(0, KEY_VALUE_HEADS, head_count)]


def attention_kernel(shape, column, kept, listed, place, own, *refs):
    head_count, group_rows, store_rows, clean_rows, slots = shape
    received, refs = refs[: head_count - 1], refs[head_count - 1 :]
    near, far, *refs = refs
    o_all, gq_all, *refs = refs[kept:]
    sends, refs = refs[: head_count - 1], refs[head_count - 1 :]
    near_grad, far_grad, k_all, v_all, q_all, g_all, o_out, gq_out, o_own, gq_own, copied = refs
    rows = own.shape[0] // 2
    width = HEAD_SIZE
    position, head = place[0], place[1]
    k_cols = slice(2 * column * width, (2 * column + 1) * width)
    v_cols = slice((2 * column + 1) * width, (2 * column + 2) * width)
    depth = (near.shape[0] - group_rows) // (2 * store_rows)

    def placed(slot):
        apart = lax.bitwise_xor(position, slot)
        store = lax.bitwise_and(lax.shift_right_logical(apart, 1), 1) * depth
        store = store + lax.shift_right_logical(apart, 2)
        block = jnp.maximum(listed[position, slot], 0)
        if clean_rows >= BLK:
            owner = lax.div(block * BLK, clean_rows)
            step = lax.rem(head - owner + head_count, head_count)
            inside = step * clean_rows + block * BLK - owner * clean_rows
        else:
            inside = block * BLK
        start = pl.multiple_of(group_rows + store * store_rows + inside, BLK)
        return lax.bitwise_and(apart, 1), pl.ds(start, BLK)

    k_all[:group_rows, :] = near[:group_rows, k_cols]
    v_all[:group_rows, :] = near[:group_rows, v_cols]
    k_all[group_rows : 2 * group_rows, :] = far[:group_rows, k_cols]
    v_all[group_rows : 2 * group_rows, :] = far[:group_rows, v_cols]
    span = 2 * group_rows
    total = span + slots * BLK
    for slot in range(slots):
        other, source = placed(slot)
        to = slice(span + slot * BLK, span + (slot + 1) * BLK)
        k_all[to, :] = jnp.where(other == 1, far[source, k_cols], near[source, k_cols])
        v_all[to, :] = jnp.where(other == 1, far[source, v_cols], near[source, v_cols])
    at = 0
    for r in range(HEADS_PER_GROUP):
        for part in (own, *received):
            q_all[at : at + rows, :] = part[:rows, r * width : (r + 1) * width]
            g_all[at : at + rows, :] = part[rows:, r * width : (r + 1) * width]
            at += rows

    keys = k_all[...]
    values = v_all[...]
    keys_t = keys.T
    values_t = values.T
    biases = [
        jnp.where(listed[position, slot] >= 0, 0.0, NEG_FILL).astype(jnp.float32)
        for slot in range(slots)
    ]
    cuts = list(range(0, at - SLICE_ROWS + 1, SLICE_ROWS)) + [at]
    slices = [slice(low, high) for low, high in zip(cuts, cuts[1:])]

    def products(piece):
        query, upstream = q_all[piece, :], g_all[piece, :]
        return query, upstream, dot(keys, query, (1, 1)), dot(values, upstream, (1, 1))

    def softmax(scores, dprob):
        scores = scores * (SCALE * LOG2E)
        pieces = [scores[:span]]
        for slot in range(slots):
            low = span + slot * BLK
            pieces.append(scores[low : low + BLK] + biases[slot])
        scores = jnp.concatenate(pieces, 0)
        top = jnp.max(scores, 0, keepdims=True)
        unscaled = jnp.exp2(scores - top)
        prob = unscaled * (1.0 / jnp.sum(unscaled, 0, keepdims=True))
        row_dot = jnp.sum(prob * dprob, 0, keepdims=True)
        return prob.astype(jnp.bfloat16), (prob * (dprob - row_dot)).astype(jnp.bfloat16)

    gk = jnp.zeros((total, width), jnp.float32)
    gv = jnp.zeros((total, width), jnp.float32)
    ahead = products(slices[0])
    for index, piece in enumerate(slices):
        query, upstream, scores, dprob = ahead
        if index + 1 < len(slices):
            ahead = products(slices[index + 1])
        weights, dscore = softmax(scores, dprob)
        o_out[piece, :] = dot(values_t, weights, (1, 0)).astype(jnp.bfloat16).T
        gq_out[piece, :] = (dot(keys_t, dscore, (1, 0)) * SCALE).astype(jnp.bfloat16).T
        gk = gk + dot(dscore, query, (1, 0))
        gv = gv + dot(weights, upstream, (1, 0))
    at = 0
    for r in range(HEADS_PER_GROUP):
        to = slice(r * width, (r + 1) * width)
        for part in (None, *sends):
            attended, gq = o_out[at : at + rows, :], gq_out[at : at + rows, :]
            if part is None:
                o_own[:, to] = attended
                gq_own[:, to] = gq
            else:
                part[:rows, to] = attended
                part[rows:, to] = gq
            at += rows
    start = (head * (KEY_VALUE_HEADS // head_count) + place[2]) * GROUP_WIDTH
    target = lanes(start, GROUP_WIDTH)
    copies = [
        pltpu.make_async_copy(o_own, o_all.at[:, target], copied.at[0]),
        pltpu.make_async_copy(gq_own, gq_all.at[:, target], copied.at[1]),
    ]
    for copy in copies:
        copy.start()
    gk = (gk * SCALE).astype(jnp.bfloat16)
    gv = gv.astype(jnp.bfloat16)
    for index, grad in enumerate((near_grad, far_grad)):
        here = slice(index * group_rows, (index + 1) * group_rows)
        grad[:group_rows, k_cols] = gk[here]
        grad[:group_rows, v_cols] = gv[here]
        rest = grad.shape[0] - group_rows
        grad[group_rows:, k_cols] = jnp.zeros((rest, width), jnp.bfloat16)
        grad[group_rows:, v_cols] = jnp.zeros((rest, width), jnp.bfloat16)
    for slot in range(slots):
        other, target = placed(slot)
        low = span + slot * BLK
        for index, grad in enumerate((near_grad, far_grad)):

            @pl.when(jnp.logical_and(listed[position, slot] >= 0, other == index))
            def _():
                grad[target, k_cols] = gk[low : low + BLK]
                grad[target, v_cols] = gv[low : low + BLK]

    for copy in copies:
        copy.wait()


def attention(listed, place, own, received, near, far, carried, shape, column):
    head_count, group_rows, store_rows, clean_rows, slots = shape
    rows = own.shape[0] // 2
    total = 2 * group_rows + slots * BLK
    stacked = HEADS_PER_GROUP * group_rows
    smem = pl.BlockSpec(memory_space=pltpu.SMEM)
    vmem = pl.BlockSpec(memory_space=pltpu.VMEM)
    hbm = pl.BlockSpec(memory_space=pl.ANY)
    kept = [i for i, array in enumerate(carried) if not isinstance(array, jax.ShapeDtypeStruct)]
    first_carried = 3 + len(received) + 2
    spaces = [hbm, hbm] + [vmem] * (len(carried) - 2)
    return pl.pallas_call(
        functools.partial(attention_kernel, shape, column, len(kept)),
        in_specs=[smem, smem] + [vmem] * (3 + len(received)) + [spaces[i] for i in kept],
        out_specs=spaces,
        scratch_shapes=[pltpu.VMEM((total, HEAD_SIZE), jnp.bfloat16)] * 2
        + [pltpu.VMEM((stacked, HEAD_SIZE), jnp.bfloat16)] * 4
        + [pltpu.VMEM((rows, GROUP_WIDTH), jnp.bfloat16)] * 2
        + [pltpu.SemaphoreType.DMA((2,))],
        out_shape=[jax.ShapeDtypeStruct(array.shape, jnp.bfloat16) for array in carried],
        input_output_aliases={first_carried + n: i for n, i in enumerate(kept)},
        compiler_params=pltpu.CompilerParams(vmem_limit_bytes=KERNEL_VMEM),
        cost_estimate=pl.CostEstimate(
            flops=8 * group_rows * HEADS_PER_GROUP * HEAD_SIZE * total,
            bytes_accessed=16 * group_rows * GROUP_WIDTH,
            transcendentals=group_rows * HEADS_PER_GROUP * total,
        ),
        name="span_attention",
    )(listed, place, own, *received, near, far, *[carried[i] for i in kept])


def unpack_kernel(head_count, groups, *refs):
    parts, outs = refs[:-4], refs[-4:]
    rows = outs[0].shape[0]
    half = outs[0].shape[1] // head_count
    width = HEAD_SIZE
    for step in range(head_count):
        source = lax.rem(lax.axis_index("head") + step, head_count)
        for group, members in enumerate(groups):
            part = parts[group * head_count + step]
            for at, member in enumerate(members):
                to = lanes(source * half + member * width, width)
                for index in range(2):
                    here = slice((2 * at + index) * width, (2 * at + index + 1) * width)
                    outs[index][:, to] = part[:rows, here]
                    outs[2 + index][:, to] = part[rows:, here]


def unpacked(head_count, groups, grads, rows, clean_rows):
    vmem = pl.BlockSpec(memory_space=pltpu.VMEM)
    parts = [part for chunk in grads for part in chunk]
    width = KEY_VALUE_HEADS * HEAD_SIZE
    return pl.pallas_call(
        functools.partial(unpack_kernel, head_count, groups),
        in_specs=[vmem] * len(parts),
        out_specs=[vmem] * 4,
        out_shape=[jax.ShapeDtypeStruct((rows, width), jnp.bfloat16)] * 2
        + [jax.ShapeDtypeStruct((clean_rows, width), jnp.bfloat16)] * 2,
        name="unpack_gradients",
    )(*parts)


def shards(
    queries,
    noisy_token_keys,
    noisy_token_values,
    clean_token_keys,
    clean_token_values,
    output_gradient,
    history_list,
):
    ctx_count = lax.axis_size("ctx")
    head_count = lax.axis_size("head")
    head = lax.axis_index("head")
    place = jnp.stack([lax.axis_index("ctx"), head]).astype(jnp.int32)
    rows = queries.shape[0]
    clean_rows = clean_token_keys.shape[0]
    store_rows = clean_rows * head_count
    group_rows = rows * head_count
    slots = ctx_count - 2
    per_device = KEY_VALUE_HEADS // head_count
    everything = list(range(per_device))
    half = max(1, per_device // 2)
    key_groups = [g for g in (everything[:half], everything[half:]) if g]
    grad_groups = key_groups
    ask_groups = send_groups = [[m] for m in everything]
    depth = ctx_count // 4
    steps = range(1, head_count)
    row_order = lax.rem(head - jnp.arange(head_count, dtype=jnp.int32) + head_count, head_count)

    def by_block(store):
        if clean_rows >= BLK:
            return store
        return store.reshape(head_count, clean_rows, -1)[row_order].reshape(store.shape)

    packs = packed(
        head_count,
        key_groups,
        noisy_token_keys,
        noisy_token_values,
        clean_token_keys,
        clean_token_values,
    )

    asks = query_blocks(head_count, queries, output_gradient)

    def swap_keys(index):
        return [packs[index][0]] + [shifted(packs[index][step], step) for step in steps]

    def swap_queries(member):
        return [shifted(asks[member][step], step) for step in steps]

    def stored(parts):
        return by_block(jnp.concatenate([part[rows:] for part in parts], 0))

    def along(store):
        return [flipped(store, z << 2) for z in range(1, depth)]

    def joined(parts, line):
        return jnp.concatenate([part[:rows] for part in parts] + [line], 0)

    def summed(near_grad, from_core):
        total = near_grad.astype(jnp.float32) + from_core.astype(jnp.float32)
        return total[:group_rows], total[group_rows:]

    def halved(line):
        middle = line.shape[0] // 2
        return line[:middle], flipped(line[middle:].astype(jnp.bfloat16), 2)

    def back_along(line):
        gives = [line[z * store_rows : (z + 1) * store_rows] for z in range(depth)]
        return gives[0], [
            flipped(give.astype(jnp.bfloat16), z << 2) for z, give in enumerate(gives[1:], 1)
        ]

    def added(keep, others):
        for other in others:
            keep = keep + other.astype(jnp.float32)
        return keep

    together = lax.optimization_barrier
    def swap_heads(noisy_sum, store_sum):
        if clean_rows < BLK:
            store_sum = store_sum.reshape(head_count, clean_rows, -1)[row_order].reshape(
                store_sum.shape
            )
        store_sum = store_sum.astype(jnp.bfloat16)
        noisy_sum = noisy_sum.astype(jnp.bfloat16)
        mixed = [
            jnp.concatenate(
                [
                    noisy_sum[step * rows : (step + 1) * rows],
                    store_sum[step * clean_rows : (step + 1) * clean_rows],
                ],
                0,
            )
            for step in range(head_count)
        ]
        return [mixed[0]] + [shifted(mixed[step], -step) for step in steps]

    shape = (head_count, group_rows, store_rows, clean_rows, slots)
    received = {}
    two = len(key_groups) > 1
    parts = swap_keys(0)
    store = stored(parts)
    others = along(store)
    if two:
        packs[1], asks[0], parts = together((packs[1], asks[0], parts))
        later_parts = swap_keys(1)
    received[0] = swap_queries(0)
    line = jnp.concatenate([store, *others], 0)
    crossing = flipped(line, 2)
    if two:
        asks[1], received[0], others = together((asks[1], received[0], others))
        received[1] = swap_queries(1)
        crossing, later_parts = together((crossing, later_parts))
        later_store = stored(later_parts)
        later_others = along(later_store)
    near = joined(parts, jnp.concatenate([line, crossing], 0))
    if two:
        near, asks[2], received[1] = together((near, asks[2], received[1]))
        received[2] = swap_queries(2)
    keys = {0: (near, flipped(near, 1))}
    outputs = [jax.ShapeDtypeStruct(queries.shape, jnp.bfloat16)] * 2
    sent = []
    held = []
    waiting = []

    def group_of(groups, member):
        return next(i for i, group in enumerate(groups) if member in group)

    for member in everything:
        k = group_of(key_groups, member)
        first = member == key_groups[k][0]
        last = member == key_groups[k][-1]
        sends = [jax.ShapeDtypeStruct((2 * rows, GROUP_WIDTH), jnp.bfloat16)] * (head_count - 1)
        if first:
            width = len(key_groups[k]) * 2 * HEAD_SIZE
            pair = [jax.ShapeDtypeStruct((near.shape[0], width), jnp.bfloat16)] * 2
        column = key_groups[k].index(member)
        outputs[0], outputs[1], *rest = attention(
            history_list,
            jnp.concatenate([place, jnp.array([member], jnp.int32)]),
            asks[member][0],
            received[member],
            *keys[k],
            [*outputs, *sends, *pair],
            shape,
            column,
        )
        sends, pair = rest[:-2], rest[-2:]
        if two and member == 0:
            outputs, later_others, received[2] = together((outputs, later_others, received[2]))
            later_line = jnp.concatenate([later_store, *later_others], 0)
            crossing = flipped(later_line, 2)
        if two and member == 1:
            outputs, crossing = together((outputs, crossing))
            near = joined(later_parts, jnp.concatenate([later_line, crossing], 0))
            keys[1] = (near, flipped(near, 1))
        if member + 3 < per_device:
            asks, outputs = together((asks, outputs))
            received[member + 3] = swap_queries(member + 3)
        if two and member + 2 == everything[-1]:
            pair, received[member + 2] = together((pair, received[member + 2]))
        held.append(sends)
        if two and member == half:
            held[half - 1], outputs = together((held[half - 1], outputs))
        if not two or member >= half - 1:
            later = len(held) if member == everything[-1] else len(held) - 1
            for block_set in held[len(sent) : later]:
                sent.append([shifted(block, -step) for step, block in zip(steps, block_set)])
        if waiting and not last:
            noisy_sum, line = summed(*waiting[0])
            line, outputs, sent[0] = together((line, outputs, sent[0]))
            waiting[0] = (noisy_sum, *halved(line))
        if last:
            if waiting:
                waiting[0], pair, sent[:half] = together((waiting[0], pair, sent[:half]))
            waiting.append((pair[0], flipped(pair[1], 1)))
    grads = []
    if two:
        first_noisy, keep, other = waiting[0]
        keep, others = back_along(added(keep, [other]))
    noisy_sum, line = summed(*waiting[-1])
    last_keep, last_other = halved(line)
    if two:
        last_other, others, sent[:half] = together((last_other, others, sent[:half]))
        grads.append(swap_heads(first_noisy, added(keep, others)))
    last_keep, last_others = back_along(added(last_keep, [last_other]))
    line = added(last_keep, last_others)
    if two:
        line, sent[half:] = together((line, sent[half:]))
    grads.append(swap_heads(noisy_sum, line))
    attended, query_grad = outputs
    for group, blocks in zip(send_groups, sent):
        for step, block in zip(steps, blocks):
            source = lax.rem(head + step, head_count)
            start = (source * per_device + group[0]) * GROUP_WIDTH
            attended = lax.dynamic_update_slice_in_dim(attended, block[:rows], start, 1)
            query_grad = lax.dynamic_update_slice_in_dim(query_grad, block[rows:], start, 1)
    finished = unpacked(head_count, grad_groups, grads, rows, clean_rows)
    return (attended, query_grad, *finished)


def solution(mesh):
    split = P(("ctx", "head"), None)
    return jax.shard_map(
        shards,
        mesh=mesh,
        in_specs=(split, split, split, split, split, split, P()),
        out_specs=(split,) * 6,
        check_vma=False,
    )
```

```python
import functools

import jax
import jax.numpy as jnp
from jax import lax
from jax.experimental import pallas as pl
from jax.experimental.pallas import tpu as pltpu
from jax.sharding import PartitionSpec as P

QUERY_HEADS = 48
KEY_VALUE_HEADS = 8
HEAD_SIZE = 128
BLK = 32
HEADS_PER_GROUP = QUERY_HEADS // KEY_VALUE_HEADS
GROUP_WIDTH = HEADS_PER_GROUP * HEAD_SIZE
SCALE = HEAD_SIZE**-0.5
LOG2E = 1.4426950408889634

NEG_FILL = -1e30
SLICE_ROWS = 256
KERNEL_VMEM = 32 * 2**20


def flipped(block, bits):
    count = lax.axis_size("ctx")
    return lax.ppermute(block, "ctx", [(i, i ^ bits) for i in range(count)])


def shifted(block, step):
    count = lax.axis_size("head")
    return lax.ppermute(block, "head", [(i, (i + step) % count) for i in range(count)])


def dot(a, b, contract):
    return lax.dot_general(
        a, b, ((contract[:1], contract[1:]), ((), ())), preferred_element_type=jnp.float32
    )


def lanes(start, size):
    return pl.ds(pl.multiple_of(start, HEAD_SIZE), size)


def pack_kernel(head_count, groups, k_noisy, v_noisy, k_clean, v_clean, *outs):
    rows = k_noisy.shape[0]
    half = k_noisy.shape[1] // head_count
    width = HEAD_SIZE
    for index, group in enumerate(groups):
        for step in range(head_count):
            out = outs[index * head_count + step]
            target = lax.rem(lax.axis_index("head") + step, head_count)
            for at, member in enumerate(group):
                source = lanes(target * half + member * width, width)
                for n, (noisy, clean) in enumerate(((k_noisy, k_clean), (v_noisy, v_clean))):
                    to = slice((2 * at + n) * width, (2 * at + n + 1) * width)
                    out[:rows, to] = noisy[:, source]
                    out[rows:, to] = clean[:, source]


def packed(head_count, groups, k_noisy, v_noisy, k_clean, v_clean):
    vmem = pl.BlockSpec(memory_space=pltpu.VMEM)
    rows = k_noisy.shape[0] + k_clean.shape[0]
    shapes = [
        jax.ShapeDtypeStruct((rows, 2 * HEAD_SIZE * len(group)), jnp.bfloat16)
        for group in groups
        for _ in range(head_count)
    ]
    outs = pl.pallas_call(
        functools.partial(pack_kernel, head_count, groups),
        in_specs=[vmem] * 4,
        out_specs=[vmem] * len(shapes),
        out_shape=shapes,
        name="pack_keys_values",
    )(k_noisy, v_noisy, k_clean, v_clean)
    return [outs[i * head_count : (i + 1) * head_count] for i in range(len(groups))]


def stack_kernel(head_count, q, g, *outs):
    rows = q.shape[0]
    per_device = KEY_VALUE_HEADS // head_count
    for member in range(per_device):
        for step in range(head_count):
            out = outs[member * head_count + step]
            target = lax.rem(lax.axis_index("head") + step, head_count)
            source = lanes((target * per_device + member) * GROUP_WIDTH, GROUP_WIDTH)
            out[:rows, :] = q[:, source]
            out[rows:, :] = g[:, source]


def query_blocks(head_count, q, g):
    vmem = pl.BlockSpec(memory_space=pltpu.VMEM)
    shape = jax.ShapeDtypeStruct((2 * q.shape[0], GROUP_WIDTH), jnp.bfloat16)
    outs = pl.pallas_call(
        functools.partial(stack_kernel, head_count),
        in_specs=[vmem] * 2,
        out_specs=[vmem] * KEY_VALUE_HEADS,
        out_shape=[shape] * KEY_VALUE_HEADS,
        name="stack_queries",
    )(q, g)
    return [outs[i : i + head_count] for i in range(0, KEY_VALUE_HEADS, head_count)]


def attention_kernel(shape, column, kept, listed, place, own, *refs):
    head_count, group_rows, store_rows, clean_rows, slots = shape
    received, refs = refs[: head_count - 1], refs[head_count - 1 :]
    near, far, *refs = refs
    o_all, gq_all, *refs = refs[kept:]
    sends, refs = refs[: head_count - 1], refs[head_count - 1 :]
    near_grad, far_grad, k_all, v_all, q_all, g_all, o_out, gq_out, o_own, gq_own, copied = refs
    rows = own.shape[0] // 2
    width = HEAD_SIZE
    position, head = place[0], place[1]
    k_cols = slice(2 * column * width, (2 * column + 1) * width)
    v_cols = slice((2 * column + 1) * width, (2 * column + 2) * width)
    depth = (near.shape[0] - group_rows) // (2 * store_rows)

    def placed(slot):
        apart = lax.bitwise_xor(position, slot)
        store = lax.bitwise_and(lax.shift_right_logical(apart, 1), 1) * depth
        store = store + lax.shift_right_logical(apart, 2)
        block = jnp.maximum(listed[position, slot], 0)
        if clean_rows >= BLK:
            owner = lax.div(block * BLK, clean_rows)
            step = lax.rem(head - owner + head_count, head_count)
            inside = step * clean_rows + block * BLK - owner * clean_rows
        else:
            inside = block * BLK
        start = pl.multiple_of(group_rows + store * store_rows + inside, BLK)
        return lax.bitwise_and(apart, 1), pl.ds(start, BLK)

    k_all[:group_rows, :] = near[:group_rows, k_cols]
    v_all[:group_rows, :] = near[:group_rows, v_cols]
    k_all[group_rows : 2 * group_rows, :] = far[:group_rows, k_cols]
    v_all[group_rows : 2 * group_rows, :] = far[:group_rows, v_cols]
    span = 2 * group_rows
    total = span + slots * BLK
    for slot in range(slots):
        other, source = placed(slot)
        to = slice(span + slot * BLK, span + (slot + 1) * BLK)
        k_all[to, :] = jnp.where(other == 1, far[source, k_cols], near[source, k_cols])
        v_all[to, :] = jnp.where(other == 1, far[source, v_cols], near[source, v_cols])
    at = 0
    for r in range(HEADS_PER_GROUP):
        for part in (own, *received):
            q_all[at : at + rows, :] = part[:rows, r * width : (r + 1) * width]
            g_all[at : at + rows, :] = part[rows:, r * width : (r + 1) * width]
            at += rows

    keys = k_all[...]
    values = v_all[...]
    keys_t = keys.T
    values_t = values.T
    biases = [
        jnp.where(listed[position, slot] >= 0, 0.0, NEG_FILL).astype(jnp.float32)
        for slot in range(slots)
    ]
    cuts = list(range(0, at - SLICE_ROWS + 1, SLICE_ROWS)) + [at]
    slices = [slice(low, high) for low, high in zip(cuts, cuts[1:])]

    def products(piece):
        query, upstream = q_all[piece, :], g_all[piece, :]
        return query, upstream, dot(keys, query, (1, 1)), dot(values, upstream, (1, 1))

    def softmax(scores, dprob):
        scores = scores * (SCALE * LOG2E)
        pieces = [scores[:span]]
        for slot in range(slots):
            low = span + slot * BLK
            pieces.append(scores[low : low + BLK] + biases[slot])
        scores = jnp.concatenate(pieces, 0)
        top = jnp.max(scores, 0, keepdims=True)
        unscaled = jnp.exp2(scores - top)
        prob = unscaled * (1.0 / jnp.sum(unscaled, 0, keepdims=True))
        row_dot = jnp.sum(prob * dprob, 0, keepdims=True)
        return prob.astype(jnp.bfloat16), (prob * (dprob - row_dot)).astype(jnp.bfloat16)

    gk = jnp.zeros((total, width), jnp.float32)
    gv = jnp.zeros((total, width), jnp.float32)
    ahead = products(slices[0])
    for index, piece in enumerate(slices):
        query, upstream, scores, dprob = ahead
        if index + 1 < len(slices):
            ahead = products(slices[index + 1])
        weights, dscore = softmax(scores, dprob)
        o_out[piece, :] = dot(values_t, weights, (1, 0)).astype(jnp.bfloat16).T
        gq_out[piece, :] = (dot(keys_t, dscore, (1, 0)) * SCALE).astype(jnp.bfloat16).T
        gk = gk + dot(dscore, query, (1, 0))
        gv = gv + dot(weights, upstream, (1, 0))
    at = 0
    for r in range(HEADS_PER_GROUP):
        to = slice(r * width, (r + 1) * width)
        for part in (None, *sends):
            attended, gq = o_out[at : at + rows, :], gq_out[at : at + rows, :]
            if part is None:
                o_own[:, to] = attended
                gq_own[:, to] = gq
            else:
                part[:rows, to] = attended
                part[rows:, to] = gq
            at += rows
    start = (head * (KEY_VALUE_HEADS // head_count) + place[2]) * GROUP_WIDTH
    target = lanes(start, GROUP_WIDTH)
    copies = [
        pltpu.make_async_copy(o_own, o_all.at[:, target], copied.at[0]),
        pltpu.make_async_copy(gq_own, gq_all.at[:, target], copied.at[1]),
    ]
    for copy in copies:
        copy.start()
    gk = (gk * SCALE).astype(jnp.bfloat16)
    gv = gv.astype(jnp.bfloat16)
    for index, grad in enumerate((near_grad, far_grad)):
        here = slice(index * group_rows, (index + 1) * group_rows)
        grad[:group_rows, k_cols] = gk[here]
        grad[:group_rows, v_cols] = gv[here]
        rest = grad.shape[0] - group_rows
        grad[group_rows:, k_cols] = jnp.zeros((rest, width), jnp.bfloat16)
        grad[group_rows:, v_cols] = jnp.zeros((rest, width), jnp.bfloat16)
    for slot in range(slots):
        other, target = placed(slot)
        low = span + slot * BLK
        for index, grad in enumerate((near_grad, far_grad)):

            @pl.when(jnp.logical_and(listed[position, slot] >= 0, other == index))
            def _():
                grad[target, k_cols] = gk[low : low + BLK]
                grad[target, v_cols] = gv[low : low + BLK]

    for copy in copies:
        copy.wait()


def attention(listed, place, own, received, near, far, carried, shape, column):
    head_count, group_rows, store_rows, clean_rows, slots = shape
    rows = own.shape[0] // 2
    total = 2 * group_rows + slots * BLK
    stacked = HEADS_PER_GROUP * group_rows
    smem = pl.BlockSpec(memory_space=pltpu.SMEM)
    vmem = pl.BlockSpec(memory_space=pltpu.VMEM)
    hbm = pl.BlockSpec(memory_space=pl.ANY)
    kept = [i for i, array in enumerate(carried) if not isinstance(array, jax.ShapeDtypeStruct)]
    first_carried = 3 + len(received) + 2
    spaces = [hbm, hbm] + [vmem] * (len(carried) - 2)
    return pl.pallas_call(
        functools.partial(attention_kernel, shape, column, len(kept)),
        in_specs=[smem, smem] + [vmem] * (3 + len(received)) + [spaces[i] for i in kept],
        out_specs=spaces,
        scratch_shapes=[pltpu.VMEM((total, HEAD_SIZE), jnp.bfloat16)] * 2
        + [pltpu.VMEM((stacked, HEAD_SIZE), jnp.bfloat16)] * 4
        + [pltpu.VMEM((rows, GROUP_WIDTH), jnp.bfloat16)] * 2
        + [pltpu.SemaphoreType.DMA((2,))],
        out_shape=[jax.ShapeDtypeStruct(array.shape, jnp.bfloat16) for array in carried],
        input_output_aliases={first_carried + n: i for n, i in enumerate(kept)},
        compiler_params=pltpu.CompilerParams(vmem_limit_bytes=KERNEL_VMEM),
        cost_estimate=pl.CostEstimate(
            flops=8 * group_rows * HEADS_PER_GROUP * HEAD_SIZE * total,
            bytes_accessed=16 * group_rows * GROUP_WIDTH,
            transcendentals=group_rows * HEADS_PER_GROUP * total,
        ),
        name="span_attention",
    )(listed, place, own, *received, near, far, *[carried[i] for i in kept])


def unpack_kernel(head_count, groups, *refs):
    parts, outs = refs[:-4], refs[-4:]
    rows = outs[0].shape[0]
    half = outs[0].shape[1] // head_count
    width = HEAD_SIZE
    for step in range(head_count):
        source = lax.rem(lax.axis_index("head") + step, head_count)
        for group, members in enumerate(groups):
            part = parts[group * head_count + step]
            for at, member in enumerate(members):
                to = lanes(source * half + member * width, width)
                for index in range(2):
                    here = slice((2 * at + index) * width, (2 * at + index + 1) * width)
                    outs[index][:, to] = part[:rows, here]
                    outs[2 + index][:, to] = part[rows:, here]


def unpacked(head_count, groups, grads, rows, clean_rows):
    vmem = pl.BlockSpec(memory_space=pltpu.VMEM)
    parts = [part for chunk in grads for part in chunk]
    width = KEY_VALUE_HEADS * HEAD_SIZE
    return pl.pallas_call(
        functools.partial(unpack_kernel, head_count, groups),
        in_specs=[vmem] * len(parts),
        out_specs=[vmem] * 4,
        out_shape=[jax.ShapeDtypeStruct((rows, width), jnp.bfloat16)] * 2
        + [jax.ShapeDtypeStruct((clean_rows, width), jnp.bfloat16)] * 2,
        name="unpack_gradients",
    )(*parts)


def shards(
    queries,
    noisy_token_keys,
    noisy_token_values,
    clean_token_keys,
    clean_token_values,
    output_gradient,
    history_list,
):
    ctx_count = lax.axis_size("ctx")
    head_count = lax.axis_size("head")
    head = lax.axis_index("head")
    place = jnp.stack([lax.axis_index("ctx"), head]).astype(jnp.int32)
    rows = queries.shape[0]
    clean_rows = clean_token_keys.shape[0]
    store_rows = clean_rows * head_count
    group_rows = rows * head_count
    slots = ctx_count - 2
    per_device = KEY_VALUE_HEADS // head_count
    everything = list(range(per_device))
    half = max(1, per_device // 2)
    key_groups = [g for g in (everything[:half], everything[half:]) if g]
    grad_groups = key_groups
    ask_groups = send_groups = [[m] for m in everything]
    depth = ctx_count // 4
    steps = range(1, head_count)
    row_order = lax.rem(head - jnp.arange(head_count, dtype=jnp.int32) + head_count, head_count)

    def by_block(store):
        if clean_rows >= BLK:
            return store
        return store.reshape(head_count, clean_rows, -1)[row_order].reshape(store.shape)

    (pack,) = packed(
        head_count,
        [everything],
        noisy_token_keys,
        noisy_token_values,
        clean_token_keys,
        clean_token_values,
    )

    asks = query_blocks(head_count, queries, output_gradient)

    def cut(array, index):
        first, last = key_groups[index][0], key_groups[index][-1] + 1
        return array[:, 2 * HEAD_SIZE * first : 2 * HEAD_SIZE * last]

    def swap_queries(member):
        return [shifted(asks[member][step], step) for step in steps]

    def stored(parts):
        return by_block(jnp.concatenate([part[rows:] for part in parts], 0))

    def along(store):
        return [flipped(store, z << 2) for z in range(1, depth)]

    def joined(index, crossed):
        noisy = [cut(part[:rows], index) for part in parts]
        return jnp.concatenate([*noisy, lines[index], crossed], 0)

    def summed(near_grad, from_core):
        total = near_grad.astype(jnp.float32) + from_core.astype(jnp.float32)
        return total[:group_rows], total[group_rows:]

    def halved(line):
        middle = line.shape[0] // 2
        return line[:middle], flipped(line[middle:].astype(jnp.bfloat16), 2)

    def back_along(line):
        gives = [line[z * store_rows : (z + 1) * store_rows] for z in range(depth)]
        return gives[0], [
            flipped(give.astype(jnp.bfloat16), z << 2) for z, give in enumerate(gives[1:], 1)
        ]

    def added(keep, others):
        for other in others:
            keep = keep + other.astype(jnp.float32)
        return keep

    together = lax.optimization_barrier
    def swap_heads(noisy_sum, store_sum):
        if clean_rows < BLK:
            store_sum = store_sum.reshape(head_count, clean_rows, -1)[row_order].reshape(
                store_sum.shape
            )
        store_sum = store_sum.astype(jnp.bfloat16)
        noisy_sum = noisy_sum.astype(jnp.bfloat16)
        mixed = [
            jnp.concatenate(
                [
                    noisy_sum[step * rows : (step + 1) * rows],
                    store_sum[step * clean_rows : (step + 1) * clean_rows],
                ],
                0,
            )
            for step in range(head_count)
        ]
        return [mixed[0]] + [shifted(mixed[step], -step) for step in steps]

    shape = (head_count, group_rows, store_rows, clean_rows, slots)
    received = {}
    two = len(key_groups) > 1
    parts = [pack[0]] + [shifted(pack[step], step) for step in steps]
    store = stored(parts)
    others = along(store)
    asks[0], parts = together((asks[0], parts))
    received[0] = swap_queries(0)
    lines = [
        jnp.concatenate([cut(part, index) for part in (store, *others)], 0)
        for index in range(len(key_groups))
    ]
    crossing = flipped(lines[0], 2)
    if two:
        asks[1], received[0], others = together((asks[1], received[0], others))
        received[1] = swap_queries(1)
    near = joined(0, crossing)
    if two:
        near, asks[2], received[1] = together((near, asks[2], received[1]))
        received[2] = swap_queries(2)
        lines[1], near = together((lines[1], near))
        crossing = flipped(lines[1], 2)
    keys = {0: (near, flipped(near, 1))}
    outputs = [jax.ShapeDtypeStruct(queries.shape, jnp.bfloat16)] * 2
    sent = []
    held = []
    waiting = []

    def group_of(groups, member):
        return next(i for i, group in enumerate(groups) if member in group)

    for member in everything:
        k = group_of(key_groups, member)
        first = member == key_groups[k][0]
        last = member == key_groups[k][-1]
        sends = [jax.ShapeDtypeStruct((2 * rows, GROUP_WIDTH), jnp.bfloat16)] * (head_count - 1)
        if first:
            width = len(key_groups[k]) * 2 * HEAD_SIZE
            pair = [jax.ShapeDtypeStruct((near.shape[0], width), jnp.bfloat16)] * 2
        column = key_groups[k].index(member)
        outputs[0], outputs[1], *rest = attention(
            history_list,
            jnp.concatenate([place, jnp.array([member], jnp.int32)]),
            asks[member][0],
            received[member],
            *keys[k],
            [*outputs, *sends, *pair],
            shape,
            column,
        )
        sends, pair = rest[:-2], rest[-2:]
        if two and member == 0:
            outputs, crossing, received[2] = together((outputs, crossing, received[2]))
            near = joined(1, crossing)
            keys[1] = (near, flipped(near, 1))
        if member + 3 < per_device:
            asks, outputs = together((asks, outputs))
            received[member + 3] = swap_queries(member + 3)
        if two and member == 1:
            pair, received[3] = together((pair, received[3]))
        held.append(sends)
        if two and member == half:
            held[half - 1], outputs = together((held[half - 1], outputs))
        if not two or member >= half - 1:
            later = len(held) if member == everything[-1] else len(held) - 1
            for block_set in held[len(sent) : later]:
                sent.append([shifted(block, -step) for step, block in zip(steps, block_set)])
        if waiting and not last:
            noisy_sum, line = summed(*waiting[0])
            line, outputs, sent[0] = together((line, outputs, sent[0]))
            waiting[0] = (noisy_sum, *halved(line))
        if last:
            if waiting:
                waiting[0], pair, sent[:half] = together((waiting[0], pair, sent[:half]))
            waiting.append((pair[0], flipped(pair[1], 1)))
    grads = []
    if two:
        first_noisy, keep, other = waiting[0]
        keep, others = back_along(added(keep, [other]))
    noisy_sum, line = summed(*waiting[-1])
    last_keep, last_other = halved(line)
    if two:
        last_other, others, sent[:half] = together((last_other, others, sent[:half]))
        grads.append(swap_heads(first_noisy, added(keep, others)))
    last_keep, last_others = back_along(added(last_keep, [last_other]))
    line = added(last_keep, last_others)
    if two:
        line, sent[half:] = together((line, sent[half:]))
    grads.append(swap_heads(noisy_sum, line))
    attended, query_grad = outputs
    for group, blocks in zip(send_groups, sent):
        for step, block in zip(steps, blocks):
            source = lax.rem(head + step, head_count)
            start = (source * per_device + group[0]) * GROUP_WIDTH
            attended = lax.dynamic_update_slice_in_dim(attended, block[:rows], start, 1)
            query_grad = lax.dynamic_update_slice_in_dim(query_grad, block[rows:], start, 1)
    finished = unpacked(head_count, grad_groups, grads, rows, clean_rows)
    return (attended, query_grad, *finished)


def solution(mesh):
    split = P(("ctx", "head"), None)
    return jax.shard_map(
        shards,
        mesh=mesh,
        in_specs=(split, split, split, split, split, split, P()),
        out_specs=(split,) * 6,
        check_vma=False,
    )
```

```python
import functools

import jax
import jax.numpy as jnp
from jax import lax
from jax.experimental import pallas as pl
from jax.experimental.pallas import tpu as pltpu
from jax.sharding import PartitionSpec as P

QUERY_HEADS = 48
KEY_VALUE_HEADS = 8
HEAD_SIZE = 128
BLK = 32
HEADS_PER_GROUP = QUERY_HEADS // KEY_VALUE_HEADS
GROUP_WIDTH = HEADS_PER_GROUP * HEAD_SIZE
SCALE = HEAD_SIZE**-0.5
LOG2E = 1.4426950408889634

NEG_FILL = -1e30
SLICE_ROWS = 256
KERNEL_VMEM = 32 * 2**20


def flipped(block, bits):
    count = lax.axis_size("ctx")
    return lax.ppermute(block, "ctx", [(i, i ^ bits) for i in range(count)])


def shifted(block, step):
    count = lax.axis_size("head")
    return lax.ppermute(block, "head", [(i, (i + step) % count) for i in range(count)])


def dot(a, b, contract):
    return lax.dot_general(
        a, b, ((contract[:1], contract[1:]), ((), ())), preferred_element_type=jnp.float32
    )


def lanes(start, size):
    return pl.ds(pl.multiple_of(start, HEAD_SIZE), size)


def pack_kernel(head_count, groups, k_noisy, v_noisy, k_clean, v_clean, *outs):
    rows = k_noisy.shape[0]
    half = k_noisy.shape[1] // head_count
    width = HEAD_SIZE
    for index, group in enumerate(groups):
        for step in range(head_count):
            out = outs[index * head_count + step]
            target = lax.rem(lax.axis_index("head") + step, head_count)
            for at, member in enumerate(group):
                source = lanes(target * half + member * width, width)
                for n, (noisy, clean) in enumerate(((k_noisy, k_clean), (v_noisy, v_clean))):
                    to = slice((2 * at + n) * width, (2 * at + n + 1) * width)
                    out[:rows, to] = noisy[:, source]
                    out[rows:, to] = clean[:, source]


def packed(head_count, groups, k_noisy, v_noisy, k_clean, v_clean):
    vmem = pl.BlockSpec(memory_space=pltpu.VMEM)
    rows = k_noisy.shape[0] + k_clean.shape[0]
    shapes = [
        jax.ShapeDtypeStruct((rows, 2 * HEAD_SIZE * len(group)), jnp.bfloat16)
        for group in groups
        for _ in range(head_count)
    ]
    outs = pl.pallas_call(
        functools.partial(pack_kernel, head_count, groups),
        in_specs=[vmem] * 4,
        out_specs=[vmem] * len(shapes),
        out_shape=shapes,
        name="pack_keys_values",
    )(k_noisy, v_noisy, k_clean, v_clean)
    return [outs[i * head_count : (i + 1) * head_count] for i in range(len(groups))]


def stack_kernel(head_count, q, g, *outs):
    rows = q.shape[0]
    per_device = KEY_VALUE_HEADS // head_count
    for member in range(per_device):
        for step in range(head_count):
            out = outs[member * head_count + step]
            target = lax.rem(lax.axis_index("head") + step, head_count)
            source = lanes((target * per_device + member) * GROUP_WIDTH, GROUP_WIDTH)
            out[:rows, :] = q[:, source]
            out[rows:, :] = g[:, source]


def query_blocks(head_count, q, g):
    vmem = pl.BlockSpec(memory_space=pltpu.VMEM)
    shape = jax.ShapeDtypeStruct((2 * q.shape[0], GROUP_WIDTH), jnp.bfloat16)
    outs = pl.pallas_call(
        functools.partial(stack_kernel, head_count),
        in_specs=[vmem] * 2,
        out_specs=[vmem] * KEY_VALUE_HEADS,
        out_shape=[shape] * KEY_VALUE_HEADS,
        name="stack_queries",
    )(q, g)
    return [outs[i : i + head_count] for i in range(0, KEY_VALUE_HEADS, head_count)]


def attention_kernel(shape, column, kept, listed, place, own, *refs):
    head_count, group_rows, store_rows, clean_rows, slots = shape
    received, refs = refs[: head_count - 1], refs[head_count - 1 :]
    near, far, *refs = refs
    o_all, gq_all, *refs = refs[kept:]
    sends, refs = refs[: head_count - 1], refs[head_count - 1 :]
    near_grad, far_grad, k_all, v_all, q_all, g_all, o_out, gq_out, o_own, gq_own, copied = refs
    rows = own.shape[0] // 2
    width = HEAD_SIZE
    position, head = place[0], place[1]
    k_cols = slice(2 * column * width, (2 * column + 1) * width)
    v_cols = slice((2 * column + 1) * width, (2 * column + 2) * width)
    depth = (near.shape[0] - group_rows) // (2 * store_rows)

    def placed(slot):
        apart = lax.bitwise_xor(position, slot)
        store = lax.bitwise_and(lax.shift_right_logical(apart, 1), 1) * depth
        store = store + lax.shift_right_logical(apart, 2)
        block = jnp.maximum(listed[position, slot], 0)
        if clean_rows >= BLK:
            owner = lax.div(block * BLK, clean_rows)
            step = lax.rem(head - owner + head_count, head_count)
            inside = step * clean_rows + block * BLK - owner * clean_rows
        else:
            inside = block * BLK
        start = pl.multiple_of(group_rows + store * store_rows + inside, BLK)
        return lax.bitwise_and(apart, 1), pl.ds(start, BLK)

    k_all[:group_rows, :] = near[:group_rows, k_cols]
    v_all[:group_rows, :] = near[:group_rows, v_cols]
    k_all[group_rows : 2 * group_rows, :] = far[:group_rows, k_cols]
    v_all[group_rows : 2 * group_rows, :] = far[:group_rows, v_cols]
    span = 2 * group_rows
    total = span + slots * BLK
    for slot in range(slots):
        other, source = placed(slot)
        to = slice(span + slot * BLK, span + (slot + 1) * BLK)
        k_all[to, :] = jnp.where(other == 1, far[source, k_cols], near[source, k_cols])
        v_all[to, :] = jnp.where(other == 1, far[source, v_cols], near[source, v_cols])
    at = 0
    for r in range(HEADS_PER_GROUP):
        for part in (own, *received):
            q_all[at : at + rows, :] = part[:rows, r * width : (r + 1) * width]
            g_all[at : at + rows, :] = part[rows:, r * width : (r + 1) * width]
            at += rows

    keys = k_all[...]
    values = v_all[...]
    keys_t = keys.T
    values_t = values.T
    biases = [
        jnp.where(listed[position, slot] >= 0, 0.0, NEG_FILL).astype(jnp.float32)
        for slot in range(slots)
    ]
    cuts = list(range(0, at - SLICE_ROWS + 1, SLICE_ROWS)) + [at]
    slices = [slice(low, high) for low, high in zip(cuts, cuts[1:])]

    def products(piece):
        query, upstream = q_all[piece, :], g_all[piece, :]
        return query, upstream, dot(keys, query, (1, 1)), dot(values, upstream, (1, 1))

    def softmax(scores, dprob):
        scores = scores * (SCALE * LOG2E)
        pieces = [scores[:span]]
        for slot in range(slots):
            low = span + slot * BLK
            pieces.append(scores[low : low + BLK] + biases[slot])
        scores = jnp.concatenate(pieces, 0)
        top = jnp.max(scores, 0, keepdims=True)
        unscaled = jnp.exp2(scores - top)
        prob = unscaled * (1.0 / jnp.sum(unscaled, 0, keepdims=True))
        row_dot = jnp.sum(prob * dprob, 0, keepdims=True)
        return prob.astype(jnp.bfloat16), (prob * (dprob - row_dot)).astype(jnp.bfloat16)

    gk = jnp.zeros((total, width), jnp.float32)
    gv = jnp.zeros((total, width), jnp.float32)
    ahead = products(slices[0])
    for index, piece in enumerate(slices):
        query, upstream, scores, dprob = ahead
        if index + 1 < len(slices):
            ahead = products(slices[index + 1])
        weights, dscore = softmax(scores, dprob)
        o_out[piece, :] = dot(values_t, weights, (1, 0)).astype(jnp.bfloat16).T
        gq_out[piece, :] = (dot(keys_t, dscore, (1, 0)) * SCALE).astype(jnp.bfloat16).T
        gk = gk + dot(dscore, query, (1, 0))
        gv = gv + dot(weights, upstream, (1, 0))
    at = 0
    for r in range(HEADS_PER_GROUP):
        to = slice(r * width, (r + 1) * width)
        for part in (None, *sends):
            attended, gq = o_out[at : at + rows, :], gq_out[at : at + rows, :]
            if part is None:
                o_own[:, to] = attended
                gq_own[:, to] = gq
            else:
                part[:rows, to] = attended
                part[rows:, to] = gq
            at += rows
    start = (head * (KEY_VALUE_HEADS // head_count) + place[2]) * GROUP_WIDTH
    target = lanes(start, GROUP_WIDTH)
    copies = [
        pltpu.make_async_copy(o_own, o_all.at[:, target], copied.at[0]),
        pltpu.make_async_copy(gq_own, gq_all.at[:, target], copied.at[1]),
    ]
    for copy in copies:
        copy.start()
    gk = (gk * SCALE).astype(jnp.bfloat16)
    gv = gv.astype(jnp.bfloat16)
    for index, grad in enumerate((near_grad, far_grad)):
        here = slice(index * group_rows, (index + 1) * group_rows)
        grad[:group_rows, k_cols] = gk[here]
        grad[:group_rows, v_cols] = gv[here]
        rest = grad.shape[0] - group_rows
        grad[group_rows:, k_cols] = jnp.zeros((rest, width), jnp.bfloat16)
        grad[group_rows:, v_cols] = jnp.zeros((rest, width), jnp.bfloat16)
    for slot in range(slots):
        other, target = placed(slot)
        low = span + slot * BLK
        for index, grad in enumerate((near_grad, far_grad)):

            @pl.when(jnp.logical_and(listed[position, slot] >= 0, other == index))
            def _():
                grad[target, k_cols] = gk[low : low + BLK]
                grad[target, v_cols] = gv[low : low + BLK]

    for copy in copies:
        copy.wait()


def attention(listed, place, own, received, near, far, carried, shape, column):
    head_count, group_rows, store_rows, clean_rows, slots = shape
    rows = own.shape[0] // 2
    total = 2 * group_rows + slots * BLK
    stacked = HEADS_PER_GROUP * group_rows
    smem = pl.BlockSpec(memory_space=pltpu.SMEM)
    vmem = pl.BlockSpec(memory_space=pltpu.VMEM)
    hbm = pl.BlockSpec(memory_space=pl.ANY)
    kept = [i for i, array in enumerate(carried) if not isinstance(array, jax.ShapeDtypeStruct)]
    first_carried = 3 + len(received) + 2
    spaces = [hbm, hbm] + [vmem] * (len(carried) - 2)
    return pl.pallas_call(
        functools.partial(attention_kernel, shape, column, len(kept)),
        in_specs=[smem, smem] + [vmem] * (3 + len(received)) + [spaces[i] for i in kept],
        out_specs=spaces,
        scratch_shapes=[pltpu.VMEM((total, HEAD_SIZE), jnp.bfloat16)] * 2
        + [pltpu.VMEM((stacked, HEAD_SIZE), jnp.bfloat16)] * 4
        + [pltpu.VMEM((rows, GROUP_WIDTH), jnp.bfloat16)] * 2
        + [pltpu.SemaphoreType.DMA((2,))],
        out_shape=[jax.ShapeDtypeStruct(array.shape, jnp.bfloat16) for array in carried],
        input_output_aliases={first_carried + n: i for n, i in enumerate(kept)},
        compiler_params=pltpu.CompilerParams(vmem_limit_bytes=KERNEL_VMEM),
        cost_estimate=pl.CostEstimate(
            flops=8 * group_rows * HEADS_PER_GROUP * HEAD_SIZE * total,
            bytes_accessed=16 * group_rows * GROUP_WIDTH,
            transcendentals=group_rows * HEADS_PER_GROUP * total,
        ),
        name="span_attention",
    )(listed, place, own, *received, near, far, *[carried[i] for i in kept])


def unpack_kernel(head_count, groups, *refs):
    parts, outs = refs[:-4], refs[-4:]
    rows = outs[0].shape[0]
    half = outs[0].shape[1] // head_count
    width = HEAD_SIZE
    for step in range(head_count):
        source = lax.rem(lax.axis_index("head") + step, head_count)
        for group, members in enumerate(groups):
            part = parts[group * head_count + step]
            for at, member in enumerate(members):
                to = lanes(source * half + member * width, width)
                for index in range(2):
                    here = slice((2 * at + index) * width, (2 * at + index + 1) * width)
                    outs[index][:, to] = part[:rows, here]
                    outs[2 + index][:, to] = part[rows:, here]


def unpacked(head_count, groups, grads, rows, clean_rows):
    vmem = pl.BlockSpec(memory_space=pltpu.VMEM)
    parts = [part for chunk in grads for part in chunk]
    width = KEY_VALUE_HEADS * HEAD_SIZE
    return pl.pallas_call(
        functools.partial(unpack_kernel, head_count, groups),
        in_specs=[vmem] * len(parts),
        out_specs=[vmem] * 4,
        out_shape=[jax.ShapeDtypeStruct((rows, width), jnp.bfloat16)] * 2
        + [jax.ShapeDtypeStruct((clean_rows, width), jnp.bfloat16)] * 2,
        name="unpack_gradients",
    )(*parts)


def shards(
    queries,
    noisy_token_keys,
    noisy_token_values,
    clean_token_keys,
    clean_token_values,
    output_gradient,
    history_list,
):
    ctx_count = lax.axis_size("ctx")
    head_count = lax.axis_size("head")
    head = lax.axis_index("head")
    place = jnp.stack([lax.axis_index("ctx"), head]).astype(jnp.int32)
    rows = queries.shape[0]
    clean_rows = clean_token_keys.shape[0]
    store_rows = clean_rows * head_count
    group_rows = rows * head_count
    slots = ctx_count - 2
    per_device = KEY_VALUE_HEADS // head_count
    everything = list(range(per_device))
    half = max(1, per_device // 2)
    key_groups = [g for g in (everything[:half], everything[half:]) if g]
    grad_groups = key_groups
    ask_groups = send_groups = [[m] for m in everything]
    depth = ctx_count // 4
    steps = range(1, head_count)
    row_order = lax.rem(head - jnp.arange(head_count, dtype=jnp.int32) + head_count, head_count)

    def by_block(store):
        if clean_rows >= BLK:
            return store
        return store.reshape(head_count, clean_rows, -1)[row_order].reshape(store.shape)

    packs = packed(
        head_count,
        key_groups,
        noisy_token_keys,
        noisy_token_values,
        clean_token_keys,
        clean_token_values,
    )

    asks = query_blocks(head_count, queries, output_gradient)

    def swap_keys(index):
        return [packs[index][0]] + [shifted(packs[index][step], step) for step in steps]

    def swap_queries(member):
        return [shifted(asks[member][step], step) for step in steps]

    def stored(parts):
        return by_block(jnp.concatenate([part[rows:] for part in parts], 0))

    def along(store):
        return [flipped(store, z << 2) for z in range(1, depth)]

    def joined(parts, line):
        return jnp.concatenate([part[:rows] for part in parts] + [line], 0)

    def summed(near_grad, from_core):
        total = near_grad.astype(jnp.float32) + from_core.astype(jnp.float32)
        return total[:group_rows], total[group_rows:]

    def halved(line):
        middle = line.shape[0] // 2
        return line[:middle], flipped(line[middle:].astype(jnp.bfloat16), 2)

    def back_along(line):
        gives = [line[z * store_rows : (z + 1) * store_rows] for z in range(depth)]
        return gives[0], [
            flipped(give.astype(jnp.bfloat16), z << 2) for z, give in enumerate(gives[1:], 1)
        ]

    def added(keep, others):
        for other in others:
            keep = keep + other.astype(jnp.float32)
        return keep

    together = lax.optimization_barrier
    def swap_heads(noisy_sum, store_sum):
        if clean_rows < BLK:
            store_sum = store_sum.reshape(head_count, clean_rows, -1)[row_order].reshape(
                store_sum.shape
            )
        store_sum = store_sum.astype(jnp.bfloat16)
        noisy_sum = noisy_sum.astype(jnp.bfloat16)
        mixed = [
            jnp.concatenate(
                [
                    noisy_sum[step * rows : (step + 1) * rows],
                    store_sum[step * clean_rows : (step + 1) * clean_rows],
                ],
                0,
            )
            for step in range(head_count)
        ]
        return [mixed[0]] + [shifted(mixed[step], -step) for step in steps]

    shape = (head_count, group_rows, store_rows, clean_rows, slots)
    received = {}
    two = len(key_groups) > 1
    parts = swap_keys(0)
    store = stored(parts)
    others = along(store)
    if two:
        asks[0], parts = together((asks[0], parts))
    received[0] = swap_queries(0)
    line = jnp.concatenate([store, *others], 0)
    crossing = flipped(line, 2)
    if two:
        packs[1], received[0], others = together((packs[1], received[0], others))
        later_parts = swap_keys(1)
        asks[1], later_parts = together((asks[1], later_parts))
        received[1] = swap_queries(1)
        later_store = stored(later_parts)
        later_others = along(later_store)
    near = joined(parts, jnp.concatenate([line, crossing], 0))
    if two:
        near, asks[2], later_parts = together((near, asks[2], later_parts))
        received[2] = swap_queries(2)
    keys = {0: (near, flipped(near, 1))}
    outputs = [jax.ShapeDtypeStruct(queries.shape, jnp.bfloat16)] * 2
    sent = []
    held = []
    waiting = []

    def group_of(groups, member):
        return next(i for i, group in enumerate(groups) if member in group)

    for member in everything:
        k = group_of(key_groups, member)
        first = member == key_groups[k][0]
        last = member == key_groups[k][-1]
        sends = [jax.ShapeDtypeStruct((2 * rows, GROUP_WIDTH), jnp.bfloat16)] * (head_count - 1)
        if first:
            width = len(key_groups[k]) * 2 * HEAD_SIZE
            pair = [jax.ShapeDtypeStruct((near.shape[0], width), jnp.bfloat16)] * 2
        column = key_groups[k].index(member)
        outputs[0], outputs[1], *rest = attention(
            history_list,
            jnp.concatenate([place, jnp.array([member], jnp.int32)]),
            asks[member][0],
            received[member],
            *keys[k],
            [*outputs, *sends, *pair],
            shape,
            column,
        )
        sends, pair = rest[:-2], rest[-2:]
        if two and member == 0:
            outputs, later_others, received[1], received[2] = together(
                (outputs, later_others, received[1], received[2])
            )
            later_line = jnp.concatenate([later_store, *later_others], 0)
            crossing = flipped(later_line, 2)
        if two and member == 1:
            outputs, crossing = together((outputs, crossing))
            near = joined(later_parts, jnp.concatenate([later_line, crossing], 0))
            keys[1] = (near, flipped(near, 1))
        if member + 3 < per_device:
            asks, outputs = together((asks, outputs))
            received[member + 3] = swap_queries(member + 3)
        if two and member == 1:
            pair, received[3] = together((pair, received[3]))
        held.append(sends)
        if two and member == half:
            held[half - 1], outputs = together((held[half - 1], outputs))
        if not two or member >= half - 1:
            later = len(held) if member == everything[-1] else len(held) - 1
            for block_set in held[len(sent) : later]:
                sent.append([shifted(block, -step) for step, block in zip(steps, block_set)])
        if waiting and not last:
            noisy_sum, line = summed(*waiting[0])
            line, outputs, sent[0] = together((line, outputs, sent[0]))
            waiting[0] = (noisy_sum, *halved(line))
        if last:
            if waiting:
                waiting[0], pair, sent[:half] = together((waiting[0], pair, sent[:half]))
            waiting.append((pair[0], flipped(pair[1], 1)))
    grads = []
    if two:
        first_noisy, keep, other = waiting[0]
        keep, others = back_along(added(keep, [other]))
    noisy_sum, line = summed(*waiting[-1])
    last_keep, last_other = halved(line)
    if two:
        last_other, others, sent[:half] = together((last_other, others, sent[:half]))
        grads.append(swap_heads(first_noisy, added(keep, others)))
    last_keep, last_others = back_along(added(last_keep, [last_other]))
    line = added(last_keep, last_others)
    if two:
        line, sent[half:] = together((line, sent[half:]))
    grads.append(swap_heads(noisy_sum, line))
    attended, query_grad = outputs
    for group, blocks in zip(send_groups, sent):
        for step, block in zip(steps, blocks):
            source = lax.rem(head + step, head_count)
            start = (source * per_device + group[0]) * GROUP_WIDTH
            attended = lax.dynamic_update_slice_in_dim(attended, block[:rows], start, 1)
            query_grad = lax.dynamic_update_slice_in_dim(query_grad, block[rows:], start, 1)
    finished = unpacked(head_count, grad_groups, grads, rows, clean_rows)
    return (attended, query_grad, *finished)


def solution(mesh):
    split = P(("ctx", "head"), None)
    return jax.shard_map(
        shards,
        mesh=mesh,
        in_specs=(split, split, split, split, split, split, P()),
        out_specs=(split,) * 6,
        check_vma=False,
    )
```

```python
import functools

import jax
import jax.numpy as jnp
from jax import lax
from jax.experimental import pallas as pl
from jax.experimental.pallas import tpu as pltpu
from jax.sharding import PartitionSpec as P

QUERY_HEADS = 48
KEY_VALUE_HEADS = 8
HEAD_SIZE = 128
BLK = 32
HEADS_PER_GROUP = QUERY_HEADS // KEY_VALUE_HEADS
GROUP_WIDTH = HEADS_PER_GROUP * HEAD_SIZE
SCALE = HEAD_SIZE**-0.5
LOG2E = 1.4426950408889634

NEG_FILL = -1e30
SLICE_ROWS = 256
KERNEL_VMEM = 32 * 2**20


def flipped(block, bits):
    count = lax.axis_size("ctx")
    return lax.ppermute(block, "ctx", [(i, i ^ bits) for i in range(count)])


def shifted(block, step):
    count = lax.axis_size("head")
    return lax.ppermute(block, "head", [(i, (i + step) % count) for i in range(count)])


def dot(a, b, contract):
    return lax.dot_general(
        a, b, ((contract[:1], contract[1:]), ((), ())), preferred_element_type=jnp.float32
    )


def lanes(start, size):
    return pl.ds(pl.multiple_of(start, HEAD_SIZE), size)


def pack_kernel(head_count, groups, k_noisy, v_noisy, k_clean, v_clean, *outs):
    rows = k_noisy.shape[0]
    half = k_noisy.shape[1] // head_count
    width = HEAD_SIZE
    for index, group in enumerate(groups):
        for step in range(head_count):
            out = outs[index * head_count + step]
            target = lax.rem(lax.axis_index("head") + step, head_count)
            for at, member in enumerate(group):
                source = lanes(target * half + member * width, width)
                for n, (noisy, clean) in enumerate(((k_noisy, k_clean), (v_noisy, v_clean))):
                    to = slice((2 * at + n) * width, (2 * at + n + 1) * width)
                    out[:rows, to] = noisy[:, source]
                    out[rows:, to] = clean[:, source]


def packed(head_count, groups, k_noisy, v_noisy, k_clean, v_clean):
    vmem = pl.BlockSpec(memory_space=pltpu.VMEM)
    rows = k_noisy.shape[0] + k_clean.shape[0]
    shapes = [
        jax.ShapeDtypeStruct((rows, 2 * HEAD_SIZE * len(group)), jnp.bfloat16)
        for group in groups
        for _ in range(head_count)
    ]
    outs = pl.pallas_call(
        functools.partial(pack_kernel, head_count, groups),
        in_specs=[vmem] * 4,
        out_specs=[vmem] * len(shapes),
        out_shape=shapes,
        name="pack_keys_values",
    )(k_noisy, v_noisy, k_clean, v_clean)
    return [outs[i * head_count : (i + 1) * head_count] for i in range(len(groups))]


def stack_kernel(head_count, q, g, *outs):
    rows = q.shape[0]
    per_device = KEY_VALUE_HEADS // head_count
    for member in range(per_device):
        for step in range(head_count):
            out = outs[member * head_count + step]
            target = lax.rem(lax.axis_index("head") + step, head_count)
            source = lanes((target * per_device + member) * GROUP_WIDTH, GROUP_WIDTH)
            out[:rows, :] = q[:, source]
            out[rows:, :] = g[:, source]


def query_blocks(head_count, q, g):
    vmem = pl.BlockSpec(memory_space=pltpu.VMEM)
    shape = jax.ShapeDtypeStruct((2 * q.shape[0], GROUP_WIDTH), jnp.bfloat16)
    outs = pl.pallas_call(
        functools.partial(stack_kernel, head_count),
        in_specs=[vmem] * 2,
        out_specs=[vmem] * KEY_VALUE_HEADS,
        out_shape=[shape] * KEY_VALUE_HEADS,
        name="stack_queries",
    )(q, g)
    return [outs[i : i + head_count] for i in range(0, KEY_VALUE_HEADS, head_count)]


def attention_kernel(shape, column, kept, listed, place, own, *refs):
    head_count, group_rows, store_rows, clean_rows, slots = shape
    received, refs = refs[: head_count - 1], refs[head_count - 1 :]
    near, far, *refs = refs
    o_all, gq_all, *refs = refs[kept:]
    sends, refs = refs[: head_count - 1], refs[head_count - 1 :]
    near_grad, far_grad, k_all, v_all, q_all, g_all, o_out, gq_out, o_own, gq_own, copied = refs
    rows = own.shape[0] // 2
    width = HEAD_SIZE
    position, head = place[0], place[1]
    k_cols = slice(2 * column * width, (2 * column + 1) * width)
    v_cols = slice((2 * column + 1) * width, (2 * column + 2) * width)
    depth = (near.shape[0] - group_rows) // (2 * store_rows)

    def placed(slot):
        apart = lax.bitwise_xor(position, slot)
        store = lax.bitwise_and(lax.shift_right_logical(apart, 1), 1) * depth
        store = store + lax.shift_right_logical(apart, 2)
        block = jnp.maximum(listed[position, slot], 0)
        if clean_rows >= BLK:
            owner = lax.div(block * BLK, clean_rows)
            step = lax.rem(head - owner + head_count, head_count)
            inside = step * clean_rows + block * BLK - owner * clean_rows
        else:
            inside = block * BLK
        start = pl.multiple_of(group_rows + store * store_rows + inside, BLK)
        return lax.bitwise_and(apart, 1), pl.ds(start, BLK)

    k_all[:group_rows, :] = near[:group_rows, k_cols]
    v_all[:group_rows, :] = near[:group_rows, v_cols]
    k_all[group_rows : 2 * group_rows, :] = far[:group_rows, k_cols]
    v_all[group_rows : 2 * group_rows, :] = far[:group_rows, v_cols]
    span = 2 * group_rows
    total = span + slots * BLK
    for slot in range(slots):
        other, source = placed(slot)
        to = slice(span + slot * BLK, span + (slot + 1) * BLK)
        k_all[to, :] = jnp.where(other == 1, far[source, k_cols], near[source, k_cols])
        v_all[to, :] = jnp.where(other == 1, far[source, v_cols], near[source, v_cols])
    at = 0
    for r in range(HEADS_PER_GROUP):
        for part in (own, *received):
            q_all[at : at + rows, :] = part[:rows, r * width : (r + 1) * width]
            g_all[at : at + rows, :] = part[rows:, r * width : (r + 1) * width]
            at += rows

    keys = k_all[...]
    values = v_all[...]
    keys_t = keys.T
    values_t = values.T
    biases = [
        jnp.where(listed[position, slot] >= 0, 0.0, NEG_FILL).astype(jnp.float32)
        for slot in range(slots)
    ]
    cuts = list(range(0, at - SLICE_ROWS + 1, SLICE_ROWS)) + [at]
    slices = [slice(low, high) for low, high in zip(cuts, cuts[1:])]

    def products(piece):
        query, upstream = q_all[piece, :], g_all[piece, :]
        return query, upstream, dot(keys, query, (1, 1)), dot(values, upstream, (1, 1))

    def softmax(scores, dprob):
        scores = scores * (SCALE * LOG2E)
        pieces = [scores[:span]]
        for slot in range(slots):
            low = span + slot * BLK
            pieces.append(scores[low : low + BLK] + biases[slot])
        scores = jnp.concatenate(pieces, 0)
        top = jnp.max(scores, 0, keepdims=True)
        unscaled = jnp.exp2(scores - top)
        prob = unscaled * (1.0 / jnp.sum(unscaled, 0, keepdims=True))
        row_dot = jnp.sum(prob * dprob, 0, keepdims=True)
        return prob.astype(jnp.bfloat16), (prob * (dprob - row_dot)).astype(jnp.bfloat16)

    gk = jnp.zeros((total, width), jnp.float32)
    gv = jnp.zeros((total, width), jnp.float32)
    ahead = products(slices[0])
    for index, piece in enumerate(slices):
        query, upstream, scores, dprob = ahead
        if index + 1 < len(slices):
            ahead = products(slices[index + 1])
        weights, dscore = softmax(scores, dprob)
        o_out[piece, :] = dot(values_t, weights, (1, 0)).astype(jnp.bfloat16).T
        gq_out[piece, :] = (dot(keys_t, dscore, (1, 0)) * SCALE).astype(jnp.bfloat16).T
        gk = gk + dot(dscore, query, (1, 0))
        gv = gv + dot(weights, upstream, (1, 0))
    at = 0
    for r in range(HEADS_PER_GROUP):
        to = slice(r * width, (r + 1) * width)
        for part in (None, *sends):
            attended, gq = o_out[at : at + rows, :], gq_out[at : at + rows, :]
            if part is None:
                o_own[:, to] = attended
                gq_own[:, to] = gq
            else:
                part[:rows, to] = attended
                part[rows:, to] = gq
            at += rows
    start = (head * (KEY_VALUE_HEADS // head_count) + place[2]) * GROUP_WIDTH
    target = lanes(start, GROUP_WIDTH)
    copies = [
        pltpu.make_async_copy(o_own, o_all.at[:, target], copied.at[0]),
        pltpu.make_async_copy(gq_own, gq_all.at[:, target], copied.at[1]),
    ]
    for copy in copies:
        copy.start()
    gk = (gk * SCALE).astype(jnp.bfloat16)
    gv = gv.astype(jnp.bfloat16)
    for index, grad in enumerate((near_grad, far_grad)):
        here = slice(index * group_rows, (index + 1) * group_rows)
        grad[:group_rows, k_cols] = gk[here]
        grad[:group_rows, v_cols] = gv[here]
        rest = grad.shape[0] - group_rows
        grad[group_rows:, k_cols] = jnp.zeros((rest, width), jnp.bfloat16)
        grad[group_rows:, v_cols] = jnp.zeros((rest, width), jnp.bfloat16)
    for slot in range(slots):
        other, target = placed(slot)
        low = span + slot * BLK
        for index, grad in enumerate((near_grad, far_grad)):

            @pl.when(jnp.logical_and(listed[position, slot] >= 0, other == index))
            def _():
                grad[target, k_cols] = gk[low : low + BLK]
                grad[target, v_cols] = gv[low : low + BLK]

    for copy in copies:
        copy.wait()


def attention(listed, place, own, received, near, far, carried, shape, column):
    head_count, group_rows, store_rows, clean_rows, slots = shape
    rows = own.shape[0] // 2
    total = 2 * group_rows + slots * BLK
    stacked = HEADS_PER_GROUP * group_rows
    smem = pl.BlockSpec(memory_space=pltpu.SMEM)
    vmem = pl.BlockSpec(memory_space=pltpu.VMEM)
    hbm = pl.BlockSpec(memory_space=pl.ANY)
    kept = [i for i, array in enumerate(carried) if not isinstance(array, jax.ShapeDtypeStruct)]
    first_carried = 3 + len(received) + 2
    spaces = [hbm, hbm] + [vmem] * (len(carried) - 2)
    return pl.pallas_call(
        functools.partial(attention_kernel, shape, column, len(kept)),
        in_specs=[smem, smem] + [vmem] * (3 + len(received)) + [spaces[i] for i in kept],
        out_specs=spaces,
        scratch_shapes=[pltpu.VMEM((total, HEAD_SIZE), jnp.bfloat16)] * 2
        + [pltpu.VMEM((stacked, HEAD_SIZE), jnp.bfloat16)] * 4
        + [pltpu.VMEM((rows, GROUP_WIDTH), jnp.bfloat16)] * 2
        + [pltpu.SemaphoreType.DMA((2,))],
        out_shape=[jax.ShapeDtypeStruct(array.shape, jnp.bfloat16) for array in carried],
        input_output_aliases={first_carried + n: i for n, i in enumerate(kept)},
        compiler_params=pltpu.CompilerParams(vmem_limit_bytes=KERNEL_VMEM),
        cost_estimate=pl.CostEstimate(
            flops=8 * group_rows * HEADS_PER_GROUP * HEAD_SIZE * total,
            bytes_accessed=16 * group_rows * GROUP_WIDTH,
            transcendentals=group_rows * HEADS_PER_GROUP * total,
        ),
        name="span_attention",
    )(listed, place, own, *received, near, far, *[carried[i] for i in kept])


def unpack_kernel(head_count, groups, *refs):
    parts, outs = refs[:-4], refs[-4:]
    rows = outs[0].shape[0]
    half = outs[0].shape[1] // head_count
    width = HEAD_SIZE
    for step in range(head_count):
        source = lax.rem(lax.axis_index("head") + step, head_count)
        for group, members in enumerate(groups):
            part = parts[group * head_count + step]
            for at, member in enumerate(members):
                to = lanes(source * half + member * width, width)
                for index in range(2):
                    here = slice((2 * at + index) * width, (2 * at + index + 1) * width)
                    outs[index][:, to] = part[:rows, here]
                    outs[2 + index][:, to] = part[rows:, here]


def unpacked(head_count, groups, grads, rows, clean_rows):
    vmem = pl.BlockSpec(memory_space=pltpu.VMEM)
    parts = [part for chunk in grads for part in chunk]
    width = KEY_VALUE_HEADS * HEAD_SIZE
    return pl.pallas_call(
        functools.partial(unpack_kernel, head_count, groups),
        in_specs=[vmem] * len(parts),
        out_specs=[vmem] * 4,
        out_shape=[jax.ShapeDtypeStruct((rows, width), jnp.bfloat16)] * 2
        + [jax.ShapeDtypeStruct((clean_rows, width), jnp.bfloat16)] * 2,
        name="unpack_gradients",
    )(*parts)


def shards(
    queries,
    noisy_token_keys,
    noisy_token_values,
    clean_token_keys,
    clean_token_values,
    output_gradient,
    history_list,
):
    ctx_count = lax.axis_size("ctx")
    head_count = lax.axis_size("head")
    head = lax.axis_index("head")
    place = jnp.stack([lax.axis_index("ctx"), head]).astype(jnp.int32)
    rows = queries.shape[0]
    clean_rows = clean_token_keys.shape[0]
    store_rows = clean_rows * head_count
    group_rows = rows * head_count
    slots = ctx_count - 2
    per_device = KEY_VALUE_HEADS // head_count
    everything = list(range(per_device))
    half = max(1, per_device // 2)
    key_groups = [g for g in (everything[:half], everything[half:]) if g]
    grad_groups = key_groups
    ask_groups = send_groups = [[m] for m in everything]
    depth = ctx_count // 4
    steps = range(1, head_count)
    row_order = lax.rem(head - jnp.arange(head_count, dtype=jnp.int32) + head_count, head_count)

    def by_block(store):
        if clean_rows >= BLK:
            return store
        return store.reshape(head_count, clean_rows, -1)[row_order].reshape(store.shape)

    packs = packed(
        head_count,
        key_groups,
        noisy_token_keys,
        noisy_token_values,
        clean_token_keys,
        clean_token_values,
    )

    asks = query_blocks(head_count, queries, output_gradient)

    def swap_keys(index):
        return [packs[index][0]] + [shifted(packs[index][step], step) for step in steps]

    def swap_queries(member):
        return [shifted(asks[member][step], step) for step in steps]

    def stored(parts):
        return by_block(jnp.concatenate([part[rows:] for part in parts], 0))

    def along(store):
        return [flipped(store, z << 2) for z in range(1, depth)]

    def joined(parts, line):
        return jnp.concatenate([part[:rows] for part in parts] + [line], 0)

    def summed(pair, low, high):
        return pair[0][low:high].astype(jnp.float32) + pair[1][low:high].astype(jnp.float32)

    middle = group_rows + depth * store_rows
    end = middle + depth * store_rows

    def to_cross(pair):
        return summed(pair, middle, end).astype(jnp.bfloat16)

    def line_of(pair, other):
        return summed(pair, group_rows, middle) + other.astype(jnp.float32)

    def back_along(line):
        gives = [line[z * store_rows : (z + 1) * store_rows] for z in range(depth)]
        return gives[0], [
            flipped(give.astype(jnp.bfloat16), z << 2) for z, give in enumerate(gives[1:], 1)
        ]

    def added(keep, others):
        for other in others:
            keep = keep + other.astype(jnp.float32)
        return keep

    together = lax.optimization_barrier
    def swap_heads(noisy_sum, store_sum):
        if clean_rows < BLK:
            store_sum = store_sum.reshape(head_count, clean_rows, -1)[row_order].reshape(
                store_sum.shape
            )
        store_sum = store_sum.astype(jnp.bfloat16)
        noisy_sum = noisy_sum.astype(jnp.bfloat16)
        mixed = [
            jnp.concatenate(
                [
                    noisy_sum[step * rows : (step + 1) * rows],
                    store_sum[step * clean_rows : (step + 1) * clean_rows],
                ],
                0,
            )
            for step in range(head_count)
        ]
        return [mixed[0]] + [shifted(mixed[step], -step) for step in steps]

    shape = (head_count, group_rows, store_rows, clean_rows, slots)
    received = {}
    two = len(key_groups) > 1
    parts = swap_keys(0)
    store = stored(parts)
    others = along(store)
    if two:
        asks[0], parts = together((asks[0], parts))
    received[0] = swap_queries(0)
    line = jnp.concatenate([store, *others], 0)
    crossing = flipped(line, 2)
    if two:
        packs[1], received[0], others = together((packs[1], received[0], others))
        later_parts = swap_keys(1)
        asks[1], later_parts = together((asks[1], later_parts))
        received[1] = swap_queries(1)
        later_store = stored(later_parts)
        later_others = along(later_store)
    near = joined(parts, jnp.concatenate([line, crossing], 0))
    if two:
        near, asks[2], later_parts = together((near, asks[2], later_parts))
        received[2] = swap_queries(2)
    keys = {0: (near, flipped(near, 1))}
    outputs = [jax.ShapeDtypeStruct(queries.shape, jnp.bfloat16)] * 2
    sent = []
    held = []
    returned = None

    def group_of(groups, member):
        return next(i for i, group in enumerate(groups) if member in group)

    for member in everything:
        k = group_of(key_groups, member)
        first = member == key_groups[k][0]
        last = member == key_groups[k][-1]
        sends = [jax.ShapeDtypeStruct((2 * rows, GROUP_WIDTH), jnp.bfloat16)] * (head_count - 1)
        if first:
            width = len(key_groups[k]) * 2 * HEAD_SIZE
            pair = [jax.ShapeDtypeStruct((near.shape[0], width), jnp.bfloat16)] * 2
        column = key_groups[k].index(member)
        outputs[0], outputs[1], *rest = attention(
            history_list,
            jnp.concatenate([place, jnp.array([member], jnp.int32)]),
            asks[member][0],
            received[member],
            *keys[k],
            [*outputs, *sends, *pair],
            shape,
            column,
        )
        sends, pair = rest[:-2], rest[-2:]
        if two and member == 0:
            outputs, later_others, received[1], received[2] = together(
                (outputs, later_others, received[1], received[2])
            )
            later_line = jnp.concatenate([later_store, *later_others], 0)
            crossing = flipped(later_line, 2)
        if two and member == 1:
            outputs, crossing = together((outputs, crossing))
            near = joined(later_parts, jnp.concatenate([later_line, crossing], 0))
            keys[1] = (near, flipped(near, 1))
        if member + 3 < per_device:
            asks, outputs = together((asks, outputs))
            received[member + 3] = swap_queries(member + 3)
        if two and member == 1:
            pair, received[3] = together((pair, received[3]))
        held.append(sends)
        if two and member == half:
            held[half - 1], outputs = together((held[half - 1], outputs))
        if not two or member >= half - 1:
            later = len(held) if member == everything[-1] else len(held) - 1
            for block_set in held[len(sent) : later]:
                sent.append([shifted(block, -step) for step, block in zip(steps, block_set)])
        if two and member == half and not last:
            first_other, outputs, sent[0] = together((first_other, outputs, sent[0]))
            returned = back_along(line_of(first_pair, first_other))
        if last and member == everything[-1]:
            if two:
                if returned is None:
                    returned = back_along(line_of(first_pair, first_other))
                returned, pair, sent[half - 1] = together((returned, pair, sent[half - 1]))
            last_pair = (pair[0], flipped(pair[1], 1))
        elif last:
            first_pair = (pair[0], flipped(pair[1], 1))
            first_pair, outputs = together((first_pair, outputs))
            first_other = flipped(to_cross(first_pair), 2)
    grads = []
    if two:
        sent[:half], _ = together((sent[:half], last_pair))
        grads.append(swap_heads(summed(first_pair, 0, group_rows), added(*returned)))
    keep, others = back_along(line_of(last_pair, flipped(to_cross(last_pair), 2)))
    line = added(keep, others)
    if two:
        line, sent[half:] = together((line, sent[half:]))
    grads.append(swap_heads(summed(last_pair, 0, group_rows), line))
    attended, query_grad = outputs
    for group, blocks in zip(send_groups, sent):
        for step, block in zip(steps, blocks):
            source = lax.rem(head + step, head_count)
            start = (source * per_device + group[0]) * GROUP_WIDTH
            attended = lax.dynamic_update_slice_in_dim(attended, block[:rows], start, 1)
            query_grad = lax.dynamic_update_slice_in_dim(query_grad, block[rows:], start, 1)
    finished = unpacked(head_count, grad_groups, grads, rows, clean_rows)
    return (attended, query_grad, *finished)


def solution(mesh):
    split = P(("ctx", "head"), None)
    return jax.shard_map(
        shards,
        mesh=mesh,
        in_specs=(split, split, split, split, split, split, P()),
        out_specs=(split,) * 6,
        check_vma=False,
    )
```

```python
import functools

import jax
import jax.numpy as jnp
from jax import lax
from jax.experimental import pallas as pl
from jax.experimental.pallas import tpu as pltpu
from jax.sharding import PartitionSpec as P

QUERY_HEADS = 48
KEY_VALUE_HEADS = 8
HEAD_SIZE = 128
BLK = 32
HEADS_PER_GROUP = QUERY_HEADS // KEY_VALUE_HEADS
GROUP_WIDTH = HEADS_PER_GROUP * HEAD_SIZE
SCALE = HEAD_SIZE**-0.5
LOG2E = 1.4426950408889634

NEG_FILL = -1e30
SLICE_ROWS = 256
KERNEL_VMEM = 16 * 2**20


def flipped(block, bits):
    count = lax.axis_size("ctx")
    return lax.ppermute(block, "ctx", [(i, i ^ bits) for i in range(count)])


def shifted(block, step):
    count = lax.axis_size("head")
    return lax.ppermute(block, "head", [(i, (i + step) % count) for i in range(count)])


def dot(a, b, contract):
    return lax.dot_general(
        a, b, ((contract[:1], contract[1:]), ((), ())), preferred_element_type=jnp.float32
    )


def lanes(start, size):
    return pl.ds(pl.multiple_of(start, HEAD_SIZE), size)


def pack_kernel(head_count, groups, k_noisy, v_noisy, k_clean, v_clean, *outs):
    rows = k_noisy.shape[0]
    half = k_noisy.shape[1] // head_count
    width = HEAD_SIZE
    for index, group in enumerate(groups):
        for step in range(head_count):
            out = outs[index * head_count + step]
            target = lax.rem(lax.axis_index("head") + step, head_count)
            for at, member in enumerate(group):
                source = lanes(target * half + member * width, width)
                for n, (noisy, clean) in enumerate(((k_noisy, k_clean), (v_noisy, v_clean))):
                    to = slice((2 * at + n) * width, (2 * at + n + 1) * width)
                    out[:rows, to] = noisy[:, source]
                    out[rows:, to] = clean[:, source]


def packed(head_count, groups, k_noisy, v_noisy, k_clean, v_clean):
    vmem = pl.BlockSpec(memory_space=pltpu.VMEM)
    rows = k_noisy.shape[0] + k_clean.shape[0]
    shapes = [
        jax.ShapeDtypeStruct((rows, 2 * HEAD_SIZE * len(group)), jnp.bfloat16)
        for group in groups
        for _ in range(head_count)
    ]
    outs = pl.pallas_call(
        functools.partial(pack_kernel, head_count, groups),
        in_specs=[vmem] * 4,
        out_specs=[vmem] * len(shapes),
        out_shape=shapes,
        name="pack_keys_values",
    )(k_noisy, v_noisy, k_clean, v_clean)
    return [outs[i * head_count : (i + 1) * head_count] for i in range(len(groups))]


def stack_kernel(head_count, q, g, *outs):
    rows = q.shape[0]
    per_device = KEY_VALUE_HEADS // head_count
    for member in range(per_device):
        for step in range(head_count):
            out = outs[member * head_count + step]
            target = lax.rem(lax.axis_index("head") + step, head_count)
            source = lanes((target * per_device + member) * GROUP_WIDTH, GROUP_WIDTH)
            out[:rows, :] = q[:, source]
            out[rows:, :] = g[:, source]


def query_blocks(head_count, q, g):
    vmem = pl.BlockSpec(memory_space=pltpu.VMEM)
    shape = jax.ShapeDtypeStruct((2 * q.shape[0], GROUP_WIDTH), jnp.bfloat16)
    outs = pl.pallas_call(
        functools.partial(stack_kernel, head_count),
        in_specs=[vmem] * 2,
        out_specs=[vmem] * KEY_VALUE_HEADS,
        out_shape=[shape] * KEY_VALUE_HEADS,
        name="stack_queries",
    )(q, g)
    return [outs[i : i + head_count] for i in range(0, KEY_VALUE_HEADS, head_count)]


def attention_kernel(shape, column, kept, listed, place, own, *refs):
    head_count, group_rows, store_rows, clean_rows, slots = shape
    received, refs = refs[: head_count - 1], refs[head_count - 1 :]
    near, far, *refs = refs
    o_all, gq_all, *refs = refs[kept:]
    sends, refs = refs[: head_count - 1], refs[head_count - 1 :]
    near_grad, far_grad, k_all, v_all, q_all, g_all, o_out, gq_out, o_own, gq_own, copied = refs
    rows = own.shape[0] // 2
    width = HEAD_SIZE
    position, head = place[0], place[1]
    k_cols = slice(2 * column * width, (2 * column + 1) * width)
    v_cols = slice((2 * column + 1) * width, (2 * column + 2) * width)
    depth = (near.shape[0] - group_rows) // (2 * store_rows)

    def placed(slot):
        apart = lax.bitwise_xor(position, slot)
        store = lax.bitwise_and(lax.shift_right_logical(apart, 1), 1) * depth
        store = store + lax.shift_right_logical(apart, 2)
        block = jnp.maximum(listed[position, slot], 0)
        if clean_rows >= BLK:
            owner = lax.div(block * BLK, clean_rows)
            step = lax.rem(head - owner + head_count, head_count)
            inside = step * clean_rows + block * BLK - owner * clean_rows
        else:
            inside = block * BLK
        start = pl.multiple_of(group_rows + store * store_rows + inside, BLK)
        return lax.bitwise_and(apart, 1), pl.ds(start, BLK)

    k_all[:group_rows, :] = near[:group_rows, k_cols]
    v_all[:group_rows, :] = near[:group_rows, v_cols]
    k_all[group_rows : 2 * group_rows, :] = far[:group_rows, k_cols]
    v_all[group_rows : 2 * group_rows, :] = far[:group_rows, v_cols]
    span = 2 * group_rows
    total = span + slots * BLK
    for slot in range(slots):
        other, source = placed(slot)
        to = slice(span + slot * BLK, span + (slot + 1) * BLK)
        k_all[to, :] = jnp.where(other == 1, far[source, k_cols], near[source, k_cols])
        v_all[to, :] = jnp.where(other == 1, far[source, v_cols], near[source, v_cols])
    at = 0
    for r in range(HEADS_PER_GROUP):
        for part in (own, *received):
            q_all[at : at + rows, :] = part[:rows, r * width : (r + 1) * width]
            g_all[at : at + rows, :] = part[rows:, r * width : (r + 1) * width]
            at += rows

    keys = k_all[...]
    values = v_all[...]
    keys_t = keys.T
    values_t = values.T
    biases = [
        jnp.where(listed[position, slot] >= 0, 0.0, NEG_FILL).astype(jnp.float32)
        for slot in range(slots)
    ]
    cuts = list(range(0, at - SLICE_ROWS + 1, SLICE_ROWS)) + [at]
    slices = [slice(low, high) for low, high in zip(cuts, cuts[1:])]

    def products(piece):
        query, upstream = q_all[piece, :], g_all[piece, :]
        return query, upstream, dot(keys, query, (1, 1)), dot(values, upstream, (1, 1))

    def softmax(scores, dprob):
        scores = scores * (SCALE * LOG2E)
        pieces = [scores[:span]]
        for slot in range(slots):
            low = span + slot * BLK
            pieces.append(scores[low : low + BLK] + biases[slot])
        scores = jnp.concatenate(pieces, 0)
        top = jnp.max(scores, 0, keepdims=True)
        unscaled = jnp.exp2(scores - top)
        prob = unscaled * (1.0 / jnp.sum(unscaled, 0, keepdims=True))
        row_dot = jnp.sum(prob * dprob, 0, keepdims=True)
        return prob.astype(jnp.bfloat16), (prob * (dprob - row_dot)).astype(jnp.bfloat16)

    gk = jnp.zeros((total, width), jnp.float32)
    gv = jnp.zeros((total, width), jnp.float32)
    ahead = products(slices[0])
    for index, piece in enumerate(slices):
        query, upstream, scores, dprob = ahead
        if index + 1 < len(slices):
            ahead = products(slices[index + 1])
        weights, dscore = softmax(scores, dprob)
        o_out[piece, :] = dot(values_t, weights, (1, 0)).astype(jnp.bfloat16).T
        gq_out[piece, :] = (dot(keys_t, dscore, (1, 0)) * SCALE).astype(jnp.bfloat16).T
        gk = gk + dot(dscore, query, (1, 0))
        gv = gv + dot(weights, upstream, (1, 0))
    at = 0
    for r in range(HEADS_PER_GROUP):
        to = slice(r * width, (r + 1) * width)
        for part in (None, *sends):
            attended, gq = o_out[at : at + rows, :], gq_out[at : at + rows, :]
            if part is None:
                o_own[:, to] = attended
                gq_own[:, to] = gq
            else:
                part[:rows, to] = attended
                part[rows:, to] = gq
            at += rows
    start = (head * (KEY_VALUE_HEADS // head_count) + place[2]) * GROUP_WIDTH
    target = lanes(start, GROUP_WIDTH)
    copies = [
        pltpu.make_async_copy(o_own, o_all.at[:, target], copied.at[0]),
        pltpu.make_async_copy(gq_own, gq_all.at[:, target], copied.at[1]),
    ]
    for copy in copies:
        copy.start()
    gk = (gk * SCALE).astype(jnp.bfloat16)
    gv = gv.astype(jnp.bfloat16)
    for index, grad in enumerate((near_grad, far_grad)):
        here = slice(index * group_rows, (index + 1) * group_rows)
        grad[:group_rows, k_cols] = gk[here]
        grad[:group_rows, v_cols] = gv[here]
        rest = grad.shape[0] - group_rows
        grad[group_rows:, k_cols] = jnp.zeros((rest, width), jnp.bfloat16)
        grad[group_rows:, v_cols] = jnp.zeros((rest, width), jnp.bfloat16)
    for slot in range(slots):
        other, target = placed(slot)
        low = span + slot * BLK
        for index, grad in enumerate((near_grad, far_grad)):

            @pl.when(jnp.logical_and(listed[position, slot] >= 0, other == index))
            def _():
                grad[target, k_cols] = gk[low : low + BLK]
                grad[target, v_cols] = gv[low : low + BLK]

    for copy in copies:
        copy.wait()


def attention(listed, place, own, received, near, far, carried, shape, column):
    head_count, group_rows, store_rows, clean_rows, slots = shape
    rows = own.shape[0] // 2
    total = 2 * group_rows + slots * BLK
    stacked = HEADS_PER_GROUP * group_rows
    smem = pl.BlockSpec(memory_space=pltpu.SMEM)
    vmem = pl.BlockSpec(memory_space=pltpu.VMEM)
    hbm = pl.BlockSpec(memory_space=pl.ANY)
    kept = [i for i, array in enumerate(carried) if not isinstance(array, jax.ShapeDtypeStruct)]
    first_carried = 3 + len(received) + 2
    spaces = [hbm, hbm] + [vmem] * (len(carried) - 2)
    return pl.pallas_call(
        functools.partial(attention_kernel, shape, column, len(kept)),
        in_specs=[smem, smem] + [vmem] * (3 + len(received)) + [spaces[i] for i in kept],
        out_specs=spaces,
        scratch_shapes=[pltpu.VMEM((total, HEAD_SIZE), jnp.bfloat16)] * 2
        + [pltpu.VMEM((stacked, HEAD_SIZE), jnp.bfloat16)] * 4
        + [pltpu.VMEM((rows, GROUP_WIDTH), jnp.bfloat16)] * 2
        + [pltpu.SemaphoreType.DMA((2,))],
        out_shape=[jax.ShapeDtypeStruct(array.shape, jnp.bfloat16) for array in carried],
        input_output_aliases={first_carried + n: i for n, i in enumerate(kept)},
        compiler_params=pltpu.CompilerParams(vmem_limit_bytes=KERNEL_VMEM),
        cost_estimate=pl.CostEstimate(
            flops=8 * group_rows * HEADS_PER_GROUP * HEAD_SIZE * total,
            bytes_accessed=16 * group_rows * GROUP_WIDTH,
            transcendentals=group_rows * HEADS_PER_GROUP * total,
        ),
        name="span_attention",
    )(listed, place, own, *received, near, far, *[carried[i] for i in kept])


def unpack_kernel(head_count, groups, *refs):
    parts, outs = refs[:-4], refs[-4:]
    rows = outs[0].shape[0]
    half = outs[0].shape[1] // head_count
    width = HEAD_SIZE
    for step in range(head_count):
        source = lax.rem(lax.axis_index("head") + step, head_count)
        for group, members in enumerate(groups):
            part = parts[group * head_count + step]
            for at, member in enumerate(members):
                to = lanes(source * half + member * width, width)
                for index in range(2):
                    here = slice((2 * at + index) * width, (2 * at + index + 1) * width)
                    outs[index][:, to] = part[:rows, here]
                    outs[2 + index][:, to] = part[rows:, here]


def unpacked(head_count, groups, grads, rows, clean_rows):
    vmem = pl.BlockSpec(memory_space=pltpu.VMEM)
    parts = [part for chunk in grads for part in chunk]
    width = KEY_VALUE_HEADS * HEAD_SIZE
    return pl.pallas_call(
        functools.partial(unpack_kernel, head_count, groups),
        in_specs=[vmem] * len(parts),
        out_specs=[vmem] * 4,
        out_shape=[jax.ShapeDtypeStruct((rows, width), jnp.bfloat16)] * 2
        + [jax.ShapeDtypeStruct((clean_rows, width), jnp.bfloat16)] * 2,
        name="unpack_gradients",
    )(*parts)


def shards(
    queries,
    noisy_token_keys,
    noisy_token_values,
    clean_token_keys,
    clean_token_values,
    output_gradient,
    history_list,
):
    ctx_count = lax.axis_size("ctx")
    head_count = lax.axis_size("head")
    head = lax.axis_index("head")
    place = jnp.stack([lax.axis_index("ctx"), head]).astype(jnp.int32)
    rows = queries.shape[0]
    clean_rows = clean_token_keys.shape[0]
    store_rows = clean_rows * head_count
    group_rows = rows * head_count
    slots = ctx_count - 2
    per_device = KEY_VALUE_HEADS // head_count
    everything = list(range(per_device))
    half = max(1, per_device // 2)
    key_groups = [g for g in (everything[:half], everything[half:]) if g]
    grad_groups = key_groups
    ask_groups = send_groups = [[m] for m in everything]
    depth = ctx_count // 4
    steps = range(1, head_count)
    row_order = lax.rem(head - jnp.arange(head_count, dtype=jnp.int32) + head_count, head_count)

    def by_block(store):
        if clean_rows >= BLK:
            return store
        return store.reshape(head_count, clean_rows, -1)[row_order].reshape(store.shape)

    packs = packed(
        head_count,
        key_groups,
        noisy_token_keys,
        noisy_token_values,
        clean_token_keys,
        clean_token_values,
    )

    asks = query_blocks(head_count, queries, output_gradient)

    def swap_keys(index):
        return [packs[index][0]] + [shifted(packs[index][step], step) for step in steps]

    def swap_queries(member):
        return [shifted(asks[member][step], step) for step in steps]

    def stored(parts):
        return by_block(jnp.concatenate([part[rows:] for part in parts], 0))

    def along(store):
        return [flipped(store, z << 2) for z in range(1, depth)]

    def joined(parts, line):
        return jnp.concatenate([part[:rows] for part in parts] + [line], 0)

    def summed(near_grad, from_core):
        total = near_grad.astype(jnp.float32) + from_core.astype(jnp.float32)
        return total[:group_rows], total[group_rows:]

    def halved(line):
        middle = line.shape[0] // 2
        return line[:middle], flipped(line[middle:].astype(jnp.bfloat16), 2)

    def back_along(line):
        gives = [line[z * store_rows : (z + 1) * store_rows] for z in range(depth)]
        return gives[0], [
            flipped(give.astype(jnp.bfloat16), z << 2) for z, give in enumerate(gives[1:], 1)
        ]

    def added(keep, others):
        for other in others:
            keep = keep + other.astype(jnp.float32)
        return keep

    together = lax.optimization_barrier
    def swap_heads(noisy_sum, store_sum):
        if clean_rows < BLK:
            store_sum = store_sum.reshape(head_count, clean_rows, -1)[row_order].reshape(
                store_sum.shape
            )
        store_sum = store_sum.astype(jnp.bfloat16)
        noisy_sum = noisy_sum.astype(jnp.bfloat16)
        mixed = [
            jnp.concatenate(
                [
                    noisy_sum[step * rows : (step + 1) * rows],
                    store_sum[step * clean_rows : (step + 1) * clean_rows],
                ],
                0,
            )
            for step in range(head_count)
        ]
        return [mixed[0]] + [shifted(mixed[step], -step) for step in steps]

    shape = (head_count, group_rows, store_rows, clean_rows, slots)
    received = {}
    two = len(key_groups) > 1
    parts = swap_keys(0)
    store = stored(parts)
    others = along(store)
    if two:
        asks[0], parts = together((asks[0], parts))
    received[0] = swap_queries(0)
    line = jnp.concatenate([store, *others], 0)
    crossing = flipped(line, 2)
    if two:
        packs[1], received[0], others = together((packs[1], received[0], others))
        later_parts = swap_keys(1)
        asks[1], later_parts = together((asks[1], later_parts))
        received[1] = swap_queries(1)
        later_store = stored(later_parts)
        later_others = along(later_store)
    near = joined(parts, jnp.concatenate([line, crossing], 0))
    if two:
        near, asks[2], later_parts = together((near, asks[2], later_parts))
        received[2] = swap_queries(2)
    keys = {0: (near, flipped(near, 1))}
    outputs = [jax.ShapeDtypeStruct(queries.shape, jnp.bfloat16)] * 2
    sent = []
    held = []
    waiting = []

    def group_of(groups, member):
        return next(i for i, group in enumerate(groups) if member in group)

    for member in everything:
        k = group_of(key_groups, member)
        first = member == key_groups[k][0]
        last = member == key_groups[k][-1]
        sends = [jax.ShapeDtypeStruct((2 * rows, GROUP_WIDTH), jnp.bfloat16)] * (head_count - 1)
        if first:
            width = len(key_groups[k]) * 2 * HEAD_SIZE
            pair = [jax.ShapeDtypeStruct((near.shape[0], width), jnp.bfloat16)] * 2
        column = key_groups[k].index(member)
        outputs[0], outputs[1], *rest = attention(
            history_list,
            jnp.concatenate([place, jnp.array([member], jnp.int32)]),
            asks[member][0],
            received[member],
            *keys[k],
            [*outputs, *sends, *pair],
            shape,
            column,
        )
        sends, pair = rest[:-2], rest[-2:]
        if two and member == 0:
            outputs, later_others, received[1], received[2] = together(
                (outputs, later_others, received[1], received[2])
            )
            later_line = jnp.concatenate([later_store, *later_others], 0)
            crossing = flipped(later_line, 2)
        if two and member == 1:
            outputs, crossing = together((outputs, crossing))
            near = joined(later_parts, jnp.concatenate([later_line, crossing], 0))
            keys[1] = (near, flipped(near, 1))
        if member + 3 < per_device:
            asks, outputs = together((asks, outputs))
            received[member + 3] = swap_queries(member + 3)
        if two and member == 1:
            pair, received[3] = together((pair, received[3]))
        held.append(sends)
        if two and member == half:
            held[half - 1], outputs = together((held[half - 1], outputs))
        if not two or member >= half - 1:
            later = len(held) if member == everything[-1] else len(held) - 1
            for block_set in held[len(sent) : later]:
                sent.append([shifted(block, -step) for step, block in zip(steps, block_set)])
        if waiting and not last:
            noisy_sum, line = summed(*waiting[0])
            line, outputs = together((line, outputs))
            waiting[0] = (noisy_sum, *halved(line))
            outputs, sent[0] = together((outputs, sent[0]))
        if last:
            if waiting:
                waiting[0], pair, sent[:half] = together((waiting[0], pair, sent[:half]))
            waiting.append((pair[0], flipped(pair[1], 1)))
    grads = []
    if two:
        first_noisy, keep, other = waiting[0]
        keep, others = back_along(added(keep, [other]))
    noisy_sum, line = summed(*waiting[-1])
    last_keep, last_other = halved(line)
    if two:
        last_other, others, sent[:half] = together((last_other, others, sent[:half]))
        grads.append(swap_heads(first_noisy, added(keep, others)))
    last_keep, last_others = back_along(added(last_keep, [last_other]))
    line = added(last_keep, last_others)
    if two:
        line, sent[half:] = together((line, sent[half:]))
    grads.append(swap_heads(noisy_sum, line))
    attended, query_grad = outputs
    for group, blocks in zip(send_groups, sent):
        for step, block in zip(steps, blocks):
            source = lax.rem(head + step, head_count)
            start = (source * per_device + group[0]) * GROUP_WIDTH
            attended = lax.dynamic_update_slice_in_dim(attended, block[:rows], start, 1)
            query_grad = lax.dynamic_update_slice_in_dim(query_grad, block[rows:], start, 1)
    finished = unpacked(head_count, grad_groups, grads, rows, clean_rows)
    return (attended, query_grad, *finished)


def solution(mesh):
    split = P(("ctx", "head"), None)
    return jax.shard_map(
        shards,
        mesh=mesh,
        in_specs=(split, split, split, split, split, split, P()),
        out_specs=(split,) * 6,
        check_vma=False,
    )
```

```python
import functools

import jax
import jax.numpy as jnp
from jax import lax
from jax.experimental import pallas as pl
from jax.experimental.pallas import tpu as pltpu
from jax.sharding import PartitionSpec as P

QUERY_HEADS = 48
KEY_VALUE_HEADS = 8
HEAD_SIZE = 128
BLK = 32
HEADS_PER_GROUP = QUERY_HEADS // KEY_VALUE_HEADS
GROUP_WIDTH = HEADS_PER_GROUP * HEAD_SIZE
SCALE = HEAD_SIZE**-0.5
LOG2E = 1.4426950408889634

NEG_FILL = -1e30
SLICE_ROWS = 256
KERNEL_VMEM = 16 * 2**20


def flipped(block, bits):
    count = lax.axis_size("ctx")
    return lax.ppermute(block, "ctx", [(i, i ^ bits) for i in range(count)])


def shifted(block, step):
    count = lax.axis_size("head")
    return lax.ppermute(block, "head", [(i, (i + step) % count) for i in range(count)])


def dot(a, b, contract):
    return lax.dot_general(
        a, b, ((contract[:1], contract[1:]), ((), ())), preferred_element_type=jnp.float32
    )


def lanes(start, size):
    return pl.ds(pl.multiple_of(start, HEAD_SIZE), size)


def pack_kernel(head_count, groups, k_noisy, v_noisy, k_clean, v_clean, *outs):
    rows = k_noisy.shape[0]
    half = k_noisy.shape[1] // head_count
    width = HEAD_SIZE
    for index, group in enumerate(groups):
        for step in range(head_count):
            out = outs[index * head_count + step]
            target = lax.rem(lax.axis_index("head") + step, head_count)
            for at, member in enumerate(group):
                source = lanes(target * half + member * width, width)
                for n, (noisy, clean) in enumerate(((k_noisy, k_clean), (v_noisy, v_clean))):
                    to = slice((2 * at + n) * width, (2 * at + n + 1) * width)
                    out[:rows, to] = noisy[:, source]
                    out[rows:, to] = clean[:, source]


def packed(head_count, groups, k_noisy, v_noisy, k_clean, v_clean):
    vmem = pl.BlockSpec(memory_space=pltpu.VMEM)
    rows = k_noisy.shape[0] + k_clean.shape[0]
    shapes = [
        jax.ShapeDtypeStruct((rows, 2 * HEAD_SIZE * len(group)), jnp.bfloat16)
        for group in groups
        for _ in range(head_count)
    ]
    outs = pl.pallas_call(
        functools.partial(pack_kernel, head_count, groups),
        in_specs=[vmem] * 4,
        out_specs=[vmem] * len(shapes),
        out_shape=shapes,
        name="pack_keys_values",
    )(k_noisy, v_noisy, k_clean, v_clean)
    return [outs[i * head_count : (i + 1) * head_count] for i in range(len(groups))]


def stack_kernel(head_count, q, g, *outs):
    rows = q.shape[0]
    per_device = KEY_VALUE_HEADS // head_count
    for member in range(per_device):
        for step in range(head_count):
            out = outs[member * head_count + step]
            target = lax.rem(lax.axis_index("head") + step, head_count)
            source = lanes((target * per_device + member) * GROUP_WIDTH, GROUP_WIDTH)
            out[:rows, :] = q[:, source]
            out[rows:, :] = g[:, source]


def query_blocks(head_count, q, g):
    vmem = pl.BlockSpec(memory_space=pltpu.VMEM)
    shape = jax.ShapeDtypeStruct((2 * q.shape[0], GROUP_WIDTH), jnp.bfloat16)
    outs = pl.pallas_call(
        functools.partial(stack_kernel, head_count),
        in_specs=[vmem] * 2,
        out_specs=[vmem] * KEY_VALUE_HEADS,
        out_shape=[shape] * KEY_VALUE_HEADS,
        name="stack_queries",
    )(q, g)
    return [outs[i : i + head_count] for i in range(0, KEY_VALUE_HEADS, head_count)]


def attention_kernel(shape, column, kept, listed, place, own, *refs):
    head_count, group_rows, store_rows, clean_rows, slots = shape
    received, refs = refs[: head_count - 1], refs[head_count - 1 :]
    near, far, *refs = refs
    o_all, gq_all, *refs = refs[kept:]
    sends, refs = refs[: head_count - 1], refs[head_count - 1 :]
    near_grad, far_grad, k_all, v_all, q_all, g_all, o_out, gq_out, o_own, gq_own, copied = refs
    rows = own.shape[0] // 2
    width = HEAD_SIZE
    position, head = place[0], place[1]
    k_cols = slice(2 * column * width, (2 * column + 1) * width)
    v_cols = slice((2 * column + 1) * width, (2 * column + 2) * width)
    depth = (near.shape[0] - group_rows) // (2 * store_rows)

    def placed(slot):
        apart = lax.bitwise_xor(position, slot)
        store = lax.bitwise_and(lax.shift_right_logical(apart, 1), 1) * depth
        store = store + lax.shift_right_logical(apart, 2)
        block = jnp.maximum(listed[position, slot], 0)
        if clean_rows >= BLK:
            owner = lax.div(block * BLK, clean_rows)
            step = lax.rem(head - owner + head_count, head_count)
            inside = step * clean_rows + block * BLK - owner * clean_rows
        else:
            inside = block * BLK
        start = pl.multiple_of(group_rows + store * store_rows + inside, BLK)
        return lax.bitwise_and(apart, 1), pl.ds(start, BLK)

    k_all[:group_rows, :] = near[:group_rows, k_cols]
    v_all[:group_rows, :] = near[:group_rows, v_cols]
    k_all[group_rows : 2 * group_rows, :] = far[:group_rows, k_cols]
    v_all[group_rows : 2 * group_rows, :] = far[:group_rows, v_cols]
    span = 2 * group_rows
    total = span + slots * BLK
    for slot in range(slots):
        other, source = placed(slot)
        to = slice(span + slot * BLK, span + (slot + 1) * BLK)
        k_all[to, :] = jnp.where(other == 1, far[source, k_cols], near[source, k_cols])
        v_all[to, :] = jnp.where(other == 1, far[source, v_cols], near[source, v_cols])
    at = 0
    for r in range(HEADS_PER_GROUP):
        for part in (own, *received):
            q_all[at : at + rows, :] = part[:rows, r * width : (r + 1) * width]
            g_all[at : at + rows, :] = part[rows:, r * width : (r + 1) * width]
            at += rows

    keys = k_all[...]
    values = v_all[...]
    keys_t = keys.T
    values_t = values.T
    biases = [
        jnp.where(listed[position, slot] >= 0, 0.0, NEG_FILL).astype(jnp.float32)
        for slot in range(slots)
    ]
    cuts = list(range(0, at - SLICE_ROWS + 1, SLICE_ROWS)) + [at]
    slices = [slice(low, high) for low, high in zip(cuts, cuts[1:])]

    def products(piece):
        query, upstream = q_all[piece, :], g_all[piece, :]
        return query, upstream, dot(keys, query, (1, 1)), dot(values, upstream, (1, 1))

    def softmax(scores, dprob):
        scores = scores * (SCALE * LOG2E)
        pieces = [scores[:span]]
        for slot in range(slots):
            low = span + slot * BLK
            pieces.append(scores[low : low + BLK] + biases[slot])
        scores = jnp.concatenate(pieces, 0)
        top = jnp.max(scores, 0, keepdims=True)
        unscaled = jnp.exp2(scores - top)
        prob = unscaled * (1.0 / jnp.sum(unscaled, 0, keepdims=True))
        row_dot = jnp.sum(prob * dprob, 0, keepdims=True)
        return prob.astype(jnp.bfloat16), (prob * (dprob - row_dot)).astype(jnp.bfloat16)

    gk = jnp.zeros((total, width), jnp.float32)
    gv = jnp.zeros((total, width), jnp.float32)
    ahead = products(slices[0])
    for index, piece in enumerate(slices):
        query, upstream, scores, dprob = ahead
        if index + 1 < len(slices):
            ahead = products(slices[index + 1])
        weights, dscore = softmax(scores, dprob)
        o_out[piece, :] = dot(values_t, weights, (1, 0)).astype(jnp.bfloat16).T
        gq_out[piece, :] = (dot(keys_t, dscore, (1, 0)) * SCALE).astype(jnp.bfloat16).T
        gk = gk + dot(dscore, query, (1, 0))
        gv = gv + dot(weights, upstream, (1, 0))
    at = 0
    for r in range(HEADS_PER_GROUP):
        to = slice(r * width, (r + 1) * width)
        for part in (None, *sends):
            attended, gq = o_out[at : at + rows, :], gq_out[at : at + rows, :]
            if part is None:
                o_own[:, to] = attended
                gq_own[:, to] = gq
            else:
                part[:rows, to] = attended
                part[rows:, to] = gq
            at += rows
    start = (head * (KEY_VALUE_HEADS // head_count) + place[2]) * GROUP_WIDTH
    target = lanes(start, GROUP_WIDTH)
    copies = [
        pltpu.make_async_copy(o_own, o_all.at[:, target], copied.at[0]),
        pltpu.make_async_copy(gq_own, gq_all.at[:, target], copied.at[1]),
    ]
    for copy in copies:
        copy.start()
    gk = (gk * SCALE).astype(jnp.bfloat16)
    gv = gv.astype(jnp.bfloat16)
    for index, grad in enumerate((near_grad, far_grad)):
        here = slice(index * group_rows, (index + 1) * group_rows)
        grad[:group_rows, k_cols] = gk[here]
        grad[:group_rows, v_cols] = gv[here]
        rest = grad.shape[0] - group_rows
        grad[group_rows:, k_cols] = jnp.zeros((rest, width), jnp.bfloat16)
        grad[group_rows:, v_cols] = jnp.zeros((rest, width), jnp.bfloat16)
    for slot in range(slots):
        other, target = placed(slot)
        low = span + slot * BLK
        for index, grad in enumerate((near_grad, far_grad)):

            @pl.when(jnp.logical_and(listed[position, slot] >= 0, other == index))
            def _():
                grad[target, k_cols] = gk[low : low + BLK]
                grad[target, v_cols] = gv[low : low + BLK]

    for copy in copies:
        copy.wait()


def attention(listed, place, own, received, near, far, carried, shape, column):
    head_count, group_rows, store_rows, clean_rows, slots = shape
    rows = own.shape[0] // 2
    total = 2 * group_rows + slots * BLK
    stacked = HEADS_PER_GROUP * group_rows
    smem = pl.BlockSpec(memory_space=pltpu.SMEM)
    vmem = pl.BlockSpec(memory_space=pltpu.VMEM)
    hbm = pl.BlockSpec(memory_space=pl.ANY)
    kept = [i for i, array in enumerate(carried) if not isinstance(array, jax.ShapeDtypeStruct)]
    first_carried = 3 + len(received) + 2
    spaces = [hbm, hbm] + [vmem] * (len(carried) - 2)
    return pl.pallas_call(
        functools.partial(attention_kernel, shape, column, len(kept)),
        in_specs=[smem, smem] + [vmem] * (3 + len(received)) + [spaces[i] for i in kept],
        out_specs=spaces,
        scratch_shapes=[pltpu.VMEM((total, HEAD_SIZE), jnp.bfloat16)] * 2
        + [pltpu.VMEM((stacked, HEAD_SIZE), jnp.bfloat16)] * 4
        + [pltpu.VMEM((rows, GROUP_WIDTH), jnp.bfloat16)] * 2
        + [pltpu.SemaphoreType.DMA((2,))],
        out_shape=[jax.ShapeDtypeStruct(array.shape, jnp.bfloat16) for array in carried],
        input_output_aliases={first_carried + n: i for n, i in enumerate(kept)},
        compiler_params=pltpu.CompilerParams(vmem_limit_bytes=KERNEL_VMEM),
        cost_estimate=pl.CostEstimate(
            flops=8 * group_rows * HEADS_PER_GROUP * HEAD_SIZE * total,
            bytes_accessed=16 * group_rows * GROUP_WIDTH,
            transcendentals=group_rows * HEADS_PER_GROUP * total,
        ),
        name="span_attention",
    )(listed, place, own, *received, near, far, *[carried[i] for i in kept])


def unpack_kernel(head_count, groups, *refs):
    parts, outs = refs[:-4], refs[-4:]
    rows = outs[0].shape[0]
    half = outs[0].shape[1] // head_count
    width = HEAD_SIZE
    for step in range(head_count):
        source = lax.rem(lax.axis_index("head") + step, head_count)
        for group, members in enumerate(groups):
            part = parts[group * head_count + step]
            for at, member in enumerate(members):
                to = lanes(source * half + member * width, width)
                for index in range(2):
                    here = slice((2 * at + index) * width, (2 * at + index + 1) * width)
                    outs[index][:, to] = part[:rows, here]
                    outs[2 + index][:, to] = part[rows:, here]


def unpacked(head_count, groups, grads, rows, clean_rows):
    vmem = pl.BlockSpec(memory_space=pltpu.VMEM)
    parts = [part for chunk in grads for part in chunk]
    width = KEY_VALUE_HEADS * HEAD_SIZE
    return pl.pallas_call(
        functools.partial(unpack_kernel, head_count, groups),
        in_specs=[vmem] * len(parts),
        out_specs=[vmem] * 4,
        out_shape=[jax.ShapeDtypeStruct((rows, width), jnp.bfloat16)] * 2
        + [jax.ShapeDtypeStruct((clean_rows, width), jnp.bfloat16)] * 2,
        name="unpack_gradients",
    )(*parts)


def shards(
    queries,
    noisy_token_keys,
    noisy_token_values,
    clean_token_keys,
    clean_token_values,
    output_gradient,
    history_list,
):
    ctx_count = lax.axis_size("ctx")
    head_count = lax.axis_size("head")
    head = lax.axis_index("head")
    place = jnp.stack([lax.axis_index("ctx"), head]).astype(jnp.int32)
    rows = queries.shape[0]
    clean_rows = clean_token_keys.shape[0]
    store_rows = clean_rows * head_count
    group_rows = rows * head_count
    slots = ctx_count - 2
    per_device = KEY_VALUE_HEADS // head_count
    everything = list(range(per_device))
    half = max(1, per_device // 2)
    key_groups = [g for g in (everything[:half], everything[half:]) if g]
    grad_groups = key_groups
    ask_groups = send_groups = [[m] for m in everything]
    depth = ctx_count // 4
    steps = range(1, head_count)
    row_order = lax.rem(head - jnp.arange(head_count, dtype=jnp.int32) + head_count, head_count)

    def by_block(store):
        if clean_rows >= BLK:
            return store
        return store.reshape(head_count, clean_rows, -1)[row_order].reshape(store.shape)

    packs = packed(
        head_count,
        key_groups,
        noisy_token_keys,
        noisy_token_values,
        clean_token_keys,
        clean_token_values,
    )

    asks = query_blocks(head_count, queries, output_gradient)

    def swap_keys(index):
        return [packs[index][0]] + [shifted(packs[index][step], step) for step in steps]

    def swap_queries(member):
        return [shifted(asks[member][step], step) for step in steps]

    def stored(parts):
        return by_block(jnp.concatenate([part[rows:] for part in parts], 0))

    def along(store):
        return [flipped(store, z << 2) for z in range(1, depth)]

    def joined(parts, line):
        return jnp.concatenate([part[:rows] for part in parts] + [line], 0)

    def summed(near_grad, from_core):
        total = near_grad.astype(jnp.float32) + from_core.astype(jnp.float32)
        return total[:group_rows], total[group_rows:]

    def halved(line, bits=2):
        middle = line.shape[0] // 2
        return line[:middle], flipped(line[middle:].astype(jnp.bfloat16), bits)

    def back_along(line):
        gives = [line[z * store_rows : (z + 1) * store_rows] for z in range(depth)]
        return gives[0], [
            flipped(give.astype(jnp.bfloat16), z << 2) for z, give in enumerate(gives[1:], 1)
        ]

    def added(keep, others):
        for other in others:
            keep = keep + other.astype(jnp.float32)
        return keep

    together = lax.optimization_barrier
    def swap_heads(noisy_sum, store_sum):
        if clean_rows < BLK:
            store_sum = store_sum.reshape(head_count, clean_rows, -1)[row_order].reshape(
                store_sum.shape
            )
        store_sum = store_sum.astype(jnp.bfloat16)
        noisy_sum = noisy_sum.astype(jnp.bfloat16)
        mixed = [
            jnp.concatenate(
                [
                    noisy_sum[step * rows : (step + 1) * rows],
                    store_sum[step * clean_rows : (step + 1) * clean_rows],
                ],
                0,
            )
            for step in range(head_count)
        ]
        return [mixed[0]] + [shifted(mixed[step], -step) for step in steps]

    shape = (head_count, group_rows, store_rows, clean_rows, slots)
    received = {}
    two = len(key_groups) > 1
    parts = swap_keys(0)
    store = stored(parts)
    others = along(store)
    if two:
        asks[0], parts = together((asks[0], parts))
    received[0] = swap_queries(0)
    line = jnp.concatenate([store, *others], 0)
    crossing = flipped(line, 2)
    if two:
        packs[1], received[0], others = together((packs[1], received[0], others))
        later_parts = swap_keys(1)
        asks[1], later_parts = together((asks[1], later_parts))
        received[1] = swap_queries(1)
        later_store = stored(later_parts)
        later_others = along(later_store)
    near = joined(parts, jnp.concatenate([line, crossing], 0))
    if two:
        near, asks[2], later_parts = together((near, asks[2], later_parts))
        received[2] = swap_queries(2)
    keys = {0: (near, flipped(near, 1))}
    outputs = [jax.ShapeDtypeStruct(queries.shape, jnp.bfloat16)] * 2
    sent = []
    held = []
    waiting = []

    def group_of(groups, member):
        return next(i for i, group in enumerate(groups) if member in group)

    for member in everything:
        k = group_of(key_groups, member)
        first = member == key_groups[k][0]
        last = member == key_groups[k][-1]
        sends = [jax.ShapeDtypeStruct((2 * rows, GROUP_WIDTH), jnp.bfloat16)] * (head_count - 1)
        if first:
            width = len(key_groups[k]) * 2 * HEAD_SIZE
            pair = [jax.ShapeDtypeStruct((near.shape[0], width), jnp.bfloat16)] * 2
        column = key_groups[k].index(member)
        outputs[0], outputs[1], *rest = attention(
            history_list,
            jnp.concatenate([place, jnp.array([member], jnp.int32)]),
            asks[member][0],
            received[member],
            *keys[k],
            [*outputs, *sends, *pair],
            shape,
            column,
        )
        sends, pair = rest[:-2], rest[-2:]
        if two and member == 0:
            outputs, later_others, received[1], received[2] = together(
                (outputs, later_others, received[1], received[2])
            )
            later_line = jnp.concatenate([later_store, *later_others], 0)
            crossing = flipped(later_line, 2)
        if two and member == 1:
            outputs, crossing = together((outputs, crossing))
            near = joined(later_parts, jnp.concatenate([later_line, crossing], 0))
            keys[1] = (near, flipped(near, 1))
        if member + 3 < per_device:
            asks, outputs = together((asks, outputs))
            received[member + 3] = swap_queries(member + 3)
        if two and member == 1:
            pair, received[3] = together((pair, received[3]))
        held.append(sends)
        if two and member == half:
            held[half - 1], outputs = together((held[half - 1], outputs))
        if not two or member >= half - 1:
            later = len(held) if member == everything[-1] else len(held) - 1
            for block_set in held[len(sent) : later]:
                sent.append([shifted(block, -step) for step, block in zip(steps, block_set)])
        if waiting and not last:
            noisy_sum, line = summed(*waiting[0])
            line, outputs = together((line, outputs))
            waiting[0] = (noisy_sum, *halved(line))
            outputs, sent[0] = together((outputs, sent[0]))
        if last:
            if waiting:
                kept_sums, other = waiting[0][:2], waiting[0][2]
                other, pair, sent[:half] = together((other, pair, sent[:half]))
                waiting[0] = (*kept_sums, other)
            waiting.append((pair[0], flipped(pair[1], 1)))
    grads = []
    if two:
        first_noisy, keep, other = waiting[0]
        first_line = added(keep, [other])
        strides = [1 << bit for bit in range(ctx_count.bit_length() - 2, 1, -1)]
        if strides:
            keep, other = halved(first_line, strides[0])
    noisy_sum, line = summed(*waiting[-1])
    last_keep, last_other = halved(line)
    if two:
        arrived = sent[: half + 1]
        last_other, other, arrived = together((last_other, other, arrived))
        sent[: half + 1] = arrived
    last_keep, last_others = back_along(added(last_keep, [last_other]))
    if two:
        for stride in strides[1:]:
            keep, other = halved(added(keep, [other]), stride)
        if strides:
            other, _ = together((other, last_others[0]))
            first_line = added(keep, [other])
        grads.append(swap_heads(first_noisy, first_line))
    line = added(last_keep, last_others)
    if two:
        line, sent[-1] = together((line, sent[-1]))
    grads.append(swap_heads(noisy_sum, line))
    attended, query_grad = outputs
    for group, blocks in zip(send_groups, sent):
        for step, block in zip(steps, blocks):
            source = lax.rem(head + step, head_count)
            start = (source * per_device + group[0]) * GROUP_WIDTH
            attended = lax.dynamic_update_slice_in_dim(attended, block[:rows], start, 1)
            query_grad = lax.dynamic_update_slice_in_dim(query_grad, block[rows:], start, 1)
    finished = unpacked(head_count, grad_groups, grads, rows, clean_rows)
    return (attended, query_grad, *finished)


def solution(mesh):
    split = P(("ctx", "head"), None)
    return jax.shard_map(
        shards,
        mesh=mesh,
        in_specs=(split, split, split, split, split, split, P()),
        out_specs=(split,) * 6,
        check_vma=False,
    )
```

```python
import functools

import jax
import jax.numpy as jnp
from jax import lax
from jax.experimental import pallas as pl
from jax.experimental.pallas import tpu as pltpu
from jax.sharding import PartitionSpec as P

QUERY_HEADS = 48
KEY_VALUE_HEADS = 8
HEAD_SIZE = 128
BLK = 32
HEADS_PER_GROUP = QUERY_HEADS // KEY_VALUE_HEADS
GROUP_WIDTH = HEADS_PER_GROUP * HEAD_SIZE
SCALE = HEAD_SIZE**-0.5
LOG2E = 1.4426950408889634

NEG_FILL = -1e30
SLICE_ROWS = 512
KERNEL_VMEM = 32 * 2**20


def flipped(block, bits):
    count = lax.axis_size("ctx")
    return lax.ppermute(block, "ctx", [(i, i ^ bits) for i in range(count)])


def shifted(block, step):
    count = lax.axis_size("head")
    return lax.ppermute(block, "head", [(i, (i + step) % count) for i in range(count)])


def dot(a, b, contract):
    return lax.dot_general(
        a, b, ((contract[:1], contract[1:]), ((), ())), preferred_element_type=jnp.float32
    )


def lanes(start, size):
    return pl.ds(pl.multiple_of(start, HEAD_SIZE), size)


def pack_kernel(head_count, groups, k_noisy, v_noisy, k_clean, v_clean, *outs):
    rows = k_noisy.shape[0]
    half = k_noisy.shape[1] // head_count
    width = HEAD_SIZE
    for index, group in enumerate(groups):
        for step in range(head_count):
            out = outs[index * head_count + step]
            target = lax.rem(lax.axis_index("head") + step, head_count)
            for at, member in enumerate(group):
                source = lanes(target * half + member * width, width)
                for n, (noisy, clean) in enumerate(((k_noisy, k_clean), (v_noisy, v_clean))):
                    to = slice((2 * at + n) * width, (2 * at + n + 1) * width)
                    out[:rows, to] = noisy[:, source]
                    out[rows:, to] = clean[:, source]


def packed(head_count, groups, k_noisy, v_noisy, k_clean, v_clean):
    vmem = pl.BlockSpec(memory_space=pltpu.VMEM)
    rows = k_noisy.shape[0] + k_clean.shape[0]
    shapes = [
        jax.ShapeDtypeStruct((rows, 2 * HEAD_SIZE * len(group)), jnp.bfloat16)
        for group in groups
        for _ in range(head_count)
    ]
    outs = pl.pallas_call(
        functools.partial(pack_kernel, head_count, groups),
        in_specs=[vmem] * 4,
        out_specs=[vmem] * len(shapes),
        out_shape=shapes,
        name="pack_keys_values",
    )(k_noisy, v_noisy, k_clean, v_clean)
    return [outs[i * head_count : (i + 1) * head_count] for i in range(len(groups))]


def stack_kernel(head_count, q, g, *outs):
    rows = q.shape[0]
    per_device = KEY_VALUE_HEADS // head_count
    for member in range(per_device):
        for step in range(head_count):
            out = outs[member * head_count + step]
            target = lax.rem(lax.axis_index("head") + step, head_count)
            source = lanes((target * per_device + member) * GROUP_WIDTH, GROUP_WIDTH)
            out[:rows, :] = q[:, source]
            out[rows:, :] = g[:, source]


def query_blocks(head_count, q, g):
    vmem = pl.BlockSpec(memory_space=pltpu.VMEM)
    shape = jax.ShapeDtypeStruct((2 * q.shape[0], GROUP_WIDTH), jnp.bfloat16)
    outs = pl.pallas_call(
        functools.partial(stack_kernel, head_count),
        in_specs=[vmem] * 2,
        out_specs=[vmem] * KEY_VALUE_HEADS,
        out_shape=[shape] * KEY_VALUE_HEADS,
        name="stack_queries",
    )(q, g)
    return [outs[i : i + head_count] for i in range(0, KEY_VALUE_HEADS, head_count)]


def attention_kernel(shape, column, kept, listed, place, own, *refs):
    head_count, group_rows, store_rows, clean_rows, slots = shape
    received, refs = refs[: head_count - 1], refs[head_count - 1 :]
    near, far, *refs = refs
    o_all, gq_all, *refs = refs[kept:]
    sends, refs = refs[: head_count - 1], refs[head_count - 1 :]
    near_grad, far_grad, k_all, v_all, q_all, g_all, o_out, gq_out, o_own, gq_own, copied = refs
    rows = own.shape[0] // 2
    width = HEAD_SIZE
    position, head = place[0], place[1]
    k_cols = slice(2 * column * width, (2 * column + 1) * width)
    v_cols = slice((2 * column + 1) * width, (2 * column + 2) * width)
    depth = (near.shape[0] - group_rows) // (2 * store_rows)

    def placed(slot):
        apart = lax.bitwise_xor(position, slot)
        store = lax.bitwise_and(lax.shift_right_logical(apart, 1), 1) * depth
        store = store + lax.shift_right_logical(apart, 2)
        block = jnp.maximum(listed[position, slot], 0)
        if clean_rows >= BLK:
            owner = lax.div(block * BLK, clean_rows)
            step = lax.rem(head - owner + head_count, head_count)
            inside = step * clean_rows + block * BLK - owner * clean_rows
        else:
            inside = block * BLK
        start = pl.multiple_of(group_rows + store * store_rows + inside, BLK)
        return lax.bitwise_and(apart, 1), pl.ds(start, BLK)

    k_all[:group_rows, :] = near[:group_rows, k_cols]
    v_all[:group_rows, :] = near[:group_rows, v_cols]
    k_all[group_rows : 2 * group_rows, :] = far[:group_rows, k_cols]
    v_all[group_rows : 2 * group_rows, :] = far[:group_rows, v_cols]
    span = 2 * group_rows
    total = span + slots * BLK
    for slot in range(slots):
        other, source = placed(slot)
        to = slice(span + slot * BLK, span + (slot + 1) * BLK)
        k_all[to, :] = jnp.where(other == 1, far[source, k_cols], near[source, k_cols])
        v_all[to, :] = jnp.where(other == 1, far[source, v_cols], near[source, v_cols])
    at = 0
    for r in range(HEADS_PER_GROUP):
        for part in (own, *received):
            q_all[at : at + rows, :] = part[:rows, r * width : (r + 1) * width]
            g_all[at : at + rows, :] = part[rows:, r * width : (r + 1) * width]
            at += rows

    keys = k_all[...]
    values = v_all[...]
    keys_t = keys.T
    values_t = values.T
    biases = [
        jnp.where(listed[position, slot] >= 0, 0.0, NEG_FILL).astype(jnp.float32)
        for slot in range(slots)
    ]
    cuts = list(range(0, at - SLICE_ROWS + 1, SLICE_ROWS)) + [at]
    slices = [slice(low, high) for low, high in zip(cuts, cuts[1:])]

    def products(piece):
        query, upstream = q_all[piece, :], g_all[piece, :]
        return query, upstream, dot(keys, query, (1, 1)), dot(values, upstream, (1, 1))

    def softmax(scores, dprob):
        scores = scores * (SCALE * LOG2E)
        pieces = [scores[:span]]
        for slot in range(slots):
            low = span + slot * BLK
            pieces.append(scores[low : low + BLK] + biases[slot])
        scores = jnp.concatenate(pieces, 0)
        top = jnp.max(scores, 0, keepdims=True)
        unscaled = jnp.exp2(scores - top)
        prob = unscaled * (1.0 / jnp.sum(unscaled, 0, keepdims=True))
        row_dot = jnp.sum(prob * dprob, 0, keepdims=True)
        return prob.astype(jnp.bfloat16), (prob * (dprob - row_dot)).astype(jnp.bfloat16)

    gk = jnp.zeros((total, width), jnp.float32)
    gv = jnp.zeros((total, width), jnp.float32)
    ahead = products(slices[0])
    for index, piece in enumerate(slices):
        query, upstream, scores, dprob = ahead
        if index + 1 < len(slices):
            ahead = products(slices[index + 1])
        weights, dscore = softmax(scores, dprob)
        o_out[piece, :] = dot(values_t, weights, (1, 0)).astype(jnp.bfloat16).T
        gq_out[piece, :] = (dot(keys_t, dscore, (1, 0)) * SCALE).astype(jnp.bfloat16).T
        gk = gk + dot(dscore, query, (1, 0))
        gv = gv + dot(weights, upstream, (1, 0))
    at = 0
    for r in range(HEADS_PER_GROUP):
        to = slice(r * width, (r + 1) * width)
        for part in (None, *sends):
            attended, gq = o_out[at : at + rows, :], gq_out[at : at + rows, :]
            if part is None:
                o_own[:, to] = attended
                gq_own[:, to] = gq
            else:
                part[:rows, to] = attended
                part[rows:, to] = gq
            at += rows
    start = (head * (KEY_VALUE_HEADS // head_count) + place[2]) * GROUP_WIDTH
    target = lanes(start, GROUP_WIDTH)
    copies = [
        pltpu.make_async_copy(o_own, o_all.at[:, target], copied.at[0]),
        pltpu.make_async_copy(gq_own, gq_all.at[:, target], copied.at[1]),
    ]
    for copy in copies:
        copy.start()
    gk = (gk * SCALE).astype(jnp.bfloat16)
    gv = gv.astype(jnp.bfloat16)
    for index, grad in enumerate((near_grad, far_grad)):
        here = slice(index * group_rows, (index + 1) * group_rows)
        grad[:group_rows, k_cols] = gk[here]
        grad[:group_rows, v_cols] = gv[here]
        rest = grad.shape[0] - group_rows
        grad[group_rows:, k_cols] = jnp.zeros((rest, width), jnp.bfloat16)
        grad[group_rows:, v_cols] = jnp.zeros((rest, width), jnp.bfloat16)
    for slot in range(slots):
        other, target = placed(slot)
        low = span + slot * BLK
        for index, grad in enumerate((near_grad, far_grad)):

            @pl.when(jnp.logical_and(listed[position, slot] >= 0, other == index))
            def _():
                grad[target, k_cols] = gk[low : low + BLK]
                grad[target, v_cols] = gv[low : low + BLK]

    for copy in copies:
        copy.wait()


def attention(listed, place, own, received, near, far, carried, shape, column):
    head_count, group_rows, store_rows, clean_rows, slots = shape
    rows = own.shape[0] // 2
    total = 2 * group_rows + slots * BLK
    stacked = HEADS_PER_GROUP * group_rows
    smem = pl.BlockSpec(memory_space=pltpu.SMEM)
    vmem = pl.BlockSpec(memory_space=pltpu.VMEM)
    hbm = pl.BlockSpec(memory_space=pl.ANY)
    kept = [i for i, array in enumerate(carried) if not isinstance(array, jax.ShapeDtypeStruct)]
    first_carried = 3 + len(received) + 2
    spaces = [hbm, hbm] + [vmem] * (len(carried) - 2)
    return pl.pallas_call(
        functools.partial(attention_kernel, shape, column, len(kept)),
        in_specs=[smem, smem] + [vmem] * (3 + len(received)) + [spaces[i] for i in kept],
        out_specs=spaces,
        scratch_shapes=[pltpu.VMEM((total, HEAD_SIZE), jnp.bfloat16)] * 2
        + [pltpu.VMEM((stacked, HEAD_SIZE), jnp.bfloat16)] * 4
        + [pltpu.VMEM((rows, GROUP_WIDTH), jnp.bfloat16)] * 2
        + [pltpu.SemaphoreType.DMA((2,))],
        out_shape=[jax.ShapeDtypeStruct(array.shape, jnp.bfloat16) for array in carried],
        input_output_aliases={first_carried + n: i for n, i in enumerate(kept)},
        compiler_params=pltpu.CompilerParams(vmem_limit_bytes=KERNEL_VMEM),
        cost_estimate=pl.CostEstimate(
            flops=8 * group_rows * HEADS_PER_GROUP * HEAD_SIZE * total,
            bytes_accessed=16 * group_rows * GROUP_WIDTH,
            transcendentals=group_rows * HEADS_PER_GROUP * total,
        ),
        name="span_attention",
    )(listed, place, own, *received, near, far, *[carried[i] for i in kept])


def unpack_kernel(head_count, groups, *refs):
    parts, outs = refs[:-4], refs[-4:]
    rows = outs[0].shape[0]
    half = outs[0].shape[1] // head_count
    width = HEAD_SIZE
    for step in range(head_count):
        source = lax.rem(lax.axis_index("head") + step, head_count)
        for group, members in enumerate(groups):
            part = parts[group * head_count + step]
            for at, member in enumerate(members):
                to = lanes(source * half + member * width, width)
                for index in range(2):
                    here = slice((2 * at + index) * width, (2 * at + index + 1) * width)
                    outs[index][:, to] = part[:rows, here]
                    outs[2 + index][:, to] = part[rows:, here]


def unpacked(head_count, groups, grads, rows, clean_rows):
    vmem = pl.BlockSpec(memory_space=pltpu.VMEM)
    parts = [part for chunk in grads for part in chunk]
    width = KEY_VALUE_HEADS * HEAD_SIZE
    return pl.pallas_call(
        functools.partial(unpack_kernel, head_count, groups),
        in_specs=[vmem] * len(parts),
        out_specs=[vmem] * 4,
        out_shape=[jax.ShapeDtypeStruct((rows, width), jnp.bfloat16)] * 2
        + [jax.ShapeDtypeStruct((clean_rows, width), jnp.bfloat16)] * 2,
        name="unpack_gradients",
    )(*parts)


def shards(
    queries,
    noisy_token_keys,
    noisy_token_values,
    clean_token_keys,
    clean_token_values,
    output_gradient,
    history_list,
):
    ctx_count = lax.axis_size("ctx")
    head_count = lax.axis_size("head")
    head = lax.axis_index("head")
    place = jnp.stack([lax.axis_index("ctx"), head]).astype(jnp.int32)
    rows = queries.shape[0]
    clean_rows = clean_token_keys.shape[0]
    store_rows = clean_rows * head_count
    group_rows = rows * head_count
    slots = ctx_count - 2
    per_device = KEY_VALUE_HEADS // head_count
    everything = list(range(per_device))
    half = max(1, per_device // 2)
    key_groups = [g for g in (everything[:half], everything[half:]) if g]
    grad_groups = key_groups
    ask_groups = send_groups = [[m] for m in everything]
    depth = ctx_count // 4
    steps = range(1, head_count)
    row_order = lax.rem(head - jnp.arange(head_count, dtype=jnp.int32) + head_count, head_count)

    def by_block(store):
        if clean_rows >= BLK:
            return store
        return store.reshape(head_count, clean_rows, -1)[row_order].reshape(store.shape)

    packs = packed(
        head_count,
        key_groups,
        noisy_token_keys,
        noisy_token_values,
        clean_token_keys,
        clean_token_values,
    )

    asks = query_blocks(head_count, queries, output_gradient)

    def swap_keys(index):
        return [packs[index][0]] + [shifted(packs[index][step], step) for step in steps]

    def swap_queries(member):
        return [shifted(asks[member][step], step) for step in steps]

    def stored(parts):
        return by_block(jnp.concatenate([part[rows:] for part in parts], 0))

    def along(store):
        return [flipped(store, z << 2) for z in range(1, depth)]

    def joined(parts, line):
        return jnp.concatenate([part[:rows] for part in parts] + [line], 0)

    def summed(near_grad, from_core):
        total = near_grad.astype(jnp.float32) + from_core.astype(jnp.float32)
        return total[:group_rows], total[group_rows:]

    def halved(line):
        middle = line.shape[0] // 2
        return line[:middle], flipped(line[middle:].astype(jnp.bfloat16), 2)

    def back_along(line):
        gives = [line[z * store_rows : (z + 1) * store_rows] for z in range(depth)]
        return gives[0], [
            flipped(give.astype(jnp.bfloat16), z << 2) for z, give in enumerate(gives[1:], 1)
        ]

    def added(keep, others):
        for other in others:
            keep = keep + other.astype(jnp.float32)
        return keep

    together = lax.optimization_barrier
    def swap_heads(noisy_sum, store_sum):
        if clean_rows < BLK:
            store_sum = store_sum.reshape(head_count, clean_rows, -1)[row_order].reshape(
                store_sum.shape
            )
        store_sum = store_sum.astype(jnp.bfloat16)
        noisy_sum = noisy_sum.astype(jnp.bfloat16)
        mixed = [
            jnp.concatenate(
                [
                    noisy_sum[step * rows : (step + 1) * rows],
                    store_sum[step * clean_rows : (step + 1) * clean_rows],
                ],
                0,
            )
            for step in range(head_count)
        ]
        return [mixed[0]] + [shifted(mixed[step], -step) for step in steps]

    shape = (head_count, group_rows, store_rows, clean_rows, slots)
    received = {}
    two = len(key_groups) > 1
    parts = swap_keys(0)
    store = stored(parts)
    others = along(store)
    if two:
        asks[0], parts = together((asks[0], parts))
    received[0] = swap_queries(0)
    line = jnp.concatenate([store, *others], 0)
    crossing = flipped(line, 2)
    if two:
        packs[1], received[0], others = together((packs[1], received[0], others))
        later_parts = swap_keys(1)
        asks[1], _ = together((asks[1], received[0]))
        received[1] = swap_queries(1)
        later_store = stored(later_parts)
        later_others = along(later_store)
    near = joined(parts, jnp.concatenate([line, crossing], 0))
    if two:
        asks[2], _ = together((asks[2], near))
        received[2] = swap_queries(2)
    keys = {0: (near, flipped(near, 1))}
    outputs = [jax.ShapeDtypeStruct(queries.shape, jnp.bfloat16)] * 2
    sent = []
    held = []
    waiting = []

    def group_of(groups, member):
        return next(i for i, group in enumerate(groups) if member in group)

    for member in everything:
        k = group_of(key_groups, member)
        first = member == key_groups[k][0]
        last = member == key_groups[k][-1]
        sends = [jax.ShapeDtypeStruct((2 * rows, GROUP_WIDTH), jnp.bfloat16)] * (head_count - 1)
        if first:
            width = len(key_groups[k]) * 2 * HEAD_SIZE
            pair = [jax.ShapeDtypeStruct((near.shape[0], width), jnp.bfloat16)] * 2
        column = key_groups[k].index(member)
        outputs[0], outputs[1], *rest = attention(
            history_list,
            jnp.concatenate([place, jnp.array([member], jnp.int32)]),
            asks[member][0],
            received[member],
            *keys[k],
            [*outputs, *sends, *pair],
            shape,
            column,
        )
        sends, pair = rest[:-2], rest[-2:]
        if two and member == 0:
            outputs, later_others, received[1], received[2] = together(
                (outputs, later_others, received[1], received[2])
            )
            later_line = jnp.concatenate([later_store, *later_others], 0)
            crossing = flipped(later_line, 2)
        if two and member == 1:
            outputs, crossing = together((outputs, crossing))
            near = joined(later_parts, jnp.concatenate([later_line, crossing], 0))
            keys[1] = (near, flipped(near, 1))
        if member + 3 < per_device:
            asks, outputs = together((asks, outputs))
            received[member + 3] = swap_queries(member + 3)
        if two and member == 1:
            pair, received[3] = together((pair, received[3]))
        held.append(sends)
        if two and member == half:
            held[half - 1], outputs = together((held[half - 1], outputs))
        if not two or member >= half - 1:
            later = len(held) if member == everything[-1] else len(held) - 1
            for block_set in held[len(sent) : later]:
                sent.append([shifted(block, -step) for step, block in zip(steps, block_set)])
        if waiting and not last:
            noisy_sum, line = summed(*waiting[0])
            line, outputs = together((line, outputs))
            waiting[0] = (noisy_sum, *halved(line))
            outputs, sent[0] = together((outputs, sent[0]))
        if last:
            if waiting:
                waiting[0], pair, sent[:half] = together((waiting[0], pair, sent[:half]))
            waiting.append((pair[0], flipped(pair[1], 1)))
    grads = []
    if two:
        first_noisy, keep, other = waiting[0]
        keep, others = back_along(added(keep, [other]))
    noisy_sum, line = summed(*waiting[-1])
    last_keep, last_other = halved(line)
    if two:
        last_other, others, sent[:half] = together((last_other, others, sent[:half]))
        grads.append(swap_heads(first_noisy, added(keep, others)))
    last_keep, last_others = back_along(added(last_keep, [last_other]))
    line = added(last_keep, last_others)
    if two:
        line, sent[half:] = together((line, sent[half:]))
    grads.append(swap_heads(noisy_sum, line))
    attended, query_grad = outputs
    for group, blocks in zip(send_groups, sent):
        for step, block in zip(steps, blocks):
            source = lax.rem(head + step, head_count)
            start = (source * per_device + group[0]) * GROUP_WIDTH
            attended = lax.dynamic_update_slice_in_dim(attended, block[:rows], start, 1)
            query_grad = lax.dynamic_update_slice_in_dim(query_grad, block[rows:], start, 1)
    finished = unpacked(head_count, grad_groups, grads, rows, clean_rows)
    return (attended, query_grad, *finished)


def solution(mesh):
    split = P(("ctx", "head"), None)
    return jax.shard_map(
        shards,
        mesh=mesh,
        in_specs=(split, split, split, split, split, split, P()),
        out_specs=(split,) * 6,
        check_vma=False,
    )
```

```python
import functools

import jax
import jax.numpy as jnp
from jax import lax
from jax.experimental import pallas as pl
from jax.experimental.pallas import tpu as pltpu
from jax.sharding import PartitionSpec as P

QUERY_HEADS = 48
KEY_VALUE_HEADS = 8
HEAD_SIZE = 128
BLK = 32
HEADS_PER_GROUP = QUERY_HEADS // KEY_VALUE_HEADS
GROUP_WIDTH = HEADS_PER_GROUP * HEAD_SIZE
SCALE = HEAD_SIZE**-0.5
LOG2E = 1.4426950408889634

NEG_FILL = -1e30
SLICE_ROWS = 512
KERNEL_VMEM = 32 * 2**20


def flipped(block, bits):
    count = lax.axis_size("ctx")
    return lax.ppermute(block, "ctx", [(i, i ^ bits) for i in range(count)])


def shifted(block, step):
    count = lax.axis_size("head")
    return lax.ppermute(block, "head", [(i, (i + step) % count) for i in range(count)])


def dot(a, b, contract):
    return lax.dot_general(
        a, b, ((contract[:1], contract[1:]), ((), ())), preferred_element_type=jnp.float32
    )


def lanes(start, size):
    return pl.ds(pl.multiple_of(start, HEAD_SIZE), size)


def pack_kernel(head_count, groups, k_noisy, v_noisy, k_clean, v_clean, *outs):
    rows = k_noisy.shape[0]
    half = k_noisy.shape[1] // head_count
    width = HEAD_SIZE
    for index, group in enumerate(groups):
        for step in range(head_count):
            out = outs[index * head_count + step]
            target = lax.rem(lax.axis_index("head") + step, head_count)
            for at, member in enumerate(group):
                source = lanes(target * half + member * width, width)
                for n, (noisy, clean) in enumerate(((k_noisy, k_clean), (v_noisy, v_clean))):
                    to = slice((2 * at + n) * width, (2 * at + n + 1) * width)
                    out[:rows, to] = noisy[:, source]
                    out[rows:, to] = clean[:, source]


def packed(head_count, groups, k_noisy, v_noisy, k_clean, v_clean):
    vmem = pl.BlockSpec(memory_space=pltpu.VMEM)
    rows = k_noisy.shape[0] + k_clean.shape[0]
    shapes = [
        jax.ShapeDtypeStruct((rows, 2 * HEAD_SIZE * len(group)), jnp.bfloat16)
        for group in groups
        for _ in range(head_count)
    ]
    outs = pl.pallas_call(
        functools.partial(pack_kernel, head_count, groups),
        in_specs=[vmem] * 4,
        out_specs=[vmem] * len(shapes),
        out_shape=shapes,
        name="pack_keys_values",
    )(k_noisy, v_noisy, k_clean, v_clean)
    return [outs[i * head_count : (i + 1) * head_count] for i in range(len(groups))]


def stack_kernel(head_count, q, g, *outs):
    rows = q.shape[0]
    per_device = KEY_VALUE_HEADS // head_count
    for member in range(per_device):
        for step in range(head_count):
            out = outs[member * head_count + step]
            target = lax.rem(lax.axis_index("head") + step, head_count)
            source = lanes((target * per_device + member) * GROUP_WIDTH, GROUP_WIDTH)
            out[:rows, :] = q[:, source]
            out[rows:, :] = g[:, source]


def query_blocks(head_count, q, g):
    vmem = pl.BlockSpec(memory_space=pltpu.VMEM)
    shape = jax.ShapeDtypeStruct((2 * q.shape[0], GROUP_WIDTH), jnp.bfloat16)
    outs = pl.pallas_call(
        functools.partial(stack_kernel, head_count),
        in_specs=[vmem] * 2,
        out_specs=[vmem] * KEY_VALUE_HEADS,
        out_shape=[shape] * KEY_VALUE_HEADS,
        name="stack_queries",
    )(q, g)
    return [outs[i : i + head_count] for i in range(0, KEY_VALUE_HEADS, head_count)]


def attention_kernel(shape, column, kept, listed, place, own, *refs):
    head_count, group_rows, store_rows, clean_rows, slots = shape
    received, refs = refs[: head_count - 1], refs[head_count - 1 :]
    near, far, *refs = refs
    o_all, gq_all, *refs = refs[kept:]
    sends, refs = refs[: head_count - 1], refs[head_count - 1 :]
    near_grad, far_grad, k_all, v_all, q_all, g_all, o_out, gq_out, o_own, gq_own, copied = refs
    rows = own.shape[0] // 2
    width = HEAD_SIZE
    position, head = place[0], place[1]
    k_cols = slice(2 * column * width, (2 * column + 1) * width)
    v_cols = slice((2 * column + 1) * width, (2 * column + 2) * width)
    depth = (near.shape[0] - group_rows) // (2 * store_rows)

    def placed(slot):
        apart = lax.bitwise_xor(position, slot)
        store = lax.bitwise_and(lax.shift_right_logical(apart, 1), 1) * depth
        store = store + lax.shift_right_logical(apart, 2)
        block = jnp.maximum(listed[position, slot], 0)
        if clean_rows >= BLK:
            owner = lax.div(block * BLK, clean_rows)
            step = lax.rem(head - owner + head_count, head_count)
            inside = step * clean_rows + block * BLK - owner * clean_rows
        else:
            inside = block * BLK
        start = pl.multiple_of(group_rows + store * store_rows + inside, BLK)
        return lax.bitwise_and(apart, 1), pl.ds(start, BLK)

    k_all[:group_rows, :] = near[:group_rows, k_cols]
    v_all[:group_rows, :] = near[:group_rows, v_cols]
    k_all[group_rows : 2 * group_rows, :] = far[:group_rows, k_cols]
    v_all[group_rows : 2 * group_rows, :] = far[:group_rows, v_cols]
    span = 2 * group_rows
    total = span + slots * BLK
    for slot in range(slots):
        other, source = placed(slot)
        to = slice(span + slot * BLK, span + (slot + 1) * BLK)
        k_all[to, :] = jnp.where(other == 1, far[source, k_cols], near[source, k_cols])
        v_all[to, :] = jnp.where(other == 1, far[source, v_cols], near[source, v_cols])
    at = 0
    for r in range(HEADS_PER_GROUP):
        for part in (own, *received):
            q_all[at : at + rows, :] = part[:rows, r * width : (r + 1) * width]
            g_all[at : at + rows, :] = part[rows:, r * width : (r + 1) * width]
            at += rows

    keys = k_all[...]
    values = v_all[...]
    keys_t = keys.T
    values_t = values.T
    biases = [
        jnp.where(listed[position, slot] >= 0, 0.0, NEG_FILL).astype(jnp.float32)
        for slot in range(slots)
    ]
    cuts = list(range(0, at - SLICE_ROWS + 1, SLICE_ROWS)) + [at]
    slices = [slice(low, high) for low, high in zip(cuts, cuts[1:])]

    def products(piece):
        query, upstream = q_all[piece, :], g_all[piece, :]
        return query, upstream, dot(keys, query, (1, 1)), dot(values, upstream, (1, 1))

    def softmax(scores, dprob):
        scores = scores * (SCALE * LOG2E)
        pieces = [scores[:span]]
        for slot in range(slots):
            low = span + slot * BLK
            pieces.append(scores[low : low + BLK] + biases[slot])
        scores = jnp.concatenate(pieces, 0)
        top = jnp.max(scores, 0, keepdims=True)
        unscaled = jnp.exp2(scores - top)
        prob = unscaled * (1.0 / jnp.sum(unscaled, 0, keepdims=True))
        row_dot = jnp.sum(prob * dprob, 0, keepdims=True)
        return prob.astype(jnp.bfloat16), (prob * (dprob - row_dot)).astype(jnp.bfloat16)

    gk = jnp.zeros((total, width), jnp.float32)
    gv = jnp.zeros((total, width), jnp.float32)
    ahead = products(slices[0])
    for index, piece in enumerate(slices):
        query, upstream, scores, dprob = ahead
        if index + 1 < len(slices):
            ahead = products(slices[index + 1])
        weights, dscore = softmax(scores, dprob)
        o_out[piece, :] = dot(values_t, weights, (1, 0)).astype(jnp.bfloat16).T
        gq_out[piece, :] = (dot(keys_t, dscore, (1, 0)) * SCALE).astype(jnp.bfloat16).T
        gk = gk + dot(dscore, query, (1, 0))
        gv = gv + dot(weights, upstream, (1, 0))
    at = 0
    for r in range(HEADS_PER_GROUP):
        to = slice(r * width, (r + 1) * width)
        for part in (None, *sends):
            attended, gq = o_out[at : at + rows, :], gq_out[at : at + rows, :]
            if part is None:
                o_own[:, to] = attended
                gq_own[:, to] = gq
            else:
                part[:rows, to] = attended
                part[rows:, to] = gq
            at += rows
    start = (head * (KEY_VALUE_HEADS // head_count) + place[2]) * GROUP_WIDTH
    target = lanes(start, GROUP_WIDTH)
    copies = [
        pltpu.make_async_copy(o_own, o_all.at[:, target], copied.at[0]),
        pltpu.make_async_copy(gq_own, gq_all.at[:, target], copied.at[1]),
    ]
    for copy in copies:
        copy.start()
    gk = (gk * SCALE).astype(jnp.bfloat16)
    gv = gv.astype(jnp.bfloat16)
    for index, grad in enumerate((near_grad, far_grad)):
        here = slice(index * group_rows, (index + 1) * group_rows)
        grad[:group_rows, k_cols] = gk[here]
        grad[:group_rows, v_cols] = gv[here]
        rest = grad.shape[0] - group_rows
        grad[group_rows:, k_cols] = jnp.zeros((rest, width), jnp.bfloat16)
        grad[group_rows:, v_cols] = jnp.zeros((rest, width), jnp.bfloat16)
    for slot in range(slots):
        other, target = placed(slot)
        low = span + slot * BLK
        for index, grad in enumerate((near_grad, far_grad)):

            @pl.when(jnp.logical_and(listed[position, slot] >= 0, other == index))
            def _():
                grad[target, k_cols] = gk[low : low + BLK]
                grad[target, v_cols] = gv[low : low + BLK]

    for copy in copies:
        copy.wait()


def attention(listed, place, own, received, near, far, carried, shape, column):
    head_count, group_rows, store_rows, clean_rows, slots = shape
    rows = own.shape[0] // 2
    total = 2 * group_rows + slots * BLK
    stacked = HEADS_PER_GROUP * group_rows
    smem = pl.BlockSpec(memory_space=pltpu.SMEM)
    vmem = pl.BlockSpec(memory_space=pltpu.VMEM)
    hbm = pl.BlockSpec(memory_space=pl.ANY)
    kept = [i for i, array in enumerate(carried) if not isinstance(array, jax.ShapeDtypeStruct)]
    first_carried = 3 + len(received) + 2
    spaces = [hbm, hbm] + [vmem] * (len(carried) - 2)
    return pl.pallas_call(
        functools.partial(attention_kernel, shape, column, len(kept)),
        in_specs=[smem, smem] + [vmem] * (3 + len(received)) + [spaces[i] for i in kept],
        out_specs=spaces,
        scratch_shapes=[pltpu.VMEM((total, HEAD_SIZE), jnp.bfloat16)] * 2
        + [pltpu.VMEM((stacked, HEAD_SIZE), jnp.bfloat16)] * 4
        + [pltpu.VMEM((rows, GROUP_WIDTH), jnp.bfloat16)] * 2
        + [pltpu.SemaphoreType.DMA((2,))],
        out_shape=[jax.ShapeDtypeStruct(array.shape, jnp.bfloat16) for array in carried],
        input_output_aliases={first_carried + n: i for n, i in enumerate(kept)},
        compiler_params=pltpu.CompilerParams(vmem_limit_bytes=KERNEL_VMEM),
        cost_estimate=pl.CostEstimate(
            flops=8 * group_rows * HEADS_PER_GROUP * HEAD_SIZE * total,
            bytes_accessed=16 * group_rows * GROUP_WIDTH,
            transcendentals=group_rows * HEADS_PER_GROUP * total,
        ),
        name="span_attention",
    )(listed, place, own, *received, near, far, *[carried[i] for i in kept])


def unpack_kernel(head_count, groups, *refs):
    parts, outs = refs[:-4], refs[-4:]
    rows = outs[0].shape[0]
    half = outs[0].shape[1] // head_count
    width = HEAD_SIZE
    for step in range(head_count):
        source = lax.rem(lax.axis_index("head") + step, head_count)
        for group, members in enumerate(groups):
            part = parts[group * head_count + step]
            for at, member in enumerate(members):
                to = lanes(source * half + member * width, width)
                for index in range(2):
                    here = slice((2 * at + index) * width, (2 * at + index + 1) * width)
                    outs[index][:, to] = part[:rows, here]
                    outs[2 + index][:, to] = part[rows:, here]


def unpacked(head_count, groups, grads, rows, clean_rows):
    vmem = pl.BlockSpec(memory_space=pltpu.VMEM)
    parts = [part for chunk in grads for part in chunk]
    width = KEY_VALUE_HEADS * HEAD_SIZE
    return pl.pallas_call(
        functools.partial(unpack_kernel, head_count, groups),
        in_specs=[vmem] * len(parts),
        out_specs=[vmem] * 4,
        out_shape=[jax.ShapeDtypeStruct((rows, width), jnp.bfloat16)] * 2
        + [jax.ShapeDtypeStruct((clean_rows, width), jnp.bfloat16)] * 2,
        name="unpack_gradients",
    )(*parts)


def shards(
    queries,
    noisy_token_keys,
    noisy_token_values,
    clean_token_keys,
    clean_token_values,
    output_gradient,
    history_list,
):
    ctx_count = lax.axis_size("ctx")
    head_count = lax.axis_size("head")
    head = lax.axis_index("head")
    place = jnp.stack([lax.axis_index("ctx"), head]).astype(jnp.int32)
    rows = queries.shape[0]
    clean_rows = clean_token_keys.shape[0]
    store_rows = clean_rows * head_count
    group_rows = rows * head_count
    slots = ctx_count - 2
    per_device = KEY_VALUE_HEADS // head_count
    everything = list(range(per_device))
    half = max(1, per_device // 2)
    key_groups = [g for g in (everything[:half], everything[half:]) if g]
    grad_groups = key_groups
    ask_groups = send_groups = [[m] for m in everything]
    depth = ctx_count // 4
    steps = range(1, head_count)
    row_order = lax.rem(head - jnp.arange(head_count, dtype=jnp.int32) + head_count, head_count)

    def by_block(store):
        if clean_rows >= BLK:
            return store
        return store.reshape(head_count, clean_rows, -1)[row_order].reshape(store.shape)

    packs = packed(
        head_count,
        key_groups,
        noisy_token_keys,
        noisy_token_values,
        clean_token_keys,
        clean_token_values,
    )

    asks = query_blocks(head_count, queries, output_gradient)

    def swap_keys(index):
        return [packs[index][0]] + [shifted(packs[index][step], step) for step in steps]

    def swap_queries(member):
        return [shifted(asks[member][step], step) for step in steps]

    def stored(parts):
        return by_block(jnp.concatenate([part[rows:] for part in parts], 0))

    def along(store):
        return [flipped(store, z << 2) for z in range(1, depth)]

    def joined(parts, line):
        return jnp.concatenate([part[:rows] for part in parts] + [line], 0)

    def summed(near_grad, from_core):
        total = near_grad.astype(jnp.float32) + from_core.astype(jnp.float32)
        return total[:group_rows], total[group_rows:]

    def halved(line):
        middle = line.shape[0] // 2
        return line[:middle], flipped(line[middle:].astype(jnp.bfloat16), 2)

    def back_along(line):
        gives = [line[z * store_rows : (z + 1) * store_rows] for z in range(depth)]
        return gives[0], [
            flipped(give.astype(jnp.bfloat16), z << 2) for z, give in enumerate(gives[1:], 1)
        ]

    def added(keep, others):
        for other in others:
            keep = keep + other.astype(jnp.float32)
        return keep

    together = lax.optimization_barrier
    def swap_heads(noisy_sum, store_sum):
        if clean_rows < BLK:
            store_sum = store_sum.reshape(head_count, clean_rows, -1)[row_order].reshape(
                store_sum.shape
            )
        store_sum = store_sum.astype(jnp.bfloat16)
        noisy_sum = noisy_sum.astype(jnp.bfloat16)
        mixed = [
            jnp.concatenate(
                [
                    noisy_sum[step * rows : (step + 1) * rows],
                    store_sum[step * clean_rows : (step + 1) * clean_rows],
                ],
                0,
            )
            for step in range(head_count)
        ]
        return [mixed[0]] + [shifted(mixed[step], -step) for step in steps]

    shape = (head_count, group_rows, store_rows, clean_rows, slots)
    received = {}
    two = len(key_groups) > 1
    parts = swap_keys(0)
    store = stored(parts)
    others = along(store)
    if two:
        asks[0], parts = together((asks[0], parts))
    received[0] = swap_queries(0)
    line = jnp.concatenate([store, *others], 0)
    crossing = flipped(line, 2)
    if two:
        packs[1], received[0], others = together((packs[1], received[0], others))
        later_parts = swap_keys(1)
        asks[1], _ = together((asks[1], received[0]))
        received[1] = swap_queries(1)
        later_store = stored(later_parts)
        later_others = along(later_store)
    near = joined(parts, jnp.concatenate([line, crossing], 0))
    if two:
        asks[2], _ = together((asks[2], near))
        received[2] = swap_queries(2)
    keys = {0: (near, flipped(near, 1))}
    outputs = [jax.ShapeDtypeStruct(queries.shape, jnp.bfloat16)] * 2
    sent = []
    held = []
    waiting = []

    def group_of(groups, member):
        return next(i for i, group in enumerate(groups) if member in group)

    for member in everything:
        k = group_of(key_groups, member)
        first = member == key_groups[k][0]
        last = member == key_groups[k][-1]
        sends = [jax.ShapeDtypeStruct((2 * rows, GROUP_WIDTH), jnp.bfloat16)] * (head_count - 1)
        if first:
            width = len(key_groups[k]) * 2 * HEAD_SIZE
            pair = [jax.ShapeDtypeStruct((near.shape[0], width), jnp.bfloat16)] * 2
        column = key_groups[k].index(member)
        outputs[0], outputs[1], *rest = attention(
            history_list,
            jnp.concatenate([place, jnp.array([member], jnp.int32)]),
            asks[member][0],
            received[member],
            *keys[k],
            [*outputs, *sends, *pair],
            shape,
            column,
        )
        sends, pair = rest[:-2], rest[-2:]
        if two and member == 0:
            outputs, later_others, received[1], received[2] = together(
                (outputs, later_others, received[1], received[2])
            )
            later_line = jnp.concatenate([later_store, *later_others], 0)
            crossing = flipped(later_line, 2)
        if two and member == 1:
            outputs, crossing = together((outputs, crossing))
            near = joined(later_parts, jnp.concatenate([later_line, crossing], 0))
            keys[1] = (near, flipped(near, 1))
        if member + 3 < per_device:
            asks, outputs = together((asks, outputs))
            received[member + 3] = swap_queries(member + 3)
        if two and member == 1:
            pair, received[3] = together((pair, received[3]))
        held.append(sends)
        if two and member == half:
            held[half - 1], outputs = together((held[half - 1], outputs))
        if not two or member >= half - 1:
            later = len(held) if member == everything[-1] and not two else len(held) - 1
            for block_set in held[len(sent) : later]:
                sent.append([shifted(block, -step) for step, block in zip(steps, block_set)])
        if waiting and not last:
            noisy_sum, line = summed(*waiting[0])
            line, outputs = together((line, outputs))
            waiting[0] = (noisy_sum, *halved(line))
            outputs, sent[0] = together((outputs, sent[0]))
        if last:
            if waiting:
                waiting[0], pair, sent[:half] = together((waiting[0], pair, sent[:half]))
            waiting.append((pair[0], flipped(pair[1], 1)))
    grads = []
    if two:
        first_noisy, keep, other = waiting[0]
        keep, others = back_along(added(keep, [other]))
    noisy_sum, line = summed(*waiting[-1])
    last_keep, last_other = halved(line)
    if two:
        last_other, others, sent[:half] = together((last_other, others, sent[:half]))
        grads.append(swap_heads(first_noisy, added(keep, others)))
    line = added(last_keep, [last_other])
    if two:
        held[-1], _ = together((held[-1], line))
        sent.append([shifted(block, -step) for step, block in zip(steps, held[-1])])
    last_keep, last_others = back_along(line)
    line = added(last_keep, last_others)
    if two:
        line, sent[half:] = together((line, sent[half:]))
    grads.append(swap_heads(noisy_sum, line))
    attended, query_grad = outputs
    for group, blocks in zip(send_groups, sent):
        for step, block in zip(steps, blocks):
            source = lax.rem(head + step, head_count)
            start = (source * per_device + group[0]) * GROUP_WIDTH
            attended = lax.dynamic_update_slice_in_dim(attended, block[:rows], start, 1)
            query_grad = lax.dynamic_update_slice_in_dim(query_grad, block[rows:], start, 1)
    finished = unpacked(head_count, grad_groups, grads, rows, clean_rows)
    return (attended, query_grad, *finished)


def solution(mesh):
    split = P(("ctx", "head"), None)
    return jax.shard_map(
        shards,
        mesh=mesh,
        in_specs=(split, split, split, split, split, split, P()),
        out_specs=(split,) * 6,
        check_vma=False,
    )
```

```python
import functools

import jax
import jax.numpy as jnp
from jax import lax
from jax.experimental import pallas as pl
from jax.experimental.pallas import tpu as pltpu
from jax.sharding import PartitionSpec as P

QUERY_HEADS = 48
KEY_VALUE_HEADS = 8
HEAD_SIZE = 128
BLK = 32
HEADS_PER_GROUP = QUERY_HEADS // KEY_VALUE_HEADS
GROUP_WIDTH = HEADS_PER_GROUP * HEAD_SIZE
SCALE = HEAD_SIZE**-0.5
LOG2E = 1.4426950408889634

NEG_FILL = -1e30
SLICE_ROWS = 256
KERNEL_VMEM = 16 * 2**20


def flipped(block, bits):
    count = lax.axis_size("ctx")
    return lax.ppermute(block, "ctx", [(i, i ^ bits) for i in range(count)])


def shifted(block, step):
    count = lax.axis_size("head")
    return lax.ppermute(block, "head", [(i, (i + step) % count) for i in range(count)])


def dot(a, b, contract):
    return lax.dot_general(
        a, b, ((contract[:1], contract[1:]), ((), ())), preferred_element_type=jnp.float32
    )


def lanes(start, size):
    return pl.ds(pl.multiple_of(start, HEAD_SIZE), size)


def pack_kernel(head_count, groups, k_noisy, v_noisy, k_clean, v_clean, *outs):
    rows = k_noisy.shape[0]
    half = k_noisy.shape[1] // head_count
    width = HEAD_SIZE
    for index, group in enumerate(groups):
        for step in range(head_count):
            out = outs[index * head_count + step]
            target = lax.rem(lax.axis_index("head") + step, head_count)
            for at, member in enumerate(group):
                source = lanes(target * half + member * width, width)
                for n, (noisy, clean) in enumerate(((k_noisy, k_clean), (v_noisy, v_clean))):
                    to = slice((2 * at + n) * width, (2 * at + n + 1) * width)
                    out[:rows, to] = noisy[:, source]
                    out[rows:, to] = clean[:, source]


def packed(head_count, groups, k_noisy, v_noisy, k_clean, v_clean):
    vmem = pl.BlockSpec(memory_space=pltpu.VMEM)
    rows = k_noisy.shape[0] + k_clean.shape[0]
    shapes = [
        jax.ShapeDtypeStruct((rows, 2 * HEAD_SIZE * len(group)), jnp.bfloat16)
        for group in groups
        for _ in range(head_count)
    ]
    outs = pl.pallas_call(
        functools.partial(pack_kernel, head_count, groups),
        in_specs=[vmem] * 4,
        out_specs=[vmem] * len(shapes),
        out_shape=shapes,
        name="pack_keys_values",
    )(k_noisy, v_noisy, k_clean, v_clean)
    return [outs[i * head_count : (i + 1) * head_count] for i in range(len(groups))]


def stack_kernel(head_count, q, g, *outs):
    rows = q.shape[0]
    per_device = KEY_VALUE_HEADS // head_count
    for member in range(per_device):
        for step in range(head_count):
            out = outs[member * head_count + step]
            target = lax.rem(lax.axis_index("head") + step, head_count)
            source = lanes((target * per_device + member) * GROUP_WIDTH, GROUP_WIDTH)
            out[:rows, :] = q[:, source]
            out[rows:, :] = g[:, source]


def query_blocks(head_count, q, g):
    vmem = pl.BlockSpec(memory_space=pltpu.VMEM)
    shape = jax.ShapeDtypeStruct((2 * q.shape[0], GROUP_WIDTH), jnp.bfloat16)
    outs = pl.pallas_call(
        functools.partial(stack_kernel, head_count),
        in_specs=[vmem] * 2,
        out_specs=[vmem] * KEY_VALUE_HEADS,
        out_shape=[shape] * KEY_VALUE_HEADS,
        name="stack_queries",
    )(q, g)
    return [outs[i : i + head_count] for i in range(0, KEY_VALUE_HEADS, head_count)]


def attention_kernel(shape, column, kept, listed, place, own, *refs):
    head_count, group_rows, store_rows, clean_rows, slots = shape
    received, refs = refs[: head_count - 1], refs[head_count - 1 :]
    near, far, *refs = refs
    o_all, gq_all, *refs = refs[kept:]
    sends, refs = refs[: head_count - 1], refs[head_count - 1 :]
    near_grad, far_grad, k_all, v_all, q_all, g_all, o_out, gq_out, o_own, gq_own, copied = refs
    rows = own.shape[0] // 2
    width = HEAD_SIZE
    position, head = place[0], place[1]
    k_cols = slice(2 * column * width, (2 * column + 1) * width)
    v_cols = slice((2 * column + 1) * width, (2 * column + 2) * width)
    depth = (near.shape[0] - group_rows) // (2 * store_rows)

    def placed(slot):
        apart = lax.bitwise_xor(position, slot)
        store = lax.bitwise_and(lax.shift_right_logical(apart, 1), 1) * depth
        store = store + lax.shift_right_logical(apart, 2)
        block = jnp.maximum(listed[position, slot], 0)
        if clean_rows >= BLK:
            owner = lax.div(block * BLK, clean_rows)
            step = lax.rem(head - owner + head_count, head_count)
            inside = step * clean_rows + block * BLK - owner * clean_rows
        else:
            inside = block * BLK
        start = pl.multiple_of(group_rows + store * store_rows + inside, BLK)
        return lax.bitwise_and(apart, 1), pl.ds(start, BLK)

    k_all[:group_rows, :] = near[:group_rows, k_cols]
    v_all[:group_rows, :] = near[:group_rows, v_cols]
    k_all[group_rows : 2 * group_rows, :] = far[:group_rows, k_cols]
    v_all[group_rows : 2 * group_rows, :] = far[:group_rows, v_cols]
    span = 2 * group_rows
    total = span + slots * BLK
    for slot in range(slots):
        other, source = placed(slot)
        to = slice(span + slot * BLK, span + (slot + 1) * BLK)
        k_all[to, :] = jnp.where(other == 1, far[source, k_cols], near[source, k_cols])
        v_all[to, :] = jnp.where(other == 1, far[source, v_cols], near[source, v_cols])
    at = 0
    for r in range(HEADS_PER_GROUP):
        for part in (own, *received):
            q_all[at : at + rows, :] = part[:rows, r * width : (r + 1) * width]
            g_all[at : at + rows, :] = part[rows:, r * width : (r + 1) * width]
            at += rows

    keys = k_all[...]
    values = v_all[...]
    keys_t = keys.T
    values_t = values.T
    biases = [
        jnp.where(listed[position, slot] >= 0, 0.0, NEG_FILL).astype(jnp.float32)
        for slot in range(slots)
    ]
    cuts = list(range(0, at - SLICE_ROWS + 1, SLICE_ROWS)) + [at]
    slices = [slice(low, high) for low, high in zip(cuts, cuts[1:])]

    def products(piece):
        query, upstream = q_all[piece, :], g_all[piece, :]
        return query, upstream, dot(keys, query, (1, 1)), dot(values, upstream, (1, 1))

    def softmax(scores, dprob):
        scores = scores * (SCALE * LOG2E)
        pieces = [scores[:span]]
        for slot in range(slots):
            low = span + slot * BLK
            pieces.append(scores[low : low + BLK] + biases[slot])
        scores = jnp.concatenate(pieces, 0)
        top = jnp.max(scores, 0, keepdims=True)
        unscaled = jnp.exp2(scores - top)
        prob = unscaled * (1.0 / jnp.sum(unscaled, 0, keepdims=True))
        row_dot = jnp.sum(prob * dprob, 0, keepdims=True)
        return prob.astype(jnp.bfloat16), (prob * (dprob - row_dot)).astype(jnp.bfloat16)

    gk = jnp.zeros((total, width), jnp.float32)
    gv = jnp.zeros((total, width), jnp.float32)
    ahead = products(slices[0])
    for index, piece in enumerate(slices):
        query, upstream, scores, dprob = ahead
        if index + 1 < len(slices):
            ahead = products(slices[index + 1])
        weights, dscore = softmax(scores, dprob)
        o_out[piece, :] = dot(values_t, weights, (1, 0)).astype(jnp.bfloat16).T
        gq_out[piece, :] = (dot(keys_t, dscore, (1, 0)) * SCALE).astype(jnp.bfloat16).T
        gk = gk + dot(dscore, query, (1, 0))
        gv = gv + dot(weights, upstream, (1, 0))
    at = 0
    for r in range(HEADS_PER_GROUP):
        to = slice(r * width, (r + 1) * width)
        for part in (None, *sends):
            attended, gq = o_out[at : at + rows, :], gq_out[at : at + rows, :]
            if part is None:
                o_own[:, to] = attended
                gq_own[:, to] = gq
            else:
                part[:rows, to] = attended
                part[rows:, to] = gq
            at += rows
    start = (head * (KEY_VALUE_HEADS // head_count) + place[2]) * GROUP_WIDTH
    target = lanes(start, GROUP_WIDTH)
    copies = [
        pltpu.make_async_copy(o_own, o_all.at[:, target], copied.at[0]),
        pltpu.make_async_copy(gq_own, gq_all.at[:, target], copied.at[1]),
    ]
    for copy in copies:
        copy.start()
    gk = (gk * SCALE).astype(jnp.bfloat16)
    gv = gv.astype(jnp.bfloat16)
    for index, grad in enumerate((near_grad, far_grad)):
        here = slice(index * group_rows, (index + 1) * group_rows)
        grad[:group_rows, k_cols] = gk[here]
        grad[:group_rows, v_cols] = gv[here]
        rest = grad.shape[0] - group_rows
        grad[group_rows:, k_cols] = jnp.zeros((rest, width), jnp.bfloat16)
        grad[group_rows:, v_cols] = jnp.zeros((rest, width), jnp.bfloat16)
    for slot in range(slots):
        other, target = placed(slot)
        low = span + slot * BLK
        for index, grad in enumerate((near_grad, far_grad)):

            @pl.when(jnp.logical_and(listed[position, slot] >= 0, other == index))
            def _():
                grad[target, k_cols] = gk[low : low + BLK]
                grad[target, v_cols] = gv[low : low + BLK]

    for copy in copies:
        copy.wait()


def attention(listed, place, own, received, near, far, carried, shape, column):
    head_count, group_rows, store_rows, clean_rows, slots = shape
    rows = own.shape[0] // 2
    total = 2 * group_rows + slots * BLK
    stacked = HEADS_PER_GROUP * group_rows
    smem = pl.BlockSpec(memory_space=pltpu.SMEM)
    vmem = pl.BlockSpec(memory_space=pltpu.VMEM)
    hbm = pl.BlockSpec(memory_space=pl.ANY)
    kept = [i for i, array in enumerate(carried) if not isinstance(array, jax.ShapeDtypeStruct)]
    first_carried = 3 + len(received) + 2
    spaces = [hbm, hbm] + [vmem] * (len(carried) - 2)
    return pl.pallas_call(
        functools.partial(attention_kernel, shape, column, len(kept)),
        in_specs=[smem, smem] + [vmem] * (3 + len(received)) + [spaces[i] for i in kept],
        out_specs=spaces,
        scratch_shapes=[pltpu.VMEM((total, HEAD_SIZE), jnp.bfloat16)] * 2
        + [pltpu.VMEM((stacked, HEAD_SIZE), jnp.bfloat16)] * 4
        + [pltpu.VMEM((rows, GROUP_WIDTH), jnp.bfloat16)] * 2
        + [pltpu.SemaphoreType.DMA((2,))],
        out_shape=[jax.ShapeDtypeStruct(array.shape, jnp.bfloat16) for array in carried],
        input_output_aliases={first_carried + n: i for n, i in enumerate(kept)},
        compiler_params=pltpu.CompilerParams(vmem_limit_bytes=KERNEL_VMEM),
        cost_estimate=pl.CostEstimate(
            flops=8 * group_rows * HEADS_PER_GROUP * HEAD_SIZE * total,
            bytes_accessed=16 * group_rows * GROUP_WIDTH,
            transcendentals=group_rows * HEADS_PER_GROUP * total,
        ),
        name="span_attention",
    )(listed, place, own, *received, near, far, *[carried[i] for i in kept])


def unpack_kernel(head_count, groups, *refs):
    parts, outs = refs[:-4], refs[-4:]
    rows = outs[0].shape[0]
    half = outs[0].shape[1] // head_count
    width = HEAD_SIZE
    for step in range(head_count):
        source = lax.rem(lax.axis_index("head") + step, head_count)
        for group, members in enumerate(groups):
            part = parts[group * head_count + step]
            for at, member in enumerate(members):
                to = lanes(source * half + member * width, width)
                for index in range(2):
                    here = slice((2 * at + index) * width, (2 * at + index + 1) * width)
                    outs[index][:, to] = part[:rows, here]
                    outs[2 + index][:, to] = part[rows:, here]


def unpacked(head_count, groups, grads, rows, clean_rows):
    vmem = pl.BlockSpec(memory_space=pltpu.VMEM)
    parts = [part for chunk in grads for part in chunk]
    width = KEY_VALUE_HEADS * HEAD_SIZE
    return pl.pallas_call(
        functools.partial(unpack_kernel, head_count, groups),
        in_specs=[vmem] * len(parts),
        out_specs=[vmem] * 4,
        out_shape=[jax.ShapeDtypeStruct((rows, width), jnp.bfloat16)] * 2
        + [jax.ShapeDtypeStruct((clean_rows, width), jnp.bfloat16)] * 2,
        name="unpack_gradients",
    )(*parts)


def shards(
    queries,
    noisy_token_keys,
    noisy_token_values,
    clean_token_keys,
    clean_token_values,
    output_gradient,
    history_list,
):
    ctx_count = lax.axis_size("ctx")
    head_count = lax.axis_size("head")
    head = lax.axis_index("head")
    place = jnp.stack([lax.axis_index("ctx"), head]).astype(jnp.int32)
    rows = queries.shape[0]
    clean_rows = clean_token_keys.shape[0]
    store_rows = clean_rows * head_count
    group_rows = rows * head_count
    slots = ctx_count - 2
    per_device = KEY_VALUE_HEADS // head_count
    everything = list(range(per_device))
    half = max(1, per_device // 2)
    key_groups = [g for g in (everything[:half], everything[half:]) if g]
    grad_groups = key_groups
    ask_groups = send_groups = [[m] for m in everything]
    depth = ctx_count // 4
    steps = range(1, head_count)
    row_order = lax.rem(head - jnp.arange(head_count, dtype=jnp.int32) + head_count, head_count)

    def by_block(store):
        if clean_rows >= BLK:
            return store
        return store.reshape(head_count, clean_rows, -1)[row_order].reshape(store.shape)

    packs = packed(
        head_count,
        key_groups,
        noisy_token_keys,
        noisy_token_values,
        clean_token_keys,
        clean_token_values,
    )

    asks = query_blocks(head_count, queries, output_gradient)

    def swap_keys(index):
        return [packs[index][0]] + [shifted(packs[index][step], step) for step in steps]

    def swap_queries(member):
        return [shifted(asks[member][step], step) for step in steps]

    def stored(parts):
        return by_block(jnp.concatenate([part[rows:] for part in parts], 0))

    def along(store):
        return [flipped(store, z << 2) for z in range(1, depth)]

    def joined(parts, line):
        return jnp.concatenate([part[:rows] for part in parts] + [line], 0)

    def summed(near_grad, from_core):
        total = near_grad.astype(jnp.float32) + from_core.astype(jnp.float32)
        return total[:group_rows], total[group_rows:]

    def halved(line):
        middle = line.shape[0] // 2
        return line[:middle], flipped(line[middle:].astype(jnp.bfloat16), 2)

    def back_along(line):
        gives = [line[z * store_rows : (z + 1) * store_rows] for z in range(depth)]
        return gives[0], [
            flipped(give.astype(jnp.bfloat16), z << 2) for z, give in enumerate(gives[1:], 1)
        ]

    def added(keep, others):
        for other in others:
            keep = keep + other.astype(jnp.float32)
        return keep

    together = lax.optimization_barrier
    def swap_heads(noisy_sum, store_sum):
        if clean_rows < BLK:
            store_sum = store_sum.reshape(head_count, clean_rows, -1)[row_order].reshape(
                store_sum.shape
            )
        store_sum = store_sum.astype(jnp.bfloat16)
        noisy_sum = noisy_sum.astype(jnp.bfloat16)
        mixed = [
            jnp.concatenate(
                [
                    noisy_sum[step * rows : (step + 1) * rows],
                    store_sum[step * clean_rows : (step + 1) * clean_rows],
                ],
                0,
            )
            for step in range(head_count)
        ]
        return [mixed[0]] + [shifted(mixed[step], -step) for step in steps]

    shape = (head_count, group_rows, store_rows, clean_rows, slots)
    received = {}
    two = len(key_groups) > 1
    parts = swap_keys(0)
    store = stored(parts)
    others = along(store)
    if two:
        asks[0], parts = together((asks[0], parts))
    received[0] = swap_queries(0)
    line = jnp.concatenate([store, *others], 0)
    crossing = flipped(line, 2)
    if two:
        packs[1], received[0], others = together((packs[1], received[0], others))
        later_parts = swap_keys(1)
        asks[1], _ = together((asks[1], received[0]))
        received[1] = swap_queries(1)
        later_store = stored(later_parts)
        later_others = along(later_store)
    near = joined(parts, jnp.concatenate([line, crossing], 0))
    if two:
        asks[2], _ = together((asks[2], near))
        received[2] = swap_queries(2)
    keys = {0: (near, flipped(near, 1))}
    outputs = [jax.ShapeDtypeStruct(queries.shape, jnp.bfloat16)] * 2
    sent = []
    held = []
    waiting = []

    def group_of(groups, member):
        return next(i for i, group in enumerate(groups) if member in group)

    for member in everything:
        k = group_of(key_groups, member)
        first = member == key_groups[k][0]
        last = member == key_groups[k][-1]
        sends = [jax.ShapeDtypeStruct((2 * rows, GROUP_WIDTH), jnp.bfloat16)] * (head_count - 1)
        if first:
            width = len(key_groups[k]) * 2 * HEAD_SIZE
            pair = [jax.ShapeDtypeStruct((near.shape[0], width), jnp.bfloat16)] * 2
        column = key_groups[k].index(member)
        outputs[0], outputs[1], *rest = attention(
            history_list,
            jnp.concatenate([place, jnp.array([member], jnp.int32)]),
            asks[member][0],
            received[member],
            *keys[k],
            [*outputs, *sends, *pair],
            shape,
            column,
        )
        sends, pair = rest[:-2], rest[-2:]
        if two and member == 0:
            outputs, later_others, received[1], received[2] = together(
                (outputs, later_others, received[1], received[2])
            )
            later_line = jnp.concatenate([later_store, *later_others], 0)
            crossing = flipped(later_line, 2)
        if two and member == 1:
            outputs, crossing = together((outputs, crossing))
            near = joined(later_parts, jnp.concatenate([later_line, crossing], 0))
            keys[1] = (near, flipped(near, 1))
        if member + 3 < per_device:
            asks, outputs = together((asks, outputs))
            received[member + 3] = swap_queries(member + 3)
        if two and member == 1:
            pair, received[3] = together((pair, received[3]))
        held.append(sends)
        if two and member == half:
            held[half - 1], outputs = together((held[half - 1], outputs))
        if not two or member >= half - 1:
            later = len(held) if member == everything[-1] else len(held) - 1
            for block_set in held[len(sent) : later]:
                sent.append([shifted(block, -step) for step, block in zip(steps, block_set)])
        if waiting and not last:
            noisy_sum, line = summed(*waiting[0])
            line, outputs = together((line, outputs))
            waiting[0] = (noisy_sum, *halved(line))
            outputs, sent[0] = together((outputs, sent[0]))
        if last:
            if waiting:
                waiting[0], pair, sent[:half] = together((waiting[0], pair, sent[:half]))
            waiting.append((pair[0], flipped(pair[1], 1)))
    grads = []
    if two:
        first_noisy, keep, other = waiting[0]
        keep, others = back_along(added(keep, [other]))
    noisy_sum, line = summed(*waiting[-1])
    last_keep, last_other = halved(line)
    if two:
        last_other, others, sent[:half] = together((last_other, others, sent[:half]))
        grads.append(swap_heads(first_noisy, added(keep, others)))
    last_keep, last_others = back_along(added(last_keep, [last_other]))
    line = added(last_keep, last_others)
    if two:
        line, sent[half:] = together((line, sent[half:]))
    grads.append(swap_heads(noisy_sum, line))
    attended, query_grad = outputs
    for group, blocks in zip(send_groups, sent):
        for step, block in zip(steps, blocks):
            source = lax.rem(head + step, head_count)
            start = (source * per_device + group[0]) * GROUP_WIDTH
            attended = lax.dynamic_update_slice_in_dim(attended, block[:rows], start, 1)
            query_grad = lax.dynamic_update_slice_in_dim(query_grad, block[rows:], start, 1)
    finished = unpacked(head_count, grad_groups, grads, rows, clean_rows)
    return (attended, query_grad, *finished)


def solution(mesh):
    split = P(("ctx", "head"), None)
    return jax.shard_map(
        shards,
        mesh=mesh,
        in_specs=(split, split, split, split, split, split, P()),
        out_specs=(split,) * 6,
        check_vma=False,
    )
```
